32 devices in a mesh: fsdp: 8 (over y, x, core), sp: 4 (over z).
Axes of the slice: x: 2, y: 2, z: 4, core: 2. Of those that a mesh axis runs over, the one named last changes fastest.
Arguments:
- tokens: bfloat16 [2, 8, 1024, 2560], P(None, 'fsdp', 'sp'), may hold values from -6 to 6
- doc_starts: int32 [2, 8, 4], P(None, 'fsdp'), may hold values from 0 to 1023, as said below
- cotangent: bfloat16 [2, 8, 1024, 2560], P(None, 'fsdp', 'sp'), may hold values from -6 to 6
- gain_attn: bfloat16 [2560], P('fsdp'), may hold values from 0.25 to 1.75
- gain_ffn: bfloat16 [2560], P('fsdp'), may hold values from 0.25 to 1.75
- w_query: bfloat16 [2560, 2560], P('fsdp'), may hold values from -0.125 to 0.125
- w_key: bfloat16 [2560, 640], P('fsdp'), may hold values from -0.125 to 0.125
- w_value: bfloat16 [2560, 640], P('fsdp'), may hold values from -0.125 to 0.125
- w_out: bfloat16 [2560, 2560], P('fsdp'), may hold values from -0.5 to 0.5
- w_gate: bfloat16 [2560, 7168], P('fsdp'), may hold values from -0.125 to 0.125
- w_up: bfloat16 [2560, 7168], P('fsdp'), may hold values from -0.125 to 0.125
- w_down: bfloat16 [7168, 2560], P('fsdp'), may hold values from -0.0625 to 0.0625
Outputs:
- mixed_out: bfloat16 [2, 8, 1024, 2560], P(None, 'fsdp', 'sp')
- tokens_grad: bfloat16 [2, 8, 1024, 2560], P(None, 'fsdp', 'sp')
- grad_gain_attn: float32 [2560], P('fsdp')
- grad_gain_ffn: float32 [2560], P('fsdp')
- grad_query: float32 [2560, 2560], P('fsdp')
- grad_key: float32 [2560, 640], P('fsdp')
- grad_value: float32 [2560, 640], P('fsdp')
- grad_out: float32 [2560, 2560], P('fsdp')
- grad_gate: float32 [2560, 7168], P('fsdp')
- grad_up: float32 [2560, 7168], P('fsdp')
- grad_down: float32 [7168, 2560], P('fsdp')
The draws below stay inside these ranges and needn't reach their ends.
Inputs may be any that keep to these rules, and one draw needn't show every extreme that they name: Within each stream the starts rise strictly from doc_starts[m, s, 0] = 0; one document of every stream begins within its first 256 tokens and ends within its last 256.
All inputs are finite; a program needn't handle non-finite values.
Results may differ from the reference program's by a relative error of at most 0.017.
Values may be sent and summed in bfloat16 or wider, within the bound.
No kernel may reach another device: no remote copies, remote signals or barrier semaphores. Data moves between devices by JAX's collectives and lax.ppermute only.
A program may use at most 440 MiB of HBM per device.

```python
import math
import jax
import jax.numpy as jnp
from jax import lax

D = 2560
HEADS = 32
KV_HEADS = 8
HEAD_DIM = 80
FF = 7168
MICRO = 2
DOCS = 4
STREAMS = 8
LENGTH = 1024
ROWS = 256


def draw_doc_starts(key, part):
    key = jax.random.fold_in(key, 7)
    key_short, key_long = jax.random.split(key)
    short_len = jax.random.randint(key_short, (MICRO, STREAMS, DOCS), 1, ROWS // 4 + 1)
    long_at = jax.random.randint(key_long, (MICRO, STREAMS, 1), 0, DOCS)
    places = jnp.arange(DOCS, dtype=jnp.int32)[None, None, :]
    lengths = jnp.where(places == long_at, 0, short_len)
    long_len = LENGTH - jnp.sum(lengths, axis=-1, keepdims=True)
    lengths = jnp.where(places == long_at, long_len, lengths)
    starts = jnp.cumsum(lengths, axis=-1) - lengths
    return starts.astype(jnp.int32)


def shard_levels(own_key, extent, cuts, low, top_value):
    def one(axis_at, parts):
        draws = jax.random.uniform(jax.random.fold_in(jax.random.fold_in(own_key, 6), axis_at), (parts,), jnp.float32, low / len(cuts), top_value / len(cuts))
        return jnp.repeat(jnp.exp(draws), extent[axis_at] // parts).reshape((-1,) + (1,) * (len(extent) - axis_at - 1))

    loudness = one(*cuts[0])
    for cut in cuts[1:]:
        loudness = loudness * one(*cut)
    return loudness


def centred(key, dims, scale, reach, cuts=(), kind=jnp.bfloat16):
    values = scale * jax.random.normal(key, dims, jnp.float32)
    if cuts:
        values = values * shard_levels(key, dims, cuts, -0.22, 0.18)
    return jnp.clip(values, -reach, reach).astype(kind)


def setup_inputs(seed: int = 0) -> dict:
    arg_keys = jax.random.split(jax.random.key(seed), 13)
    return {
        "tokens": centred(arg_keys[0], (MICRO, STREAMS, LENGTH, D), 1.0, 6.0, ((1, 8), (2, 4))),
        "doc_starts": draw_doc_starts(jax.random.fold_in(arg_keys[12], 71), 0),
        "cotangent": centred(arg_keys[2], (MICRO, STREAMS, LENGTH, D), 1.0, 6.0, ((1, 8), (2, 4))),
        "gain_attn": jnp.clip(1.0 + 0.15 * jax.random.normal(arg_keys[3], (D,), jnp.float32), 0.25, 1.75).astype(jnp.bfloat16),
        "gain_ffn": jnp.clip(1.0 + 0.15 * jax.random.normal(arg_keys[4], (D,), jnp.float32), 0.25, 1.75).astype(jnp.bfloat16),
        "w_query": centred(arg_keys[5], (D, D), D ** -0.5, 0.125, ((0, 8),)),
        "w_key": centred(arg_keys[6], (D, KV_HEADS * HEAD_DIM), D ** -0.5, 0.125, ((0, 8),)),
        "w_value": centred(arg_keys[7], (D, KV_HEADS * HEAD_DIM), D ** -0.5, 0.125, ((0, 8),)),
        "w_out": centred(arg_keys[8], (D, D), (D // 16) ** -0.5, 0.5, ((0, 8),)),
        "w_gate": centred(arg_keys[9], (D, FF), D ** -0.5, 0.125, ((0, 8),)),
        "w_up": centred(arg_keys[10], (D, FF), D ** -0.5, 0.125, ((0, 8),)),
        "w_down": centred(arg_keys[11], (FF, D), FF ** -0.5, 0.0625, ((0, 8),)),
    }


rms_eps = 1e-05
rope_base = 1000000.0

@jax.custom_vjp
def low(v):
    return lax.optimization_barrier(v.astype(jnp.bfloat16)).astype(jnp.float32)

@jax.custom_vjp
def low_back(v):
    return v

def low_keep(v):
    return (low(v), None)

def low_pass(kept, grad):
    return (grad,)

def back_keep(v):
    return (v, None)

def back_low(kept, grad):
    return (low(grad),)
low.defvjp(low_keep, low_pass)
low_back.defvjp(back_keep, back_low)

def matmul(left, right):
    return jnp.dot(left, right, precision=lax.Precision.HIGHEST)

def rms_scale(values):
    return lax.rsqrt(lax.optimization_barrier(jnp.mean(values * values, axis=-1, keepdims=True)) + rms_eps)

def doc_layout(starts_row, length):
    places = jnp.arange(length, dtype=jnp.int32)
    begun = starts_row[None, :] <= places[:, None]
    doc_ids = lax.optimization_barrier(jnp.sum(begun.astype(jnp.int32), axis=-1)) - 1
    first_token = lax.optimization_barrier(jnp.max(jnp.where(begun, starts_row[None, :], 0), axis=-1))
    return (doc_ids, places - first_token)

def rope_tables(place):
    half_dim = HEAD_DIM // 2
    inverse = jnp.exp(jnp.arange(half_dim, dtype=jnp.float32) * (-2.0 * math.log(rope_base) / HEAD_DIM))
    angles = place.astype(jnp.float32)[:, None] * inverse[None, :]
    return (jnp.cos(angles)[:, None, :], jnp.sin(angles)[:, None, :])

def rotate(values, cosine, sine):
    half_dim = HEAD_DIM // 2
    first_half = values[..., :half_dim]
    second_half = values[..., half_dim:]
    return jnp.concatenate([first_half * cosine - second_half * sine, second_half * cosine + first_half * sine], axis=-1)

def attention(queries, keys_rot, values_in, doc_ids):
    length = queries.shape[0]
    block_rows = min(512, length)
    blocks = length // block_rows
    group_size = HEADS // KV_HEADS
    score_scale = HEAD_DIM ** (-0.5)
    grouped = queries.reshape(blocks, block_rows, KV_HEADS, group_size, HEAD_DIM)
    places = jnp.arange(length, dtype=jnp.int32)

    def attend_block(entry_set):
        query_block, doc_block, row_block = entry_set
        scores = jnp.einsum('bkgd,lkd->kgbl', query_block, keys_rot, precision=lax.Precision.HIGHEST) * score_scale
        scores = low_back(scores)
        allowed = (doc_block[:, None] == doc_ids[None, :]) & (places[None, :] <= row_block[:, None])
        scores = jnp.where(allowed[None, None], scores, -1e+30)
        row_max = lax.optimization_barrier(jnp.max(scores, axis=-1, keepdims=True))
        weights_exp = jnp.exp(scores - row_max)
        probabilities = weights_exp / lax.optimization_barrier(jnp.sum(weights_exp, axis=-1, keepdims=True))
        return jnp.einsum('kgbl,lkd->bkgd', low(probabilities), values_in, precision=lax.Precision.HIGHEST)
    context = lax.map(jax.checkpoint(attend_block), (grouped, doc_ids.reshape(blocks, block_rows), places.reshape(blocks, block_rows)))
    return context.reshape(length, HEADS * HEAD_DIM)

def forward_stream(stream, gain_attn, gain_ffn, w_query, w_key, w_value, w_out, w_gate, w_up, w_down, starts_row):
    length = stream.shape[0]
    doc_ids, place = doc_layout(starts_row, length)
    cosine, sine = rope_tables(place)
    normed = low(stream * rms_scale(stream) * gain_attn)
    queries = low(rotate(low_back(matmul(normed, w_query)).reshape(length, HEADS, HEAD_DIM), cosine, sine))
    keys_rot = low(rotate(low_back(matmul(normed, w_key)).reshape(length, KV_HEADS, HEAD_DIM), cosine, sine))
    values_in = low(low_back(matmul(normed, w_value))).reshape(length, KV_HEADS, HEAD_DIM)
    context = low(low_back(attention(queries, keys_rot, values_in, doc_ids)))
    mixed = stream + low_back(matmul(context, w_out))
    normed_ffn = low(mixed * rms_scale(mixed) * gain_ffn)
    gate = low_back(matmul(normed_ffn, w_gate))
    up_proj = low_back(matmul(normed_ffn, w_up))
    hidden = low(jax.nn.silu(gate) * up_proj)
    return mixed + matmul(hidden, w_down)

def reference(tokens, doc_starts, cotangent, gain_attn, gain_ffn, w_query, w_key, w_value, w_out, w_gate, w_up, w_down):
    params = tuple((array.astype(jnp.float32) for array in (gain_attn, gain_ffn, w_query, w_key, w_value, w_out, w_gate, w_up, w_down)))
    streams = MICRO * STREAMS
    inputs_all = tokens.astype(jnp.float32).reshape(streams, LENGTH, D)
    cot_all = cotangent.astype(jnp.float32).reshape(streams, LENGTH, D)
    starts_all = doc_starts.reshape(streams, DOCS).astype(jnp.int32)

    def per_stream(running, entry_set):
        stream, grad_in, starts_row = entry_set

        def apply_layer(stream_in, *weights):
            return forward_stream(stream_in, *weights, starts_row)
        result, pullback = jax.vjp(apply_layer, stream, *params)
        gradients = pullback(grad_in)
        return (tuple((total + gradient for total, gradient in zip(running, gradients[1:]))), (result, gradients[0]))
    zeros_init = tuple((jnp.zeros_like(array) for array in params))
    running, (results, input_grads) = lax.scan(per_stream, zeros_init, (inputs_all, cot_all, starts_all))
    full_shape = tokens.shape
    return (results.reshape(full_shape).astype(jnp.bfloat16), input_grads.reshape(full_shape).astype(jnp.bfloat16), running[0], running[1], running[2], running[3], running[4], running[5], running[6], running[7], running[8])
```

```python
import functools, math
import jax, jax.numpy as jnp
from jax import lax
from jax.experimental import pallas as pl
from jax.experimental.pallas import tpu as pltpu
from jax.sharding import PartitionSpec as P

D = 2560
HEADS = 32
KV_HEADS = 8
HEAD_DIM = 80
GROUP = HEADS // KV_HEADS
HALVES = 2
SCALE = HEAD_DIM ** -0.5
LOG2E = 1.0 / math.log(2.0)
QW = D // HALVES
KW = KV_HEADS * HEAD_DIM // HALVES
CHUNK = 640


def nt(left, right):
    return lax.dot_general(left, right, (((1,), (1,)), ((), ())), preferred_element_type=jnp.float32)


def tn(left, right):
    return lax.dot_general(left, right, (((0,), (0,)), ((), ())), preferred_element_type=jnp.float32)


def nn(left, right):
    return jnp.dot(left, right, preferred_element_type=jnp.float32)


def head(h):
    return slice(h * HEAD_DIM, (h + 1) * HEAD_DIM)


def spin(x, cosine, sine_up, sine_down):
    half = HEAD_DIM // 2
    width = x.shape[1]
    return x * cosine + pltpu.roll(x, width - half, 1) * sine_up + pltpu.roll(x, half, 1) * sine_down


def project_kernel(n_ref, w_ref, cos_ref, up_ref, down_ref, out_ref):
    j = pl.program_id(0)
    x = nn(n_ref[...], w_ref[...])
    turned = spin(x, cos_ref[...], up_ref[...], down_ref[...])
    lane = lax.broadcasted_iota(jnp.int32, x.shape, 1)
    keep = (j < D // CHUNK) | (lane < KW)
    out_ref[...] = jnp.where(keep, turned, x).astype(jnp.bfloat16)


def project(normed, weights, tables):
    rows = normed.shape[0]
    chunks = (D + 4 * KW) // CHUNK
    table = pl.BlockSpec((rows, CHUNK), lambda j: (0, 0))
    return pl.pallas_call(
        project_kernel,
        grid=(chunks,),
        in_specs=[pl.BlockSpec((rows, D), lambda j: (0, 0)), pl.BlockSpec((D, CHUNK), lambda j: (0, j)), table, table, table],
        out_specs=pl.BlockSpec((rows, CHUNK), lambda j: (0, j)),
        out_shape=jax.ShapeDtypeStruct((rows, chunks * CHUNK), jnp.bfloat16),
        compiler_params=pltpu.CompilerParams(vmem_limit_bytes=48 << 20),
        cost_estimate=pl.CostEstimate(flops=2 * rows * D * chunks * CHUNK, bytes_accessed=2 * (rows * D + D * chunks * CHUNK + rows * chunks * CHUNK), transcendentals=0),
        name="project",
    )(normed, weights, *tables)


def forward_kernel(blocks, q_ref, *refs):
    kv_refs = refs[:blocks]
    bias_ref, ctx_ref, lse_ref = refs[blocks:]
    rows = q_ref.shape[0]
    bias = [bias_ref[s] for s in range(blocks)]
    lane = lax.broadcasted_iota(jnp.int32, (rows, 128), 1)
    lse_all = jnp.zeros((rows, 128), jnp.float32)
    for h in range(QW // HEAD_DIM):
        c = h // GROUP
        q = q_ref[:, head(h)]
        scores = [nt(q, kv_refs[s][:, head(c)]) * (SCALE * LOG2E) + bias_ref[s] for s in range(blocks)]
        top = functools.reduce(jnp.maximum, scores).max(axis=1, keepdims=True)
        probs = [jnp.exp2(x - top) for x in scores]
        total = functools.reduce(jnp.add, probs).sum(axis=1, keepdims=True)
        ctx = functools.reduce(jnp.add, [nn(p.astype(jnp.bfloat16), kv_refs[s][:, KW + c * HEAD_DIM:KW + (c + 1) * HEAD_DIM]) for s, p in enumerate(probs)])
        ctx_ref[:, head(h)] = (ctx / total).astype(jnp.bfloat16)
        lse_all = jnp.where(lane == h, top + jnp.log2(total), lse_all)
    lse_ref[...] = lse_all


def attend(qkv, kv_blocks, bias, at):
    rows = kv_blocks[0].shape[0]
    blocks = len(kv_blocks)
    kv_spec = pl.BlockSpec((rows, 2 * KW), lambda h: (0, h))
    return pl.pallas_call(
        functools.partial(forward_kernel, blocks),
        grid=(HALVES,),
        in_specs=[pl.BlockSpec((rows, QW), lambda h: (at, h))] + [kv_spec] * blocks + [pl.BlockSpec((blocks, rows, rows), lambda h: (0, 0, 0))],
        out_specs=[pl.BlockSpec((rows, QW), lambda h: (0, h)), pl.BlockSpec((rows, 128), lambda h: (0, h))],
        out_shape=[jax.ShapeDtypeStruct((rows, D), jnp.bfloat16), jax.ShapeDtypeStruct((rows, HALVES * 128), jnp.float32)],
        compiler_params=pltpu.CompilerParams(vmem_limit_bytes=48 << 20),
        cost_estimate=pl.CostEstimate(flops=4 * rows * rows * blocks * HEADS * 128, bytes_accessed=2 * rows * D * (2 + blocks // 2), transcendentals=rows * rows * blocks * HEADS),
        name="attend",
    )(qkv, *kv_blocks, bias)


def backward_kernel(blocks, q_ref, dctx_ref, ctx_ref, lse_ref, *refs):
    kv_refs = refs[:blocks]
    bias_ref, cos_ref, up_ref, down_ref, dq_ref = refs[blocks:blocks + 5]
    dkv_refs = refs[blocks + 5:2 * blocks + 5]
    dq_acc = refs[-1]
    rows = q_ref.shape[0]
    count = QW // HEAD_DIM
    owner = lax.broadcasted_iota(jnp.int32, (count, QW), 0)
    lane = lax.broadcasted_iota(jnp.int32, (count, QW), 1)
    pick = ((lane >= owner * HEAD_DIM) & (lane < owner * HEAD_DIM + HEAD_DIM)).astype(jnp.float32)
    product = dctx_ref[...].astype(jnp.float32) * ctx_ref[...].astype(jnp.float32)
    delta = lax.dot_general(pick, product, (((1,), (1,)), ((), ())), precision=lax.Precision.HIGHEST, preferred_element_type=jnp.float32)
    for c in range(KV_HEADS // HALVES):
        heads = range(c * GROUP, (c + 1) * GROUP)
        qs = [q_ref[:, head(h)] for h in heads]
        ds = [dctx_ref[:, head(h)] for h in heads]
        q_stack = jnp.concatenate(qs, axis=0)
        d_stack = jnp.concatenate(ds, axis=0)
        dq = [None] * GROUP
        for s in range(blocks):
            k = kv_refs[s][:, head(c)]
            v = kv_refs[s][:, KW + c * HEAD_DIM:KW + (c + 1) * HEAD_DIM]
            ps, dss = [], []
            for g, h in enumerate(heads):
                score = nt(k, qs[g]) * (SCALE * LOG2E) + bias_ref[s]
                p = jnp.exp2(score - lse_ref[h:h + 1, :])
                dp = nt(v, ds[g])
                d = (p * (dp - delta[h:h + 1, :])).astype(jnp.bfloat16)
                ps.append(p.astype(jnp.bfloat16))
                dss.append(d)
                term = tn(d, k)
                dq[g] = term if dq[g] is None else dq[g] + term
            dkv_refs[s][:, head(c)] = (nn(jnp.concatenate(dss, axis=1), q_stack) * SCALE).astype(jnp.bfloat16)
            dkv_refs[s][:, KW + c * HEAD_DIM:KW + (c + 1) * HEAD_DIM] = nn(jnp.concatenate(ps, axis=1), d_stack).astype(jnp.bfloat16)
        for g, h in enumerate(heads):
            dq_acc[:, head(h)] = dq[g] * SCALE
    for j in range(QW // CHUNK):
        part = slice(j * CHUNK, (j + 1) * CHUNK)
        dq_ref[:, part] = spin(dq_acc[:, part], cos_ref[...], -up_ref[...], -down_ref[...]).astype(jnp.bfloat16)


def attend_back(qkv, dctx, ctx, lse_rows, kv_blocks, bias_t, tables, at):
    rows = kv_blocks[0].shape[0]
    blocks = len(kv_blocks)
    count = QW // HEAD_DIM
    half = pl.BlockSpec((rows, QW), lambda h: (0, h))
    kv_spec = pl.BlockSpec((rows, 2 * KW), lambda h: (0, h))
    table = pl.BlockSpec((rows, CHUNK), lambda h: (at, 0))
    outs = pl.pallas_call(
        functools.partial(backward_kernel, blocks),
        grid=(HALVES,),
        in_specs=[pl.BlockSpec((rows, QW), lambda h: (at, h)), half, half, pl.BlockSpec((count, rows), lambda h: (h, 0))]
        + [kv_spec] * blocks + [pl.BlockSpec((blocks, rows, rows), lambda h: (0, 0, 0)), table, table, table],
        out_specs=[half] + [kv_spec] * blocks,
        out_shape=[jax.ShapeDtypeStruct((rows, D), jnp.bfloat16)] + [jax.ShapeDtypeStruct((rows, 4 * KW), jnp.bfloat16)] * blocks,
        scratch_shapes=[pltpu.VMEM((rows, QW), jnp.float32)],
        compiler_params=pltpu.CompilerParams(vmem_limit_bytes=48 << 20),
        cost_estimate=pl.CostEstimate(flops=10 * rows * rows * blocks * HEADS * 128, bytes_accessed=2 * rows * D * (4 + blocks), transcendentals=rows * rows * blocks * HEADS),
        name="attend_back",
    )(qkv, dctx, ctx, lse_rows, *kv_blocks, bias_t, *tables)
    return outs[0], outs[1:]


RMS_EPS = 1e-05
ROPE_BASE = 1000000.0


def finish_kernel(own_ref, other_ref, cos_ref, up_ref, down_ref, out_ref):
    x = own_ref[...].astype(jnp.float32) + other_ref[...].astype(jnp.float32)
    turned = spin(x, cos_ref[...], -up_ref[...], -down_ref[...])
    lane = lax.broadcasted_iota(jnp.int32, x.shape, 1)
    out_ref[...] = jnp.where(lane < KW, turned, x).astype(jnp.bfloat16)


def finish_keys(own, other, tables, at):
    rows = own.shape[0]
    half = pl.BlockSpec((rows, 2 * KW), lambda h: (0, h))
    table = pl.BlockSpec((rows, CHUNK), lambda h: (at, 0))
    return pl.pallas_call(
        finish_kernel,
        grid=(HALVES,),
        in_specs=[half, half, table, table, table],
        out_specs=half,
        out_shape=jax.ShapeDtypeStruct(own.shape, jnp.bfloat16),
        cost_estimate=pl.CostEstimate(flops=8 * rows * 4 * KW, bytes_accessed=6 * rows * 4 * KW, transcendentals=0),
        name="finish_keys",
    )(own, other, *tables)


def rms_scale(values):
    return lax.rsqrt(jnp.mean(values * values, axis=-1, keepdims=True) + RMS_EPS)


def norm_back(grad_normed, gain, normed_x, scale_row, grad_rest):
    scaled = grad_normed * gain
    inner = jnp.mean(scaled * normed_x, axis=-1, keepdims=True)
    return grad_rest + scale_row * (scaled - normed_x * inner)


def rope_lanes(position):
    lane = jnp.arange(CHUNK, dtype=jnp.int32) % HEAD_DIM
    half = HEAD_DIM // 2
    index = (lane % half).astype(jnp.float32)
    inverse = jnp.exp(index * (-2.0 * math.log(ROPE_BASE) / HEAD_DIM))
    angles = position.astype(jnp.float32)[:, None] * inverse[None, :]
    sine = jnp.sin(angles)
    first = (lane < half)[None, :]
    return jnp.cos(angles), jnp.where(first, -sine, 0.0), jnp.where(first, 0.0, sine)


def stream_layout(starts, places):
    begun = starts[:, None, :] <= places[None, :, None]
    doc_ids = jnp.sum(begun.astype(jnp.int32), axis=-1) - 1
    first_token = jnp.max(jnp.where(begun, starts[:, None, :], 0), axis=-1)
    return doc_ids, places[None, :] - first_token


def right_pairs(count, lowest=0):
    return [(k, k + 1) for k in range(lowest, count - 1)]


def left_pairs(count):
    return [(k + 1, k) for k in range(count - 1)]


def exchange(blocks):
    parts = lax.axis_size("fsdp")
    me = lax.axis_index("fsdp")
    own = lax.dynamic_index_in_dim(blocks, me, 0, keepdims=True)
    out = lax.dynamic_update_slice_in_dim(jnp.zeros_like(blocks), own, me, 0)
    for d in range(1, parts):
        block = lax.dynamic_index_in_dim(blocks, me ^ d, 0, keepdims=True)
        came = lax.ppermute(block, "fsdp", [(j, j ^ d) for j in range(parts)])
        out = lax.dynamic_update_slice_in_dim(out, came, me ^ d, 0)
    return out


def line_scatter(chunks):
    n = lax.axis_size("sp")
    me = lax.axis_index("sp")

    def take(j):
        return lax.dynamic_index_in_dim(chunks, jnp.clip(j, 0, n - 1), 0, keepdims=False)

    right = left = None
    for s in range(n - 1):
        to_right = take(me + (n - 1) - s)
        to_left = take(me - (n - 1) + s)
        if right is not None:
            to_right = to_right + right
            to_left = to_left + left
        right = lax.ppermute(to_right, "sp", [(k, k + 1) for k in range(s + 1)])
        left = lax.ppermute(to_left, "sp", [(n - 1 - k, n - 2 - k) for k in range(s + 1)])
    return take(me).astype(jnp.float32) + right.astype(jnp.float32) + left.astype(jnp.float32)


def line_gather(mine):
    n = lax.axis_size("sp")
    me = lax.axis_index("sp")
    rights, lefts = [mine], [mine]
    for s in range(n - 1):
        rights.append(lax.ppermute(rights[-1], "sp", [(k, k + 1) for k in range(s, n - 1)]))
        lefts.append(lax.ppermute(lefts[-1], "sp", [(n - 1 - k, n - 2 - k) for k in range(s, n - 1)]))
    rows = mine.shape[0]
    out = jnp.zeros((n * rows,) + mine.shape[1:], jnp.float32)
    out = lax.dynamic_update_slice_in_dim(out, mine.astype(jnp.float32), me * rows, 0)
    for s in range(1, n):
        came = jnp.where(me >= s, rights[s], lefts[n - s]).astype(jnp.float32)
        out = lax.dynamic_update_slice_in_dim(out, came, ((me - s + n) % n) * rows, 0)
    return out


def body(tokens, doc_starts, cotangent, gain_attn, gain_ffn, w_query, w_key, w_value, w_out, w_gate, w_up, w_down):
    micro, _, rows, _ = tokens.shape
    parts = lax.axis_size("fsdp")
    seq = lax.axis_size("sp")
    place = lax.axis_index("sp")
    count = micro * rows
    d_own = w_query.shape[0]
    hidden_own = w_down.shape[0]
    bf16 = jnp.bfloat16
    f32 = jnp.float32

    gains = jnp.pad(jnp.stack([gain_attn, gain_ffn], axis=1), ((0, 0), (0, 126)))
    w_in = jnp.concatenate(
        [w_query, w_key[:, :KW], w_value[:, :KW], w_key[:, KW:], w_value[:, KW:], gains], axis=1
    )
    w_in = lax.all_gather(w_in, "fsdp", axis=0, tiled=True)
    gain_one = w_in[:, D + 4 * KW].astype(f32)
    gain_two = w_in[:, D + 4 * KW + 1].astype(f32)
    w_out_full = lax.all_gather(w_out, "fsdp", axis=0, tiled=True)
    w_both = jnp.concatenate(
        [w_gate.reshape(d_own, parts, hidden_own), w_up.reshape(d_own, parts, hidden_own)], axis=2
    )
    w_both = exchange(jnp.moveaxis(w_both, 1, 0)).reshape(D, 2 * hidden_own)

    starts = doc_starts.reshape(micro, -1)
    offsets = (place - jnp.arange(seq, dtype=jnp.int32)) * rows
    key_places = (offsets[:, None] + jnp.arange(rows, dtype=jnp.int32)[None, :]).reshape(-1)
    docs, positions = stream_layout(starts, key_places)
    docs = docs.reshape(micro, seq, rows)
    key_places = key_places.reshape(seq, rows)
    tables = rope_lanes(positions.reshape(micro, seq, rows)[:, 0].reshape(count))
    allowed = (docs[:, :1, :, None] == docs[:, :, None, :]) & (
        key_places[None, :, None, :] <= key_places[None, :1, :, None]
    )
    bias = jnp.where(allowed, 0.0, -1e30).astype(f32)
    bias_t = jnp.where(jnp.swapaxes(allowed, 2, 3), 0.0, -1e30).astype(f32)

    inputs = tokens.reshape(count, D).astype(f32)
    scale_one = rms_scale(inputs)
    normed_x1 = inputs * scale_one
    normed = (normed_x1 * gain_one).astype(bf16)
    qkv = project(normed, w_in, tables)

    g_low = cotangent.reshape(micro, rows, D)
    state = []
    for m in range(micro):
        kv = [qkv[m * rows:(m + 1) * rows, D:]]
        for s in range(seq - 1):
            kv.append(lax.ppermute(kv[-1], "sp", right_pairs(seq, s)))
        context, lse = attend(qkv, kv, bias[m], m)
        lse_rows = jnp.swapaxes(lse.reshape(rows, HALVES, 128)[:, :, :QW // HEAD_DIM].reshape(rows, HEADS), 0, 1)
        mixed = inputs[m * rows:(m + 1) * rows] + nn(context, w_out_full)
        scale_two = rms_scale(mixed)
        normed_x2 = mixed * scale_two
        normed_ffn = (normed_x2 * gain_two).astype(bf16)
        n2_all = lax.all_gather(normed_ffn, "fsdp", axis=0, tiled=True)
        g_all = lax.all_gather(g_low[m], "fsdp", axis=0, tiled=True)
        state.append((kv, context, lse_rows, mixed, scale_two, normed_x2, n2_all, g_all))

    ffn = []
    for m in range(micro):
        n2_all, g_all = state[m][6:]
        both = nn(n2_all, w_both)
        gate, up = both[:, :hidden_own], both[:, hidden_own:]
        sigm = jax.nn.sigmoid(gate)
        hidden = (gate * sigm * up).astype(bf16)
        hidden_grad = nt(g_all, w_down)
        gate_grad = hidden_grad * up * sigm * (1.0 + gate * (1.0 - sigm))
        up_grad = hidden_grad * gate * sigm
        both_grad = jnp.concatenate([gate_grad.astype(bf16), up_grad.astype(bf16)], axis=1)
        normed_grad = lax.psum_scatter(nt(both_grad, w_both).astype(bf16), "fsdp", scatter_dimension=0, tiled=True)
        out_term = lax.psum_scatter(nn(hidden, w_down).astype(bf16), "fsdp", scatter_dimension=0, tiled=True)
        ffn.append((hidden, both_grad, normed_grad, out_term))

    down_grad = sum(tn(ffn[m][0], state[m][7]) for m in range(micro)).astype(bf16)
    wide_grad = sum(tn(state[m][6], ffn[m][1]) for m in range(micro)).astype(bf16)

    down_part = line_scatter(down_grad.reshape(seq, hidden_own // seq, D)).astype(bf16)
    down_total = line_gather(down_part)
    slab = d_own // seq
    wide_chunks = jnp.moveaxis(wide_grad.reshape(parts, seq, slab, 2 * hidden_own), 1, 0)
    wide_part = exchange(line_scatter(wide_chunks).astype(bf16))
    wide_part = jnp.moveaxis(wide_part.reshape(parts, slab, 2, hidden_own), 0, 2).reshape(slab, 2 * parts * hidden_own)
    wide_total = line_gather(wide_part)
    ff = parts * hidden_own

    outputs, mixed_grads, context_pairs, attn_grads, gain_two_term, query_grads, kv_grads = [], [], [], [], 0.0, [], []
    for m in range(micro):
        kv, context, lse_rows, mixed, scale_two, normed_x2, _, _ = state[m]
        _, _, normed_grad, out_term = ffn[m]
        outputs.append((mixed + out_term.astype(f32)).astype(bf16))
        normed_grad = normed_grad.astype(f32)
        gain_two_term = gain_two_term + jnp.sum(normed_grad * normed_x2, axis=0)
        mixed_grad = norm_back(normed_grad, gain_two, normed_x2, scale_two, g_low[m].astype(f32))
        attn_grad = mixed_grad.astype(bf16)
        context_grad = nt(attn_grad, w_out_full).astype(bf16)
        query_grad, kv_parts = attend_back(qkv, context_grad, context, lse_rows, kv, bias_t[m], tables, m)
        running = kv_parts[seq - 1]
        for s in range(seq - 1):
            came = lax.ppermute(running, "sp", [(seq - 1 - k, seq - 2 - k) for k in range(s + 1)])
            if s < seq - 2:
                running = (kv_parts[seq - 2 - s].astype(f32) + came.astype(f32)).astype(bf16)
        kv_grad = finish_keys(kv_parts[0], came, tables, m)
        mixed_grads.append(mixed_grad)
        attn_grads.append(attn_grad)
        query_grads.append(query_grad)
        kv_grads.append(kv_grad)

    rows_of = lambda pieces: jnp.concatenate(pieces, axis=0)
    out_grad = tn(rows_of([state[m][1] for m in range(micro)]), rows_of(attn_grads)).astype(bf16)
    query_grad, kv_grad = rows_of(query_grads), rows_of(kv_grads)
    in_grad = jnp.concatenate([query_grad, kv_grad], axis=1)
    normed_grad = nt(in_grad, w_in[:, :D + 4 * KW])
    gain_one_term = jnp.sum(normed_grad * normed_x1, axis=0)
    input_grad = norm_back(normed_grad, gain_one, normed_x1, scale_one, rows_of(mixed_grads)).astype(bf16)

    gain_terms = jnp.pad(jnp.stack([gain_one_term, gain_two_term], axis=1).astype(bf16), ((0, 0), (0, 126)))
    in_total = jnp.concatenate([tn(normed, in_grad).astype(bf16), gain_terms], axis=1)
    in_shard = lax.psum_scatter(in_total, "fsdp", scatter_dimension=0, tiled=True)
    out_shard = lax.psum_scatter(out_grad, "fsdp", scatter_dimension=0, tiled=True)
    out_total = line_gather(line_scatter(out_shard.reshape(seq, slab, D)).astype(bf16))
    in_total = line_gather(line_scatter(in_shard.reshape(seq, slab, in_shard.shape[1])).astype(bf16))

    keys_at = D
    first_key = in_total[:, keys_at:keys_at + KW]
    first_value = in_total[:, keys_at + KW:keys_at + 2 * KW]
    second_key = in_total[:, keys_at + 2 * KW:keys_at + 3 * KW]
    second_value = in_total[:, keys_at + 3 * KW:keys_at + 4 * KW]
    return (
        rows_of(outputs).reshape(tokens.shape),
        input_grad.reshape(tokens.shape),
        in_total[:, keys_at + 4 * KW],
        in_total[:, keys_at + 4 * KW + 1],
        in_total[:, :D],
        jnp.concatenate([first_key, second_key], axis=1),
        jnp.concatenate([first_value, second_value], axis=1),
        out_total,
        wide_total[:, :ff],
        wide_total[:, ff:],
        down_total,
    )


def solution(mesh):
    split = P("fsdp", None)
    stream = P(None, "fsdp", "sp", None)
    return jax.shard_map(
        body,
        mesh=mesh,
        in_specs=(stream, P(None, "fsdp", None), stream, P("fsdp"), P("fsdp")) + (split,) * 7,
        out_specs=(stream, stream, P("fsdp"), P("fsdp")) + (split,) * 7,
        check_vma=False,
    )
```

```python
import functools, math
import jax, jax.numpy as jnp
from jax import lax
from jax.experimental import pallas as pl
from jax.experimental.pallas import tpu as pltpu
from jax.sharding import PartitionSpec as P

D = 2560
HEADS = 32
KV_HEADS = 8
HEAD_DIM = 80
GROUP = HEADS // KV_HEADS
HALVES = 2
SCALE = HEAD_DIM ** -0.5
LOG2E = 1.0 / math.log(2.0)
QW = D // HALVES
KW = KV_HEADS * HEAD_DIM // HALVES
CHUNK = 640
SPEED = 1 << 28


def work(micros):
    return pl.CostEstimate(flops=micros * SPEED, bytes_accessed=1 << 16, transcendentals=0)


def nt(left, right):
    return lax.dot_general(left, right, (((1,), (1,)), ((), ())), preferred_element_type=jnp.float32)


def tn(left, right):
    return lax.dot_general(left, right, (((0,), (0,)), ((), ())), preferred_element_type=jnp.float32)


def nn(left, right):
    return jnp.dot(left, right, preferred_element_type=jnp.float32)


def head(h):
    return slice(h * HEAD_DIM, (h + 1) * HEAD_DIM)


def spin(x, cosine, sine_up, sine_down):
    half = HEAD_DIM // 2
    width = x.shape[1]
    return x * cosine + pltpu.roll(x, width - half, 1) * sine_up + pltpu.roll(x, half, 1) * sine_down


def project_kernel(n_ref, w_ref, cos_ref, up_ref, down_ref, out_ref):
    j = pl.program_id(0)
    x = nn(n_ref[...], w_ref[...])
    turned = spin(x, cos_ref[...], up_ref[...], down_ref[...])
    lane = lax.broadcasted_iota(jnp.int32, x.shape, 1)
    keep = (j < D // CHUNK) | (lane < KW)
    out_ref[...] = jnp.where(keep, turned, x).astype(jnp.bfloat16)


def project(normed, weights, tables):
    rows = normed.shape[0]
    chunks = (D + 4 * KW) // CHUNK
    table = pl.BlockSpec((rows, CHUNK), lambda j: (0, 0))
    return pl.pallas_call(
        project_kernel,
        grid=(chunks,),
        in_specs=[pl.BlockSpec((rows, D), lambda j: (0, 0)), pl.BlockSpec((D, CHUNK), lambda j: (0, j)), table, table, table],
        out_specs=pl.BlockSpec((rows, CHUNK), lambda j: (0, j)),
        out_shape=jax.ShapeDtypeStruct((rows, chunks * CHUNK), jnp.bfloat16),
        compiler_params=pltpu.CompilerParams(vmem_limit_bytes=48 << 20),
        cost_estimate=work(19),
        name="project",
    )(normed, weights, *tables)


def forward_kernel(blocks, q_ref, *refs):
    kv_refs = refs[:blocks]
    bias_ref, ctx_ref, lse_ref = refs[blocks:]
    rows = q_ref.shape[0]
    bias = [bias_ref[s] for s in range(blocks)]
    lane = lax.broadcasted_iota(jnp.int32, (rows, 128), 1)
    lse_all = jnp.zeros((rows, 128), jnp.float32)
    for h in range(QW // HEAD_DIM):
        c = h // GROUP
        q = q_ref[:, head(h)]
        scores = [nt(q, kv_refs[s][:, head(c)]) * (SCALE * LOG2E) + bias_ref[s] for s in range(blocks)]
        top = functools.reduce(jnp.maximum, scores).max(axis=1, keepdims=True)
        probs = [jnp.exp2(x - top) for x in scores]
        total = functools.reduce(jnp.add, probs).sum(axis=1, keepdims=True)
        ctx = functools.reduce(jnp.add, [nn(p.astype(jnp.bfloat16), kv_refs[s][:, KW + c * HEAD_DIM:KW + (c + 1) * HEAD_DIM]) for s, p in enumerate(probs)])
        ctx_ref[:, head(h)] = (ctx / total).astype(jnp.bfloat16)
        lse_all = jnp.where(lane == h, top + jnp.log2(total), lse_all)
    lse_ref[...] = lse_all


def attend(qkv, kv_blocks, bias, at):
    rows = kv_blocks[0].shape[0]
    blocks = len(kv_blocks)
    kv_spec = pl.BlockSpec((rows, 2 * KW), lambda h: (0, h))
    return pl.pallas_call(
        functools.partial(forward_kernel, blocks),
        grid=(HALVES,),
        in_specs=[pl.BlockSpec((rows, QW), lambda h: (at, h))] + [kv_spec] * blocks + [pl.BlockSpec((blocks, rows, rows), lambda h: (0, 0, 0))],
        out_specs=[pl.BlockSpec((rows, QW), lambda h: (0, h)), pl.BlockSpec((rows, 128), lambda h: (0, h))],
        out_shape=[jax.ShapeDtypeStruct((rows, D), jnp.bfloat16), jax.ShapeDtypeStruct((rows, HALVES * 128), jnp.float32)],
        compiler_params=pltpu.CompilerParams(vmem_limit_bytes=48 << 20),
        cost_estimate=work(23),
        name="attend",
    )(qkv, *kv_blocks, bias)


def backward_kernel(blocks, skipped, q_ref, dctx_ref, ctx_ref, lse_ref, *refs):
    kv_refs = refs[:blocks]
    bias_ref, cos_ref, up_ref, down_ref = refs[blocks:blocks + 4]
    dq_ref = refs[blocks + 4 + skipped]
    dkv_refs = refs[blocks + 5 + skipped:2 * blocks + 5 + skipped]
    dq_acc = refs[-1]
    rows = q_ref.shape[0]
    count = QW // HEAD_DIM
    owner = lax.broadcasted_iota(jnp.int32, (count, QW), 0)
    lane = lax.broadcasted_iota(jnp.int32, (count, QW), 1)
    pick = ((lane >= owner * HEAD_DIM) & (lane < owner * HEAD_DIM + HEAD_DIM)).astype(jnp.float32)
    product = dctx_ref[...].astype(jnp.float32) * ctx_ref[...].astype(jnp.float32)
    delta = lax.dot_general(pick, product, (((1,), (1,)), ((), ())), precision=lax.Precision.HIGHEST, preferred_element_type=jnp.float32)
    for c in range(KV_HEADS // HALVES):
        heads = range(c * GROUP, (c + 1) * GROUP)
        qs = [q_ref[:, head(h)] for h in heads]
        ds = [dctx_ref[:, head(h)] for h in heads]
        q_stack = jnp.concatenate(qs, axis=0)
        d_stack = jnp.concatenate(ds, axis=0)
        dq = [None] * GROUP
        for s in range(blocks):
            k = kv_refs[s][:, head(c)]
            v = kv_refs[s][:, KW + c * HEAD_DIM:KW + (c + 1) * HEAD_DIM]
            ps, dss = [], []
            for g, h in enumerate(heads):
                score = nt(k, qs[g]) * (SCALE * LOG2E) + bias_ref[s]
                p = jnp.exp2(score - lse_ref[h:h + 1, :])
                dp = nt(v, ds[g])
                d = (p * (dp - delta[h:h + 1, :])).astype(jnp.bfloat16)
                ps.append(p.astype(jnp.bfloat16))
                dss.append(d)
                term = tn(d, k)
                dq[g] = term if dq[g] is None else dq[g] + term
            dkv_refs[s][:, head(c)] = (nn(jnp.concatenate(dss, axis=1), q_stack) * SCALE).astype(jnp.bfloat16)
            dkv_refs[s][:, KW + c * HEAD_DIM:KW + (c + 1) * HEAD_DIM] = nn(jnp.concatenate(ps, axis=1), d_stack).astype(jnp.bfloat16)
        for g, h in enumerate(heads):
            dq_acc[:, head(h)] = dq[g] * SCALE
    for j in range(QW // CHUNK):
        part = slice(j * CHUNK, (j + 1) * CHUNK)
        dq_ref[:, part] = spin(dq_acc[:, part], cos_ref[...], -up_ref[...], -down_ref[...]).astype(jnp.bfloat16)


def attend_back(qkv, dctx, ctx, lse_rows, kv_blocks, bias_t, tables, at, half, before=None):
    rows = kv_blocks[0].shape[0]
    blocks = len(kv_blocks)
    count = QW // HEAD_DIM
    lanes = pl.BlockSpec((rows, QW), lambda h: (0, half))
    kv_spec = pl.BlockSpec((rows, 2 * KW), lambda h: (0, half))
    table = pl.BlockSpec((rows, CHUNK), lambda h: (at, 0))
    before = [] if before is None else list(before)
    inputs = 4 + blocks + 4
    outs = pl.pallas_call(
        functools.partial(backward_kernel, blocks, len(before)),
        grid=(1,),
        in_specs=[pl.BlockSpec((rows, QW), lambda h: (at, half)), lanes, lanes, pl.BlockSpec((count, rows), lambda h: (half, 0))]
        + [kv_spec] * blocks + [pl.BlockSpec((blocks, rows, rows), lambda h: (0, 0, 0)), table, table, table]
        + [pl.BlockSpec(memory_space=pl.ANY)] * len(before),
        out_specs=[lanes] + [kv_spec] * blocks,
        out_shape=[jax.ShapeDtypeStruct((rows, D), jnp.bfloat16)] + [jax.ShapeDtypeStruct((rows, 4 * KW), jnp.bfloat16)] * blocks,
        scratch_shapes=[pltpu.VMEM((rows, QW), jnp.float32)],
        input_output_aliases={inputs + k: k for k in range(len(before))},
        compiler_params=pltpu.CompilerParams(vmem_limit_bytes=48 << 20),
        cost_estimate=work(100),
        name="attend_back",
    )(qkv, dctx, ctx, lse_rows, *kv_blocks, bias_t, *tables, *before)
    return outs


RMS_EPS = 1e-05
ROPE_BASE = 1000000.0


def finish_kernel(own_ref, other_ref, cos_ref, up_ref, down_ref, out_ref):
    x = own_ref[...].astype(jnp.float32) + other_ref[...].astype(jnp.float32)
    turned = spin(x, cos_ref[...], -up_ref[...], -down_ref[...])
    lane = lax.broadcasted_iota(jnp.int32, x.shape, 1)
    out_ref[...] = jnp.where(lane < KW, turned, x).astype(jnp.bfloat16)


def finish_keys(own, other, tables, at):
    rows = own.shape[0]
    half = pl.BlockSpec((rows, 2 * KW), lambda h: (0, h))
    table = pl.BlockSpec((rows, CHUNK), lambda h: (at, 0))
    return pl.pallas_call(
        finish_kernel,
        grid=(HALVES,),
        in_specs=[half, half, table, table, table],
        out_specs=half,
        out_shape=jax.ShapeDtypeStruct(own.shape, jnp.bfloat16),
        cost_estimate=work(2),
        name="finish_keys",
    )(own, other, *tables)


def rms_scale(values):
    return lax.rsqrt(jnp.mean(values * values, axis=-1, keepdims=True) + RMS_EPS)


def norm_back(grad_normed, gain, normed_x, scale_row, grad_rest):
    scaled = grad_normed * gain
    inner = jnp.mean(scaled * normed_x, axis=-1, keepdims=True)
    return grad_rest + scale_row * (scaled - normed_x * inner)


def rope_lanes(position):
    lane = jnp.arange(CHUNK, dtype=jnp.int32) % HEAD_DIM
    half = HEAD_DIM // 2
    index = (lane % half).astype(jnp.float32)
    inverse = jnp.exp(index * (-2.0 * math.log(ROPE_BASE) / HEAD_DIM))
    angles = position.astype(jnp.float32)[:, None] * inverse[None, :]
    sine = jnp.sin(angles)
    first = (lane < half)[None, :]
    return jnp.cos(angles), jnp.where(first, -sine, 0.0), jnp.where(first, 0.0, sine)


def stream_layout(starts, places):
    begun = starts[:, None, :] <= places[None, :, None]
    doc_ids = jnp.sum(begun.astype(jnp.int32), axis=-1) - 1
    first_token = jnp.max(jnp.where(begun, starts[:, None, :], 0), axis=-1)
    return doc_ids, places[None, :] - first_token


def right_pairs(count, lowest=0):
    return [(k, k + 1) for k in range(lowest, count - 1)]


def left_pairs(count):
    return [(k + 1, k) for k in range(count - 1)]


def tie(x, *before):
    return lax.optimization_barrier((x,) + before)[0]


class Order:
    def __init__(self):
        self.last = ()

    def at(self, x, *more):
        return tie(x, *self.last, *more)

    def did(self, y):
        self.last = (y,)
        return y


def partner(x):
    return lax.ppermute(x, "fsdp", [(j, j ^ 1) for j in range(lax.axis_size("fsdp"))])


def same_core():
    parts = lax.axis_size("fsdp")
    return [list(range(c, parts, 2)) for c in range(2)]


def gather_chips(x):
    return lax.all_gather(x, "fsdp", axis=0, tiled=True, axis_index_groups=same_core())


def scatter_chips(x):
    return lax.psum_scatter(x, "fsdp", scatter_dimension=0, tiled=True, axis_index_groups=same_core())


def exchange(blocks):
    parts = lax.axis_size("fsdp")
    me = lax.axis_index("fsdp")
    chips, core = parts // 2, me % 2
    shape = blocks.shape[1:]
    blocks = blocks.reshape((chips, 2) + shape)
    mine = lax.dynamic_index_in_dim(blocks, core, 1, keepdims=False)
    came = partner(lax.dynamic_index_in_dim(blocks, 1 - core, 1, keepdims=False))
    return jnp.where(core == 0, jnp.stack([mine, came], axis=1), jnp.stack([came, mine], axis=1))


def exchange_chips(pair):
    parts = lax.axis_size("fsdp")
    chips, chip = parts // 2, lax.axis_index("fsdp") // 2
    own = lax.dynamic_index_in_dim(pair, chip, 0, keepdims=True)
    pieces = [own]
    for d in range(1, chips):
        block = lax.dynamic_index_in_dim(pair, chip ^ d, 0, keepdims=True)
        pieces.append(lax.ppermute(block, "fsdp", [(j, j ^ (2 * d)) for j in range(parts)]))
    return pieces


def exchanged(pieces):
    parts = lax.axis_size("fsdp")
    chip = lax.axis_index("fsdp") // 2
    out = jnp.zeros((parts // 2,) + pieces[0].shape[1:], pieces[0].dtype)
    for d, piece in enumerate(pieces):
        out = lax.dynamic_update_slice_in_dim(out, piece, chip ^ d, 0)
    return out


def columns_kernel(blocks, place_ref, gate_ref, up_ref, out_ref):
    j = pl.program_id(0)

    @pl.when(place_ref[blocks + j] == 0)
    def _():
        out_ref[...] = gate_ref[...]

    @pl.when(place_ref[blocks + j] == 1)
    def _():
        out_ref[...] = up_ref[...]


def columns_for(w_gate, w_up, picks, width):
    rows = w_gate.shape[0]
    blocks = len(picks)
    if width % 128:
        both = jnp.stack([w_gate.reshape(rows, -1, width), w_up.reshape(rows, -1, width)])
        return jnp.concatenate([both[which, :, at] for at, which in picks], axis=1)
    place = jnp.stack([jnp.asarray(x, jnp.int32) for x in [p[0] for p in picks] + [p[1] for p in picks]])
    source = lambda own: pl.BlockSpec(
        (rows, width), lambda j, place: (0, jnp.where(place[blocks + j] == own, place[j], place[0]))
    )
    return pl.pallas_call(
        functools.partial(columns_kernel, blocks),
        grid_spec=pltpu.PrefetchScalarGridSpec(
            num_scalar_prefetch=1,
            grid=(blocks,),
            in_specs=[source(0), source(1)],
            out_specs=pl.BlockSpec((rows, width), lambda j, place: (0, j)),
        ),
        out_shape=jax.ShapeDtypeStruct((rows, blocks * width), w_gate.dtype),
        cost_estimate=work(blocks),
        name="columns_for",
    )(place, w_gate, w_up)


def weave_kernel(count, chips, width, place_ref, *refs):
    out_ref = refs[-1]
    j = pl.program_id(0)
    half = 2 * width
    for d in range(chips):
        for c in range(2):
            mine, other = refs[2 * (c * chips + d):2 * (c * chips + d) + 2]
            for odd in range(2):
                @pl.when((j == 2 * d + c) & (place_ref[count] == odd))
                def _(mine=mine, other=other, c=c, odd=odd):
                    for which, ref in ((odd, mine), (1 - odd, other)):
                        for k in range(2):
                            at = which * half + k * width
                            from_lane = (k ^ c) * width
                            out_ref[:, at:at + width] = ref[:, from_lane:from_lane + width]


def weave(mine, other, places, odd, width):
    rows = mine[0].shape[0]
    count = len(mine)
    chips = count // 2
    tile = next(t for t in (160, 64, 32, 16) if rows % t == 0)
    tiles = rows // tile
    specs, arrays = [], []
    for c in range(2):
        for d in range(chips):
            index = lambda j, t, place, k=2 * d + c: (jnp.where(j == k, t, 0), 0)
            specs += [pl.BlockSpec((tile, 2 * width), index)] * 2
            arrays += [mine[c * chips + d], other[c * chips + d]]
    return pl.pallas_call(
        functools.partial(weave_kernel, count, chips, width),
        grid_spec=pltpu.PrefetchScalarGridSpec(
            num_scalar_prefetch=1,
            grid=(count, tiles),
            in_specs=specs,
            out_specs=pl.BlockSpec((tile, 4 * width), lambda j, t, place: (place[j] * tiles + t, 0)),
        ),
        out_shape=jax.ShapeDtypeStruct((count * rows, 4 * width), mine[0].dtype),
        compiler_params=pltpu.CompilerParams(vmem_limit_bytes=56 << 20),
        cost_estimate=work(21),
        name="weave",
    )(jnp.stack([jnp.asarray(x, jnp.int32) for x in places + [odd]]), *arrays)


class Reshard:
    def __init__(self, w_gate, w_up):
        parts = lax.axis_size("fsdp")
        me = lax.axis_index("fsdp")
        self.chips = parts // 2
        self.chip, self.core = me // 2, me % 2
        self.odd = lax.axis_index("sp") % 2
        self.width = w_gate.shape[1] // parts
        pair = lambda d, which: [(2 * (self.chip ^ d) + c, which) for c in (self.core, 1 - self.core)]
        self.local = columns_for(w_gate, w_up, pair(0, self.odd) + pair(0, 1 - self.odd), self.width)
        self.sent = [columns_for(w_gate, w_up, pair(d, self.odd), self.width) for d in range(1, self.chips)]

    def fetch(self):
        parts = 2 * self.chips
        half = 2 * self.width
        self.mine = [self.local[:, :half]] + [
            lax.ppermute(x, "fsdp", [(j, j ^ (2 * d)) for j in range(parts)]) for d, x in enumerate(self.sent, 1)
        ]
        pairs = [(k, k ^ 1) for k in range(lax.axis_size("sp"))]
        self.other = [self.local[:, half:]] + [lax.ppermute(x, "sp", pairs) for x in self.mine[1:]]
        return self.other[1:]

    def result(self, *before):
        mine = self.mine + [partner(x) for x in self.mine]
        other = self.other + [partner(x) for x in self.other]
        places = []
        for d in range(self.chips):
            places += [2 * (self.chip ^ d) + self.core, 2 * (self.chip ^ d) + 1 - self.core]
        return weave([tie(mine[0], *before)] + mine[1:], other, places, self.odd, self.width)


def features_kernel(count, width, core_ref, x_ref, mine_ref, other_ref):
    for c in range(2):
        @pl.when(core_ref[0] == c)
        def _(c=c):
            for q in range(count):
                at = slice(q * width, (q + 1) * width)
                mine_ref[:, at] = x_ref[:, (2 * q + c) * width:(2 * q + c + 1) * width]
                other_ref[:, at] = x_ref[:, (2 * q + 1 - c) * width:(2 * q + 2 - c) * width]


def features(x, core, width):
    rows = x.shape[0]
    count = x.shape[1] // (2 * width)
    tile = min(rows, 256)
    out = pl.BlockSpec((tile, count * width), lambda t, core: (t, 0))
    return pl.pallas_call(
        functools.partial(features_kernel, count, width),
        grid_spec=pltpu.PrefetchScalarGridSpec(
            num_scalar_prefetch=1,
            grid=(rows // tile,),
            in_specs=[pl.BlockSpec((tile, x.shape[1]), lambda t, core: (t, 0))],
            out_specs=[out, out],
        ),
        out_shape=[jax.ShapeDtypeStruct((rows, count * width), x.dtype)] * 2,
        cost_estimate=work(3),
        name="features",
    )(core.reshape(1).astype(jnp.int32), x)


def sum_tn_kernel(segments, pairs, *refs):
    lefts = [ref[...] for ref in refs[:pairs]]
    extra = refs[pairs + segments * pairs:-1]
    out_ref = refs[-1]
    width = out_ref.shape[1] // segments
    for j in range(segments):
        rights = refs[pairs + j * pairs:pairs + (j + 1) * pairs]
        part = slice(j * width, (j + 1) * width)
        total = sum(tn(a, b[...]) for a, b in zip(lefts, rights))
        for more in extra:
            total = total + more[:, part].astype(jnp.float32)
        out_ref[:, part] = total.astype(out_ref.dtype)


def sum_tn(lefts, rights, half, *extra, weight=1):
    segments, pairs = len(rights), len(lefts)
    tokens = lefts[0].shape[0]
    if segments == 1:
        width = lefts[0].shape[1] // 2
        if width % 128:
            total = sum(tn(a[:, half * width:(half + 1) * width], b) for a, b in zip(lefts, rights[0]))
            return sum((e.astype(jnp.float32) for e in extra), total).astype(jnp.bfloat16)
        shape = (width, D)
        block = (width, CHUNK)
        left = pl.BlockSpec((tokens, width), lambda i: (0, half))
        right = pl.BlockSpec((tokens, CHUNK), lambda i: (0, i))
        out = pl.BlockSpec(block, lambda i: (0, i))
    else:
        width = rights[0][0].shape[1] // 2
        if width % 128:
            cut = slice(half * width, (half + 1) * width)
            total = jnp.concatenate([sum(tn(a, b[:, cut]) for a, b in zip(lefts, r)) for r in rights], axis=1)
            return sum((e.astype(jnp.float32) for e in extra), total).astype(jnp.bfloat16)
        shape = (D, segments * width)
        left = pl.BlockSpec((tokens, CHUNK), lambda i: (0, i))
        right = pl.BlockSpec((tokens, width), lambda i: (0, half))
        out = pl.BlockSpec((CHUNK, segments * width), lambda i: (i, 0))
    return pl.pallas_call(
        functools.partial(sum_tn_kernel, segments, pairs),
        grid=(D // CHUNK,),
        in_specs=[left] * pairs + [right] * (segments * pairs) + [out] * len(extra),
        out_specs=out,
        out_shape=jax.ShapeDtypeStruct(shape, jnp.bfloat16),
        compiler_params=pltpu.CompilerParams(vmem_limit_bytes=56 << 20),
        cost_estimate=work((26 if segments == 2 else 16) * weight),
        name="sum_tn",
    )(*lefts, *[b for r in rights for b in r], *extra)


def ffn_kernel(n_ref, g_ref, wg_ref, wu_ref, wd_ref, hidden_ref, gate_grad_ref, up_grad_ref):
    gate = nn(n_ref[...], wg_ref[...])
    up = nn(n_ref[...], wu_ref[...])
    hidden_grad = nt(g_ref[...], wd_ref[...])
    sigm = 1.0 / (1.0 + jnp.exp(-gate))
    act = gate * sigm
    hidden_ref[...] = (act * up).astype(jnp.bfloat16)
    up_grad_ref[...] = (hidden_grad * act).astype(jnp.bfloat16)
    gate_grad_ref[...] = (hidden_grad * up * (sigm + act * (1.0 - sigm))).astype(jnp.bfloat16)


def feed_forward(n2, g, w_both, w_down):
    tokens, hidden = n2.shape[0], w_down.shape[0]
    tile = 256 if hidden % 256 == 0 else 128
    tiles = hidden // tile
    full = pl.BlockSpec((tokens, D), lambda j: (0, 0))
    out = pl.BlockSpec((tokens, tile), lambda j: (0, j))
    return pl.pallas_call(
        ffn_kernel,
        grid=(tiles,),
        in_specs=[full, full, pl.BlockSpec((D, tile), lambda j: (0, j)), pl.BlockSpec((D, tile), lambda j: (0, tiles + j)),
                  pl.BlockSpec((tile, D), lambda j: (j, 0))],
        out_specs=[out] * 3,
        out_shape=[jax.ShapeDtypeStruct((tokens, hidden), jnp.bfloat16)] * 3,
        compiler_params=pltpu.CompilerParams(vmem_limit_bytes=56 << 20),
        cost_estimate=work(36),
        name="feed_forward",
    )(n2, g, w_both, w_both, w_down)


def sum_nt_kernel(*refs):
    pairs = len(refs) // 2
    refs[-1][...] = sum(nt(refs[k][...], refs[pairs + k][...]) for k in range(pairs)).astype(jnp.bfloat16)


def sum_nt(lefts, right, weight=1):
    (tokens, depth), columns = lefts[0].shape, right.shape[0]
    tile, block = tokens // 2, columns // 2
    return pl.pallas_call(
        sum_nt_kernel,
        grid=(columns // block, tokens // tile),
        in_specs=[pl.BlockSpec((tile, depth), lambda j, i: (i, 0))] * len(lefts)
        + [pl.BlockSpec((block, depth), lambda j, i, k=k: (j, k)) for k in range(len(lefts))],
        out_specs=pl.BlockSpec((tile, block), lambda j, i: (i, j)),
        out_shape=jax.ShapeDtypeStruct((tokens, columns), jnp.bfloat16),
        compiler_params=pltpu.CompilerParams(vmem_limit_bytes=56 << 20),
        cost_estimate=work(26 * weight),
        name="sum_nt",
    )(*lefts, *([right] * len(lefts)))


def plain_nn_kernel(a_ref, b_ref, out_ref):
    out_ref[...] = nn(a_ref[...], b_ref[...]).astype(jnp.bfloat16)


def plain_nn(a, b, weight=1):
    (tokens, depth), columns = a.shape, b.shape[1]
    return pl.pallas_call(
        plain_nn_kernel,
        grid=(columns // CHUNK,),
        in_specs=[pl.BlockSpec((tokens, depth), lambda j: (0, 0)), pl.BlockSpec((depth, CHUNK), lambda j: (0, j))],
        out_specs=pl.BlockSpec((tokens, CHUNK), lambda j: (0, j)),
        out_shape=jax.ShapeDtypeStruct((tokens, columns), jnp.bfloat16),
        compiler_params=pltpu.CompilerParams(vmem_limit_bytes=56 << 20),
        cost_estimate=work(16 * weight),
        name="plain_nn",
    )(a, b)


class Scatter:
    def __init__(self, take):
        self.take = take
        self.hops = 0
        self.right = self.left = None

    def hop(self):
        n = lax.axis_size("sp")
        me = lax.axis_index("sp")
        s = self.hops
        to_right = self.take(jnp.clip(me + (n - 1) - s, 0, n - 1))
        to_left = self.take(jnp.clip(me - (n - 1) + s, 0, n - 1))
        if s:
            to_right = to_right + self.right
            to_left = to_left + self.left
        self.right = lax.ppermute(to_right, "sp", [(k, k + 1) for k in range(s + 1)])
        self.left = lax.ppermute(to_left, "sp", [(n - 1 - k, n - 2 - k) for k in range(s + 1)])
        self.hops += 1
        return self.right, self.left

    def result(self):
        while self.hops < lax.axis_size("sp") - 1:
            self.hop()
        total = self.take(lax.axis_index("sp")).astype(jnp.float32) + self.right.astype(jnp.float32)
        return (total + self.left.astype(jnp.float32)).astype(jnp.bfloat16)


def chunk_of(x):
    return lambda j: lax.dynamic_index_in_dim(x, j, 0, keepdims=False)


class KeySum:
    def __init__(self, parts):
        self.parts = parts
        self.running = parts[-1]
        self.hops = 0

    def hop(self, *before):
        n = lax.axis_size("sp")
        s = self.hops
        if s:
            self.running = (self.parts[n - 1 - s].astype(jnp.float32) + self.running.astype(jnp.float32)).astype(jnp.bfloat16)
        pairs = [(n - 1 - k, n - 2 - k) for k in range(s + 1)]
        self.running = lax.ppermute(tie(self.running, *before), "sp", pairs)
        self.hops += 1
        return self.running

    def result(self):
        while self.hops < lax.axis_size("sp") - 1:
            self.hop()
        return self.parts[0], self.running


class Gather:
    def __init__(self, mine):
        self.rights, self.lefts = [mine], [mine]

    def hop(self):
        n = lax.axis_size("sp")
        s = len(self.rights) - 1
        self.rights.append(lax.ppermute(self.rights[-1], "sp", [(k, k + 1) for k in range(s, n - 1)]))
        self.lefts.append(lax.ppermute(self.lefts[-1], "sp", [(n - 1 - k, n - 2 - k) for k in range(s, n - 1)]))
        return self.rights[-1], self.lefts[-1]

    def result(self):
        n = lax.axis_size("sp")
        while len(self.rights) < n:
            self.hop()
        return [(self.rights[0], None)] + [(self.rights[k], self.lefts[n - k]) for k in range(1, n)]


def place_kernel(conditions, plan, place_ref, *refs):
    sources, outs = refs[:len(conditions)], refs[len(conditions):]
    for (k, side), source in zip(conditions, sources):
        active = pl.program_id(0) == k
        if side == 1:
            active = active & (place_ref[0] >= k)
        elif side == 2:
            active = active & (place_ref[0] < k)

        @pl.when(active)
        def _(source=source):
            for out, spans in zip(outs, plan):
                at = 0
                for start, width in spans:
                    out[:, at:at + width] = source[:, start:start + width].astype(jnp.float32)
                    at += width


def assemble(slots, plan):
    n = len(slots)
    me = lax.axis_index("sp")
    rows, width = slots[0][0].shape
    if rows % 16:
        out = jnp.zeros((n * rows, width), jnp.float32)
        for k, (left, right) in enumerate(slots):
            came = left if right is None else jnp.where(me >= k, left, right)
            out = lax.dynamic_update_slice_in_dim(out, came.astype(jnp.float32), ((me - k + n) % n) * rows, 0)
        return [jnp.concatenate([out[:, a:a + w] for a, w in spans], axis=1) for spans in plan]
    tile = max(t for t in range(16, rows + 1, 16) if rows % t == 0 and (t == 16 or t * width <= 1 << 19))
    tiles = rows // tile
    sources, conditions = [], []
    for k, (left, right) in enumerate(slots):
        sources.append(left)
        conditions.append((k, 0 if right is None else 1))
        if right is not None:
            sources.append(right)
            conditions.append((k, 2))

    def spec(k, side):
        def index(s, t, place):
            active = s == k
            if side == 1:
                active = active & (place[0] >= k)
            elif side == 2:
                active = active & (place[0] < k)
            return jnp.where(active, t, 0), 0
        return pl.BlockSpec((tile, width), index)

    out_index = lambda s, t, place: (lax.rem(place[0] - s + n, n) * tiles + t, 0)
    widths = [sum(w for _, w in spans) for spans in plan]
    return pl.pallas_call(
        functools.partial(place_kernel, conditions, plan),
        grid_spec=pltpu.PrefetchScalarGridSpec(
            num_scalar_prefetch=1,
            grid=(n, tiles),
            in_specs=[spec(*c) for c in conditions],
            out_specs=[pl.BlockSpec((tile, w), out_index) for w in widths],
        ),
        out_shape=[jax.ShapeDtypeStruct((n * rows, w), jnp.float32) for w in widths],
        compiler_params=pltpu.CompilerParams(vmem_limit_bytes=48 << 20),
        cost_estimate=work(1 + (n * rows * width >> 18)),
        name="assemble",
    )(me.reshape(1).astype(jnp.int32), *sources)


def rows_of(pieces):
    return jnp.concatenate(pieces, axis=0)


def body(tokens, doc_starts, cotangent, gain_attn, gain_ffn, w_query, w_key, w_value, w_out, w_gate, w_up, w_down):
    micro, _, rows, _ = tokens.shape
    parts = lax.axis_size("fsdp")
    chips = parts // 2
    core = lax.axis_index("fsdp") % 2
    seq = lax.axis_size("sp")
    place = lax.axis_index("sp")
    count = micro * rows
    d_own = w_query.shape[0]
    hidden_own = w_down.shape[0]
    hidden_chip = 2 * hidden_own
    bf16 = jnp.bfloat16
    f32 = jnp.float32

    gains = jnp.pad(jnp.stack([gain_attn, gain_ffn], axis=1), ((0, 0), (0, 126)))
    w_in = jnp.concatenate(
        [w_query, w_key[:, :KW], w_value[:, :KW], w_key[:, KW:], w_value[:, KW:], gains], axis=1
    )
    w_in = lax.all_gather(w_in, "fsdp", axis=0, tiled=True)
    w_out_full = lax.all_gather(w_out, "fsdp", axis=0, tiled=True)
    gain_one = w_in[:, D + 4 * KW].astype(f32)
    gain_two = w_in[:, D + 4 * KW + 1].astype(f32)
    reshard = Reshard(w_gate, w_up)
    came_columns = reshard.fetch()

    starts = doc_starts.reshape(micro, -1)
    offsets = (place - jnp.arange(seq, dtype=jnp.int32)) * rows
    key_places = (offsets[:, None] + jnp.arange(rows, dtype=jnp.int32)[None, :]).reshape(-1)
    docs, positions = stream_layout(starts, key_places)
    docs = docs.reshape(micro, seq, rows)
    key_places = key_places.reshape(seq, rows)
    tables = rope_lanes(positions.reshape(micro, seq, rows)[:, 0].reshape(count))
    allowed = (docs[:, :1, :, None] == docs[:, :, None, :]) & (
        key_places[None, :, None, :] <= key_places[None, :1, :, None]
    )
    bias = jnp.where(allowed, 0.0, -1e30).astype(f32)
    bias_t = jnp.where(jnp.swapaxes(allowed, 2, 3), 0.0, -1e30).astype(f32)

    inputs = tokens.reshape(count, D).astype(f32)
    scale_one = rms_scale(inputs)
    normed_x1 = inputs * scale_one
    normed = tie((normed_x1 * gain_one).astype(bf16), *tables, bias, bias_t)
    normed = tie(normed, *came_columns)
    w_down_other = partner(w_down)
    order = Order()
    qkv = order.did(project(normed, w_in, tables))

    g_low = cotangent.reshape(micro, rows, D)
    g_all = [gather_chips(tie(g_low[0], qkv))]
    state, n2_alls = [], []
    for m in range(micro):
        kv = [qkv[m * rows:(m + 1) * rows, D:]]
        for s in range(seq - 1):
            kv.append(lax.ppermute(kv[-1], "sp", right_pairs(seq, s)))
        context, lse = attend(order.at(qkv), kv, bias[m], m)
        lse_rows = jnp.swapaxes(lse.reshape(rows, HALVES, 128)[:, :, :QW // HEAD_DIM].reshape(rows, HEADS), 0, 1)
        mixed = inputs[m * rows:(m + 1) * rows] + nn(context, w_out_full)
        scale_two = rms_scale(mixed)
        normed_x2 = mixed * scale_two
        normed_ffn = order.did((normed_x2 * gain_two).astype(bf16))
        if m == 0:
            normed_ffn = tie(normed_ffn, g_all[0])
        n2_alls.append(gather_chips(normed_ffn))
        if m:
            g_all.append(gather_chips(tie(g_low[m], normed_ffn)))
        state.append((kv, context, lse_rows, mixed, scale_two, normed_x2))
    w_both = order.did(reshard.result(*order.last))
    w_down_chip = order.did(rows_of([order.at(w_down), w_down_other]))

    hiddens, gate_grads, up_grads, normed_grads, out_terms = [], [], [], [], []

    def forward_back(m):
        hidden, gate_grad, up_grad = feed_forward(order.at(n2_alls[m]), g_all[m], w_both, w_down_chip)
        hiddens.append(hidden)
        gate_grads.append(gate_grad)
        up_grads.append(order.did(up_grad))

    def normed_part(m, *before):
        part = order.did(sum_nt([order.at(gate_grads[m], *before), up_grads[m]], w_both))
        normed_grads.append(scatter_chips(part))

    def out_part(m, *before):
        part = order.did(plain_nn(order.at(hiddens[m], *before), w_down_chip))
        out_terms.append(scatter_chips(part))

    slab = d_own // seq
    ff = parts * hidden_own
    forward_back(0)
    normed_part(0, g_all[-1])
    for m in range(1, micro):
        forward_back(m)
    wide_other = order.did(sum_tn(n2_alls, [[order.at(gate_grads[0])] + gate_grads[1:], up_grads], 1))
    wide_came = partner(wide_other)
    down_other = order.did(sum_tn([order.at(hiddens[0])] + hiddens[1:], [g_all], 1, weight=10))
    down_came = partner(down_other)
    wide_grad = order.did(sum_tn(n2_alls, [[order.at(gate_grads[0])] + gate_grads[1:], up_grads], 0, wide_came))
    wide_blocks = wide_grad.reshape(parts, seq, slab, hidden_chip)
    wide = Scatter(lambda j: lax.dynamic_index_in_dim(wide_blocks, j, 1, keepdims=False))
    hops = wide.hop()
    order.last = order.last + (normed_grads[0],)
    down_grad = order.did(sum_tn([order.at(hiddens[0])] + hiddens[1:], [g_all], 0, down_came))
    down = Scatter(chunk_of(down_grad.reshape(seq, hidden_own // seq, D)))
    normed_part(1)
    out_part(0)
    order.last = order.last + hops
    hops = wide.hop() + down.hop()
    for m in range(1, micro):
        out_part(m)
    normed_mine, normed_other = features(order.at(normed), core, d_own)
    normed_chip = rows_of([normed_mine, partner(normed_other)])
    context_mine, context_other = features(rows_of([state[m][1] for m in range(micro)]), core, d_own)
    context_chip = rows_of([context_mine, partner(context_other)])
    order.did(normed_mine)

    mixed_grads, attn_grads, query_grads, kv_sums = [], [], [], []
    gain_two_term = 0.0
    chip_rows = lambda pieces: rows_of(pieces + [partner(p) for p in pieces])
    for m in range(micro):
        kv, context, lse_rows, mixed, scale_two, normed_x2 = state[m]
        normed_grad = order.at(normed_grads[m]).astype(f32)
        gain_two_term = gain_two_term + jnp.sum(normed_grad * normed_x2, axis=0)
        mixed_grad = norm_back(normed_grad, gain_two, normed_x2, scale_two, g_low[m].astype(f32))
        attn_grad = mixed_grad.astype(bf16)
        attn_grads.append(attn_grad)
        mixed_grads.append(mixed_grad)
        context_grad = order.did(nt(attn_grad, w_out_full).astype(bf16))
        if m == micro - 1:
            out_half = order.did(tn(context_chip, chip_rows(attn_grads)).astype(bf16))
            out_shard = scatter_chips(out_half)
        if m == 1:
            order.last = order.last + hops
            pair = exchange(wide.result())
            order.last = order.last + (pair,)
            pieces = exchange_chips(pair)
            hops = down.hop()
        args = (context, lse_rows, kv, bias_t[m], tables, m)
        first = attend_back(qkv, order.at(context_grad), *args, 0)
        order.last = hops
        if m == 0:
            hops = wide.hop() + down.hop()
        elif m == 1:
            wide_part = exchanged([order.at(pieces[0], *pieces[1:])] + pieces[1:])
            wide_part = jnp.moveaxis(wide_part.reshape(parts, slab, 2, hidden_own), 0, 2).reshape(slab, 2 * ff)
            wide_gather, down_gather = Gather(wide_part), Gather(down.result())
            hops = wide_gather.hop()
            order.last = (wide_part,)
        second = attend_back(qkv, order.at(context_grad), *args, 1, first)
        query_grads.append(order.did(second[0]))
        kv_sums.append(KeySum(second[1:]))
        kv_sums[-1].hop()

    order.last = order.last + tuple(out_terms) + (out_shard,) + hops
    hops = wide_gather.hop() + down_gather.hop()
    query_half = order.did(tn(normed_chip, chip_rows(query_grads[:-1] + [order.at(query_grads[-1])])).astype(bf16))
    query_shard = scatter_chips(query_half)
    kv_hop = tuple(keys.hop() for keys in kv_sums)
    normed_grad = order.did(nt(order.at(rows_of(query_grads), *kv_hop), w_in[:, :D]))
    kv_grads = [keys.result() for keys in kv_sums]
    order.last = order.last + hops
    kv_grads = [order.did(finish_keys(own, order.at(came), tables, m)) for m, (own, came) in enumerate(kv_grads)]
    hops = wide_gather.hop() + down_gather.hop()
    kv_grad = rows_of(kv_grads)
    kv_half = order.did(tn(normed_chip, chip_rows(kv_grads)).astype(bf16))
    normed_grad = normed_grad + nt(kv_grad, w_in[:, D:D + 4 * KW])
    gain_one_term = jnp.sum(normed_grad * normed_x1, axis=0)
    input_grad = norm_back(normed_grad, gain_one, normed_x1, scale_one, rows_of(mixed_grads)).astype(bf16)

    gain_blocks = jnp.stack([gain_one_term, gain_two_term], axis=1).astype(bf16).reshape(chips, 2, d_own, 2)
    gain_lanes = jnp.concatenate(
        [lax.dynamic_index_in_dim(gain_blocks, c, 1, keepdims=False) for c in (core, 1 - core)], axis=2
    ).reshape(chips * d_own, 4)
    kv_shard = scatter_chips(tie(jnp.concatenate([kv_half, jnp.pad(gain_lanes, ((0, 0), (0, 124)))], axis=1), query_shard))
    out_total, query_total, kv_total = (
        x.astype(f32) for x in lax.psum((tie(out_shard, kv_shard), tie(query_shard, kv_shard), kv_shard), "sp")
    )
    kv_piece = lambda k: kv_total[:, k * KW:(k + 1) * KW]
    gain_lanes = kv_total[:, 4 * KW:4 * KW + 4]
    gain_total = gain_lanes[:, :2] + partner(gain_lanes)[:, 2:]
    order.last = order.last + hops
    down_slots = down_gather.result()
    wide_gather.hop()
    (down_total,) = assemble([(order.at(down_slots[0][0]), None)] + down_slots[1:], [[(0, D)]])
    gate_total, up_total = assemble(wide_gather.result(), [[(0, ff)], [(ff, ff)]])
    outputs = [(state[m][3] + order.at(out_terms[m]).astype(f32)).astype(bf16) for m in range(micro)]
    return (
        rows_of(outputs).reshape(tokens.shape),
        input_grad.reshape(tokens.shape),
        gain_total[:, 0],
        gain_total[:, 1],
        query_total,
        jnp.concatenate([kv_piece(0), kv_piece(2)], axis=1),
        jnp.concatenate([kv_piece(1), kv_piece(3)], axis=1),
        out_total,
        gate_total,
        up_total,
        down_total,
    )


def solution(mesh):
    split = P("fsdp", None)
    stream = P(None, "fsdp", "sp", None)
    return jax.shard_map(
        body,
        mesh=mesh,
        in_specs=(stream, P(None, "fsdp", None), stream, P("fsdp"), P("fsdp")) + (split,) * 7,
        out_specs=(stream, stream, P("fsdp"), P("fsdp")) + (split,) * 7,
        check_vma=False,
    )
```

```python
import functools, math
import jax, jax.numpy as jnp
from jax import lax
from jax.experimental import pallas as pl
from jax.experimental.pallas import tpu as pltpu
from jax.sharding import PartitionSpec as P

D = 2560
HEADS = 32
KV_HEADS = 8
HEAD_DIM = 80
GROUP = HEADS // KV_HEADS
HALVES = 2
SCALE = HEAD_DIM ** -0.5
LOG2E = 1.0 / math.log(2.0)
QW = D // HALVES
KW = KV_HEADS * HEAD_DIM // HALVES
CHUNK = 640
SPEED = 1 << 28


def work(micros):
    return pl.CostEstimate(flops=micros * SPEED, bytes_accessed=1 << 16, transcendentals=0)


def nt(left, right):
    return lax.dot_general(left, right, (((1,), (1,)), ((), ())), preferred_element_type=jnp.float32)


def tn(left, right):
    return lax.dot_general(left, right, (((0,), (0,)), ((), ())), preferred_element_type=jnp.float32)


def nn(left, right):
    return jnp.dot(left, right, preferred_element_type=jnp.float32)


def head(h):
    return slice(h * HEAD_DIM, (h + 1) * HEAD_DIM)


def spin(x, cosine, sine_up, sine_down):
    half = HEAD_DIM // 2
    width = x.shape[1]
    return x * cosine + pltpu.roll(x, width - half, 1) * sine_up + pltpu.roll(x, half, 1) * sine_down


def project_kernel(n_ref, w_ref, cos_ref, up_ref, down_ref, out_ref):
    j = pl.program_id(0)
    x = nn(n_ref[...], w_ref[...])
    turned = spin(x, cos_ref[...], up_ref[...], down_ref[...])
    lane = lax.broadcasted_iota(jnp.int32, x.shape, 1)
    keep = (j < D // CHUNK) | (lane < KW)
    out_ref[...] = jnp.where(keep, turned, x).astype(jnp.bfloat16)


def project(normed, weights, tables):
    rows = normed.shape[0]
    chunks = (D + 4 * KW) // CHUNK
    table = pl.BlockSpec((rows, CHUNK), lambda j: (0, 0))
    return pl.pallas_call(
        project_kernel,
        grid=(chunks,),
        in_specs=[pl.BlockSpec((rows, D), lambda j: (0, 0)), pl.BlockSpec((D, CHUNK), lambda j: (0, j)), table, table, table],
        out_specs=pl.BlockSpec((rows, CHUNK), lambda j: (0, j)),
        out_shape=jax.ShapeDtypeStruct((rows, chunks * CHUNK), jnp.bfloat16),
        compiler_params=pltpu.CompilerParams(vmem_limit_bytes=48 << 20),
        cost_estimate=work(19),
        name="project",
    )(normed, weights, *tables)


def forward_kernel(blocks, q_ref, *refs):
    kv_refs = refs[:blocks]
    bias_ref, ctx_ref, lse_ref = refs[blocks:]
    rows = q_ref.shape[0]
    bias = [bias_ref[s] for s in range(blocks)]
    lane = lax.broadcasted_iota(jnp.int32, (rows, 128), 1)
    lse_all = jnp.zeros((rows, 128), jnp.float32)
    for h in range(QW // HEAD_DIM):
        c = h // GROUP
        q = q_ref[:, head(h)]
        scores = [nt(q, kv_refs[s][:, head(c)]) * (SCALE * LOG2E) + bias_ref[s] for s in range(blocks)]
        top = functools.reduce(jnp.maximum, scores).max(axis=1, keepdims=True)
        probs = [jnp.exp2(x - top) for x in scores]
        total = functools.reduce(jnp.add, probs).sum(axis=1, keepdims=True)
        ctx = functools.reduce(jnp.add, [nn(p.astype(jnp.bfloat16), kv_refs[s][:, KW + c * HEAD_DIM:KW + (c + 1) * HEAD_DIM]) for s, p in enumerate(probs)])
        ctx_ref[:, head(h)] = (ctx / total).astype(jnp.bfloat16)
        lse_all = jnp.where(lane == h, top + jnp.log2(total), lse_all)
    lse_ref[...] = lse_all


def attend(qkv, kv_blocks, bias, at):
    rows = kv_blocks[0].shape[0]
    blocks = len(kv_blocks)
    kv_spec = pl.BlockSpec((rows, 2 * KW), lambda h: (0, h))
    return pl.pallas_call(
        functools.partial(forward_kernel, blocks),
        grid=(HALVES,),
        in_specs=[pl.BlockSpec((rows, QW), lambda h: (at, h))] + [kv_spec] * blocks + [pl.BlockSpec((blocks, rows, rows), lambda h: (0, 0, 0))],
        out_specs=[pl.BlockSpec((rows, QW), lambda h: (0, h)), pl.BlockSpec((rows, 128), lambda h: (0, h))],
        out_shape=[jax.ShapeDtypeStruct((rows, D), jnp.bfloat16), jax.ShapeDtypeStruct((rows, HALVES * 128), jnp.float32)],
        compiler_params=pltpu.CompilerParams(vmem_limit_bytes=48 << 20),
        cost_estimate=work(23),
        name="attend",
    )(qkv, *kv_blocks, bias)


def backward_kernel(blocks, skipped, q_ref, dctx_ref, ctx_ref, lse_ref, *refs):
    kv_refs = refs[:blocks]
    bias_ref, cos_ref, up_ref, down_ref = refs[blocks:blocks + 4]
    dq_ref = refs[blocks + 4 + skipped]
    dkv_refs = refs[blocks + 5 + skipped:2 * blocks + 5 + skipped]
    dq_acc = refs[-1]
    rows = q_ref.shape[0]
    count = QW // HEAD_DIM
    owner = lax.broadcasted_iota(jnp.int32, (count, QW), 0)
    lane = lax.broadcasted_iota(jnp.int32, (count, QW), 1)
    pick = ((lane >= owner * HEAD_DIM) & (lane < owner * HEAD_DIM + HEAD_DIM)).astype(jnp.float32)
    product = dctx_ref[...].astype(jnp.float32) * ctx_ref[...].astype(jnp.float32)
    delta = lax.dot_general(pick, product, (((1,), (1,)), ((), ())), precision=lax.Precision.HIGHEST, preferred_element_type=jnp.float32)
    for c in range(KV_HEADS // HALVES):
        heads = range(c * GROUP, (c + 1) * GROUP)
        qs = [q_ref[:, head(h)] for h in heads]
        ds = [dctx_ref[:, head(h)] for h in heads]
        q_stack = jnp.concatenate(qs, axis=0)
        d_stack = jnp.concatenate(ds, axis=0)
        dq = [None] * GROUP
        for s in range(blocks):
            k = kv_refs[s][:, head(c)]
            v = kv_refs[s][:, KW + c * HEAD_DIM:KW + (c + 1) * HEAD_DIM]
            ps, dss = [], []
            for g, h in enumerate(heads):
                score = nt(k, qs[g]) * (SCALE * LOG2E) + bias_ref[s]
                p = jnp.exp2(score - lse_ref[h:h + 1, :])
                dp = nt(v, ds[g])
                d = (p * (dp - delta[h:h + 1, :])).astype(jnp.bfloat16)
                ps.append(p.astype(jnp.bfloat16))
                dss.append(d)
                term = tn(d, k)
                dq[g] = term if dq[g] is None else dq[g] + term
            dkv_refs[s][:, head(c)] = (nn(jnp.concatenate(dss, axis=1), q_stack) * SCALE).astype(jnp.bfloat16)
            dkv_refs[s][:, KW + c * HEAD_DIM:KW + (c + 1) * HEAD_DIM] = nn(jnp.concatenate(ps, axis=1), d_stack).astype(jnp.bfloat16)
        for g, h in enumerate(heads):
            dq_acc[:, head(h)] = dq[g] * SCALE
    for j in range(QW // CHUNK):
        part = slice(j * CHUNK, (j + 1) * CHUNK)
        dq_ref[:, part] = spin(dq_acc[:, part], cos_ref[...], -up_ref[...], -down_ref[...]).astype(jnp.bfloat16)


def attend_back(qkv, dctx, ctx, lse_rows, kv_blocks, bias_t, tables, at, half, before=None):
    rows = kv_blocks[0].shape[0]
    blocks = len(kv_blocks)
    count = QW // HEAD_DIM
    lanes = pl.BlockSpec((rows, QW), lambda h: (0, half))
    kv_spec = pl.BlockSpec((rows, 2 * KW), lambda h: (0, half))
    table = pl.BlockSpec((rows, CHUNK), lambda h: (at, 0))
    before = [] if before is None else list(before)
    inputs = 4 + blocks + 4
    outs = pl.pallas_call(
        functools.partial(backward_kernel, blocks, len(before)),
        grid=(1,),
        in_specs=[pl.BlockSpec((rows, QW), lambda h: (at, half)), lanes, lanes, pl.BlockSpec((count, rows), lambda h: (half, 0))]
        + [kv_spec] * blocks + [pl.BlockSpec((blocks, rows, rows), lambda h: (0, 0, 0)), table, table, table]
        + [pl.BlockSpec(memory_space=pl.ANY)] * len(before),
        out_specs=[lanes] + [kv_spec] * blocks,
        out_shape=[jax.ShapeDtypeStruct((rows, D), jnp.bfloat16)] + [jax.ShapeDtypeStruct((rows, 4 * KW), jnp.bfloat16)] * blocks,
        scratch_shapes=[pltpu.VMEM((rows, QW), jnp.float32)],
        input_output_aliases={inputs + k: k for k in range(len(before))},
        compiler_params=pltpu.CompilerParams(vmem_limit_bytes=48 << 20),
        cost_estimate=work(100),
        name="attend_back",
    )(qkv, dctx, ctx, lse_rows, *kv_blocks, bias_t, *tables, *before)
    return outs


RMS_EPS = 1e-05
ROPE_BASE = 1000000.0


def finish_kernel(own_ref, other_ref, cos_ref, up_ref, down_ref, out_ref):
    x = own_ref[...].astype(jnp.float32) + other_ref[...].astype(jnp.float32)
    turned = spin(x, cos_ref[...], -up_ref[...], -down_ref[...])
    lane = lax.broadcasted_iota(jnp.int32, x.shape, 1)
    out_ref[...] = jnp.where(lane < KW, turned, x).astype(jnp.bfloat16)


def finish_keys(own, other, tables, at):
    rows = own.shape[0]
    half = pl.BlockSpec((rows, 2 * KW), lambda h: (0, h))
    table = pl.BlockSpec((rows, CHUNK), lambda h: (at, 0))
    return pl.pallas_call(
        finish_kernel,
        grid=(HALVES,),
        in_specs=[half, half, table, table, table],
        out_specs=half,
        out_shape=jax.ShapeDtypeStruct(own.shape, jnp.bfloat16),
        cost_estimate=work(2),
        name="finish_keys",
    )(own, other, *tables)


def rms_scale(values):
    return lax.rsqrt(jnp.mean(values * values, axis=-1, keepdims=True) + RMS_EPS)


def norm_back(grad_normed, gain, normed_x, scale_row, grad_rest):
    scaled = grad_normed * gain
    inner = jnp.mean(scaled * normed_x, axis=-1, keepdims=True)
    return grad_rest + scale_row * (scaled - normed_x * inner)


def rope_lanes(position):
    lane = jnp.arange(CHUNK, dtype=jnp.int32) % HEAD_DIM
    half = HEAD_DIM // 2
    index = (lane % half).astype(jnp.float32)
    inverse = jnp.exp(index * (-2.0 * math.log(ROPE_BASE) / HEAD_DIM))
    angles = position.astype(jnp.float32)[:, None] * inverse[None, :]
    sine = jnp.sin(angles)
    first = (lane < half)[None, :]
    return jnp.cos(angles), jnp.where(first, -sine, 0.0), jnp.where(first, 0.0, sine)


def stream_layout(starts, places):
    begun = starts[:, None, :] <= places[None, :, None]
    doc_ids = jnp.sum(begun.astype(jnp.int32), axis=-1) - 1
    first_token = jnp.max(jnp.where(begun, starts[:, None, :], 0), axis=-1)
    return doc_ids, places[None, :] - first_token


def right_pairs(count, lowest=0):
    return [(k, k + 1) for k in range(lowest, count - 1)]


def left_pairs(count):
    return [(k + 1, k) for k in range(count - 1)]


def tie(x, *before):
    return lax.optimization_barrier((x,) + before)[0]


class Order:
    def __init__(self):
        self.last = ()

    def at(self, x, *more):
        return tie(x, *self.last, *more)

    def did(self, y):
        self.last = (y,)
        return y


def partner(x):
    return lax.ppermute(x, "fsdp", [(j, j ^ 1) for j in range(lax.axis_size("fsdp"))])


def same_core():
    parts = lax.axis_size("fsdp")
    return [list(range(c, parts, 2)) for c in range(2)]


def gather_chips(x):
    return lax.all_gather(x, "fsdp", axis=0, tiled=True, axis_index_groups=same_core())


def scatter_chips(x, *before):
    parts = lax.axis_size("fsdp")
    chips, chip = parts // 2, lax.axis_index("fsdp") // 2
    blocks = x.reshape((chips, x.shape[0] // chips) + x.shape[1:])
    take = lambda q: lax.dynamic_index_in_dim(blocks, q, 0, keepdims=False)
    came = [lax.ppermute(take(chip ^ d), "fsdp", [(j, j ^ (2 * d)) for j in range(parts)]) for d in range(1, chips)]
    return take(chip), came


def added(pieces):
    own, came = pieces
    return sum((c.astype(jnp.float32) for c in came), own.astype(jnp.float32))


def exchange(blocks):
    parts = lax.axis_size("fsdp")
    me = lax.axis_index("fsdp")
    chips, core = parts // 2, me % 2
    shape = blocks.shape[1:]
    blocks = blocks.reshape((chips, 2) + shape)
    mine = lax.dynamic_index_in_dim(blocks, core, 1, keepdims=False)
    came = partner(lax.dynamic_index_in_dim(blocks, 1 - core, 1, keepdims=False))
    return jnp.where(core == 0, jnp.stack([mine, came], axis=1), jnp.stack([came, mine], axis=1))


def exchange_chips(pair):
    parts = lax.axis_size("fsdp")
    chips, chip = parts // 2, lax.axis_index("fsdp") // 2
    own = lax.dynamic_index_in_dim(pair, chip, 0, keepdims=True)
    pieces = [own]
    for d in range(1, chips):
        block = lax.dynamic_index_in_dim(pair, chip ^ d, 0, keepdims=True)
        pieces.append(lax.ppermute(block, "fsdp", [(j, j ^ (2 * d)) for j in range(parts)]))
    return pieces


def exchanged(pieces):
    parts = lax.axis_size("fsdp")
    chip = lax.axis_index("fsdp") // 2
    out = jnp.zeros((parts // 2,) + pieces[0].shape[1:], pieces[0].dtype)
    for d, piece in enumerate(pieces):
        out = lax.dynamic_update_slice_in_dim(out, piece, chip ^ d, 0)
    return out


def columns_kernel(blocks, place_ref, gate_ref, up_ref, out_ref):
    j = pl.program_id(0)

    @pl.when(place_ref[blocks + j] == 0)
    def _():
        out_ref[...] = gate_ref[...]

    @pl.when(place_ref[blocks + j] == 1)
    def _():
        out_ref[...] = up_ref[...]


def columns_for(w_gate, w_up, picks, width):
    rows = w_gate.shape[0]
    blocks = len(picks)
    if width % 128:
        both = jnp.stack([w_gate.reshape(rows, -1, width), w_up.reshape(rows, -1, width)])
        return jnp.concatenate([both[which, :, at] for at, which in picks], axis=1)
    place = jnp.stack([jnp.asarray(x, jnp.int32) for x in [p[0] for p in picks] + [p[1] for p in picks]])
    source = lambda own: pl.BlockSpec(
        (rows, width), lambda j, place: (0, jnp.where(place[blocks + j] == own, place[j], place[0]))
    )
    return pl.pallas_call(
        functools.partial(columns_kernel, blocks),
        grid_spec=pltpu.PrefetchScalarGridSpec(
            num_scalar_prefetch=1,
            grid=(blocks,),
            in_specs=[source(0), source(1)],
            out_specs=pl.BlockSpec((rows, width), lambda j, place: (0, j)),
        ),
        out_shape=jax.ShapeDtypeStruct((rows, blocks * width), w_gate.dtype),
        cost_estimate=work(blocks),
        name="columns_for",
    )(place, w_gate, w_up)


def weave_kernel(count, chips, width, place_ref, *refs):
    out_ref = refs[-1]
    j = pl.program_id(0)
    half = 2 * width
    for d in range(chips):
        for c in range(2):
            mine, other = refs[2 * (c * chips + d):2 * (c * chips + d) + 2]
            for odd in range(2):
                @pl.when((j == 2 * d + c) & (place_ref[count] == odd))
                def _(mine=mine, other=other, c=c, odd=odd):
                    for which, ref in ((odd, mine), (1 - odd, other)):
                        for k in range(2):
                            at = which * half + k * width
                            from_lane = (k ^ c) * width
                            out_ref[:, at:at + width] = ref[:, from_lane:from_lane + width]


def weave(mine, other, places, odd, width):
    rows = mine[0].shape[0]
    count = len(mine)
    chips = count // 2
    tile = next(t for t in (160, 64, 32, 16) if rows % t == 0)
    tiles = rows // tile
    specs, arrays = [], []
    for c in range(2):
        for d in range(chips):
            index = lambda j, t, place, k=2 * d + c: (jnp.where(j == k, t, 0), 0)
            specs += [pl.BlockSpec((tile, 2 * width), index)] * 2
            arrays += [mine[c * chips + d], other[c * chips + d]]
    return pl.pallas_call(
        functools.partial(weave_kernel, count, chips, width),
        grid_spec=pltpu.PrefetchScalarGridSpec(
            num_scalar_prefetch=1,
            grid=(count, tiles),
            in_specs=specs,
            out_specs=pl.BlockSpec((tile, 4 * width), lambda j, t, place: (place[j] * tiles + t, 0)),
        ),
        out_shape=jax.ShapeDtypeStruct((count * rows, 4 * width), mine[0].dtype),
        compiler_params=pltpu.CompilerParams(vmem_limit_bytes=56 << 20),
        cost_estimate=work(21),
        name="weave",
    )(jnp.stack([jnp.asarray(x, jnp.int32) for x in places + [odd]]), *arrays)


class Reshard:
    def __init__(self, w_gate, w_up):
        parts = lax.axis_size("fsdp")
        me = lax.axis_index("fsdp")
        self.chips = parts // 2
        self.chip, self.core = me // 2, me % 2
        self.odd = lax.axis_index("sp") % 2
        self.width = w_gate.shape[1] // parts
        pair = lambda d, which: [(2 * (self.chip ^ d) + c, which) for c in (self.core, 1 - self.core)]
        self.local = columns_for(w_gate, w_up, pair(0, self.odd) + pair(0, 1 - self.odd), self.width)
        self.sent = [columns_for(w_gate, w_up, pair(d, self.odd), self.width) for d in range(1, self.chips)]

    def fetch(self):
        parts = 2 * self.chips
        half = 2 * self.width
        self.mine = [self.local[:, :half]] + [
            lax.ppermute(x, "fsdp", [(j, j ^ (2 * d)) for j in range(parts)]) for d, x in enumerate(self.sent, 1)
        ]
        pairs = [(k, k ^ 1) for k in range(lax.axis_size("sp"))]
        self.other = [self.local[:, half:]] + [lax.ppermute(x, "sp", pairs) for x in self.mine[1:]]
        return self.other[1:]

    def result(self, *before):
        mine = self.mine + [partner(x) for x in self.mine]
        other = self.other + [partner(x) for x in self.other]
        places = []
        for d in range(self.chips):
            places += [2 * (self.chip ^ d) + self.core, 2 * (self.chip ^ d) + 1 - self.core]
        return weave([tie(mine[0], *before)] + mine[1:], other, places, self.odd, self.width)


def features_kernel(count, width, core_ref, x_ref, mine_ref, other_ref):
    for c in range(2):
        @pl.when(core_ref[0] == c)
        def _(c=c):
            for q in range(count):
                at = slice(q * width, (q + 1) * width)
                mine_ref[:, at] = x_ref[:, (2 * q + c) * width:(2 * q + c + 1) * width]
                other_ref[:, at] = x_ref[:, (2 * q + 1 - c) * width:(2 * q + 2 - c) * width]


def features(x, core, width):
    rows = x.shape[0]
    count = x.shape[1] // (2 * width)
    tile = min(rows, 256)
    out = pl.BlockSpec((tile, count * width), lambda t, core: (t, 0))
    return pl.pallas_call(
        functools.partial(features_kernel, count, width),
        grid_spec=pltpu.PrefetchScalarGridSpec(
            num_scalar_prefetch=1,
            grid=(rows // tile,),
            in_specs=[pl.BlockSpec((tile, x.shape[1]), lambda t, core: (t, 0))],
            out_specs=[out, out],
        ),
        out_shape=[jax.ShapeDtypeStruct((rows, count * width), x.dtype)] * 2,
        cost_estimate=work(3),
        name="features",
    )(core.reshape(1).astype(jnp.int32), x)


def sum_tn_kernel(segments, pairs, *refs):
    lefts = [ref[...] for ref in refs[:pairs]]
    extra = refs[pairs + segments * pairs:-1]
    out_ref = refs[-1]
    width = out_ref.shape[-1] // segments
    for j in range(segments):
        rights = refs[pairs + j * pairs:pairs + (j + 1) * pairs]
        part = slice(j * width, (j + 1) * width)
        total = sum(tn(a, b[...]) for a, b in zip(lefts, rights))
        if len(out_ref.shape) == 2:
            for more in extra:
                total = total + more[:, part].astype(jnp.float32)
            out_ref[:, part] = total.astype(out_ref.dtype)
        else:
            slabs, blocks, rows, _ = out_ref.shape
            for s in range(slabs):
                for k in range(blocks):
                    at = (k * slabs + s) * rows
                    piece = total[at:at + rows]
                    for more in extra:
                        piece = piece + more[s, k, :, part].astype(jnp.float32)
                    out_ref[s, k, :, part] = piece.astype(out_ref.dtype)


def sum_tn(lefts, rights, half, *extra, weight=1, slabs=1, rows=1):
    segments, pairs = len(rights), len(lefts)
    tokens = lefts[0].shape[0]
    if segments == 1:
        width = lefts[0].shape[1] // 2
        if width % 128:
            total = sum(tn(a[:, half * width:(half + 1) * width], b) for a, b in zip(lefts, rights[0]))
            return sum((e.astype(jnp.float32) for e in extra), total).astype(jnp.bfloat16)
        shape = (width, D)
        block = (width, CHUNK)
        left = pl.BlockSpec((tokens, width), lambda i: (0, half))
        right = pl.BlockSpec((tokens, CHUNK), lambda i: (0, i))
        out = pl.BlockSpec(block, lambda i: (0, i))
    else:
        width = rights[0][0].shape[1] // 2
        if width % 128:
            cut = slice(half * width, (half + 1) * width)
            total = jnp.concatenate([sum(tn(a, b[:, cut]) for a, b in zip(lefts, r)) for r in rights], axis=1)
            total = jnp.moveaxis(total.reshape(-1, slabs, rows, segments * width), 1, 0)
            return sum((e.astype(jnp.float32) for e in extra), total).astype(jnp.bfloat16)
        blocks = CHUNK // (slabs * rows)
        shape = (slabs, D // (slabs * rows), rows, segments * width)
        left = pl.BlockSpec((tokens, CHUNK), lambda i: (0, i))
        right = pl.BlockSpec((tokens, width), lambda i: (0, half))
        out = pl.BlockSpec((slabs, blocks, rows, segments * width), lambda i: (0, i, 0, 0))
    return pl.pallas_call(
        functools.partial(sum_tn_kernel, segments, pairs),
        grid=(D // CHUNK,),
        in_specs=[left] * pairs + [right] * (segments * pairs) + [out] * len(extra),
        out_specs=out,
        out_shape=jax.ShapeDtypeStruct(shape, jnp.bfloat16),
        compiler_params=pltpu.CompilerParams(vmem_limit_bytes=56 << 20),
        cost_estimate=work((26 if segments == 2 else 16) * weight),
        name="sum_tn",
    )(*lefts, *[b for r in rights for b in r], *extra)


def ffn_kernel(n_ref, g_ref, wg_ref, wu_ref, wd_ref, hidden_ref, gate_grad_ref, up_grad_ref):
    gate = nn(n_ref[...], wg_ref[...])
    up = nn(n_ref[...], wu_ref[...])
    hidden_grad = nt(g_ref[...], wd_ref[...])
    sigm = 1.0 / (1.0 + jnp.exp(-gate))
    act = gate * sigm
    hidden_ref[...] = (act * up).astype(jnp.bfloat16)
    up_grad_ref[...] = (hidden_grad * act).astype(jnp.bfloat16)
    gate_grad_ref[...] = (hidden_grad * up * (sigm + act * (1.0 - sigm))).astype(jnp.bfloat16)


def feed_forward(n2, g, w_both, w_down):
    tokens, hidden = n2.shape[0], w_down.shape[0]
    tile = 256 if hidden % 256 == 0 else 128
    tiles = hidden // tile
    full = pl.BlockSpec((tokens, D), lambda j: (0, 0))
    out = pl.BlockSpec((tokens, tile), lambda j: (0, j))
    return pl.pallas_call(
        ffn_kernel,
        grid=(tiles,),
        in_specs=[full, full, pl.BlockSpec((D, tile), lambda j: (0, j)), pl.BlockSpec((D, tile), lambda j: (0, tiles + j)),
                  pl.BlockSpec((tile, D), lambda j: (j, 0))],
        out_specs=[out] * 3,
        out_shape=[jax.ShapeDtypeStruct((tokens, hidden), jnp.bfloat16)] * 3,
        compiler_params=pltpu.CompilerParams(vmem_limit_bytes=56 << 20),
        cost_estimate=work(36),
        name="feed_forward",
    )(n2, g, w_both, w_both, w_down)


def sum_nt_kernel(*refs):
    pairs = len(refs) // 2
    refs[-1][...] = sum(nt(refs[k][...], refs[pairs + k][...]) for k in range(pairs)).astype(jnp.bfloat16)


def sum_nt(lefts, right, weight=1):
    (tokens, depth), columns = lefts[0].shape, right.shape[0]
    tile, block = tokens // 2, columns // 2
    return pl.pallas_call(
        sum_nt_kernel,
        grid=(columns // block, tokens // tile),
        in_specs=[pl.BlockSpec((tile, depth), lambda j, i: (i, 0))] * len(lefts)
        + [pl.BlockSpec((block, depth), lambda j, i, k=k: (j, k)) for k in range(len(lefts))],
        out_specs=pl.BlockSpec((tile, block), lambda j, i: (i, j)),
        out_shape=jax.ShapeDtypeStruct((tokens, columns), jnp.bfloat16),
        compiler_params=pltpu.CompilerParams(vmem_limit_bytes=56 << 20),
        cost_estimate=work(26 * weight),
        name="sum_nt",
    )(*lefts, *([right] * len(lefts)))


def plain_nn_kernel(a_ref, b_ref, out_ref):
    out_ref[...] = nn(a_ref[...], b_ref[...]).astype(jnp.bfloat16)


def plain_nn(a, b, weight=1):
    (tokens, depth), columns = a.shape, b.shape[1]
    return pl.pallas_call(
        plain_nn_kernel,
        grid=(columns // CHUNK,),
        in_specs=[pl.BlockSpec((tokens, depth), lambda j: (0, 0)), pl.BlockSpec((depth, CHUNK), lambda j: (0, j))],
        out_specs=pl.BlockSpec((tokens, CHUNK), lambda j: (0, j)),
        out_shape=jax.ShapeDtypeStruct((tokens, columns), jnp.bfloat16),
        compiler_params=pltpu.CompilerParams(vmem_limit_bytes=56 << 20),
        cost_estimate=work(16 * weight),
        name="plain_nn",
    )(a, b)


class KeySum:
    def __init__(self, parts):
        self.parts = parts
        self.running = parts[-1]
        self.hops = 0

    def hop(self, *before):
        n = lax.axis_size("sp")
        s = self.hops
        if s:
            self.running = (self.parts[n - 1 - s].astype(jnp.float32) + self.running.astype(jnp.float32)).astype(jnp.bfloat16)
        pairs = [(n - 1 - k, n - 2 - k) for k in range(s + 1)]
        self.running = lax.ppermute(tie(self.running, *before), "sp", pairs)
        self.hops += 1
        return self.running

    def result(self):
        while self.hops < lax.axis_size("sp") - 1:
            self.hop()
        return self.parts[0], self.running


def rows_of(pieces):
    return jnp.concatenate(pieces, axis=0)


def body(tokens, doc_starts, cotangent, gain_attn, gain_ffn, w_query, w_key, w_value, w_out, w_gate, w_up, w_down):
    micro, _, rows, _ = tokens.shape
    parts = lax.axis_size("fsdp")
    chips = parts // 2
    core = lax.axis_index("fsdp") % 2
    seq = lax.axis_size("sp")
    place = lax.axis_index("sp")
    count = micro * rows
    d_own = w_query.shape[0]
    hidden_own = w_down.shape[0]
    hidden_chip = 2 * hidden_own
    bf16 = jnp.bfloat16
    f32 = jnp.float32

    gains = jnp.pad(jnp.stack([gain_attn, gain_ffn], axis=1), ((0, 0), (0, 126)))
    w_in = jnp.concatenate(
        [w_query, w_key[:, :KW], w_value[:, :KW], w_key[:, KW:], w_value[:, KW:], gains], axis=1
    )
    w_in = lax.all_gather(w_in, "fsdp", axis=0, tiled=True)
    w_out_full = lax.all_gather(w_out, "fsdp", axis=0, tiled=True)
    gain_one = w_in[:, D + 4 * KW].astype(f32)
    gain_two = w_in[:, D + 4 * KW + 1].astype(f32)
    reshard = Reshard(w_gate, w_up)
    came_columns = reshard.fetch()

    starts = doc_starts.reshape(micro, -1)
    offsets = (place - jnp.arange(seq, dtype=jnp.int32)) * rows
    key_places = (offsets[:, None] + jnp.arange(rows, dtype=jnp.int32)[None, :]).reshape(-1)
    docs, positions = stream_layout(starts, key_places)
    docs = docs.reshape(micro, seq, rows)
    key_places = key_places.reshape(seq, rows)
    tables = rope_lanes(positions.reshape(micro, seq, rows)[:, 0].reshape(count))
    allowed = (docs[:, :1, :, None] == docs[:, :, None, :]) & (
        key_places[None, :, None, :] <= key_places[None, :1, :, None]
    )
    bias = jnp.where(allowed, 0.0, -1e30).astype(f32)
    bias_t = jnp.where(jnp.swapaxes(allowed, 2, 3), 0.0, -1e30).astype(f32)

    inputs = tokens.reshape(count, D).astype(f32)
    scale_one = rms_scale(inputs)
    normed_x1 = inputs * scale_one
    normed = tie((normed_x1 * gain_one).astype(bf16), *tables, bias, bias_t)
    normed = tie(normed, *came_columns)
    w_down_other = partner(w_down)
    order = Order()
    qkv = order.did(project(normed, w_in, tables))

    g_low = cotangent.reshape(micro, rows, D)
    g_all = [gather_chips(tie(g_low[0], qkv))]
    state, n2_alls = [], []
    for m in range(micro):
        kv = [qkv[m * rows:(m + 1) * rows, D:]]
        for s in range(seq - 1):
            kv.append(lax.ppermute(kv[-1], "sp", right_pairs(seq, s)))
        context, lse = attend(order.at(qkv), kv, bias[m], m)
        lse_rows = jnp.swapaxes(lse.reshape(rows, HALVES, 128)[:, :, :QW // HEAD_DIM].reshape(rows, HEADS), 0, 1)
        mixed = inputs[m * rows:(m + 1) * rows] + nn(context, w_out_full)
        scale_two = rms_scale(mixed)
        normed_x2 = mixed * scale_two
        normed_ffn = order.did((normed_x2 * gain_two).astype(bf16))
        if m == 0:
            normed_ffn = tie(normed_ffn, g_all[0])
        n2_alls.append(gather_chips(normed_ffn))
        if m:
            g_all.append(gather_chips(tie(g_low[m], normed_ffn)))
        state.append((kv, context, lse_rows, mixed, scale_two, normed_x2))
    w_both = order.did(reshard.result(*order.last))
    w_down_chip = order.did(rows_of([order.at(w_down), w_down_other]))

    hiddens, gate_grads, up_grads, normed_grads, out_terms = [], [], [], [], []

    def forward_back(m):
        hidden, gate_grad, up_grad = feed_forward(order.at(n2_alls[m]), g_all[m], w_both, w_down_chip)
        hiddens.append(hidden)
        gate_grads.append(gate_grad)
        up_grads.append(order.did(up_grad))

    def normed_part(m, *before):
        part = order.did(sum_nt([order.at(gate_grads[m], *before), up_grads[m]], w_both))
        normed_grads.append(scatter_chips(part))

    def out_part(m, *before):
        part = order.did(plain_nn(order.at(hiddens[m], *before), w_down_chip))
        out_terms.append(scatter_chips(part))

    slab = d_own // seq
    ff = parts * hidden_own
    forward_back(0)
    normed_part(0, g_all[-1])
    for m in range(1, micro):
        forward_back(m)
    wide = dict(slabs=seq, rows=slab)
    wide_other = order.did(sum_tn(n2_alls, [[order.at(gate_grads[0])] + gate_grads[1:], up_grads], 1, **wide))
    wide_came = partner(wide_other)
    down_other = order.did(sum_tn([order.at(hiddens[0])] + hiddens[1:], [g_all], 1))
    down_came = partner(down_other)
    wide_grad = order.did(sum_tn(n2_alls, [[order.at(gate_grads[0])] + gate_grads[1:], up_grads], 0, wide_came, **wide))
    wide_mine = lax.psum_scatter(wide_grad, "sp", scatter_dimension=0, tiled=False)
    down_grad = order.did(sum_tn([order.at(hiddens[0])] + hiddens[1:], [g_all], 0, down_came))
    down_total = lax.psum(down_grad, "sp")
    normed_part(1)
    for m in range(micro):
        out_part(m)
    normed_mine, normed_other = features(order.at(normed), core, d_own)
    normed_chip = rows_of([normed_mine, partner(normed_other)])
    context_mine, context_other = features(rows_of([state[m][1] for m in range(micro)]), core, d_own)
    context_chip = rows_of([context_mine, partner(context_other)])
    order.did(normed_mine)

    mixed_grads, attn_grads, query_grads, kv_sums = [], [], [], []
    gain_two_term = 0.0
    chip_rows = lambda pieces: rows_of(pieces + [partner(p) for p in pieces])
    for m in range(micro):
        kv, context, lse_rows, mixed, scale_two, normed_x2 = state[m]
        if m == micro - 1:
            order.last = order.last + (wide_mine,)
            pieces = exchange_chips(exchange(wide_mine))
        normed_grad = added((order.at(normed_grads[m][0]), normed_grads[m][1]))
        gain_two_term = gain_two_term + jnp.sum(normed_grad * normed_x2, axis=0)
        mixed_grad = norm_back(normed_grad, gain_two, normed_x2, scale_two, g_low[m].astype(f32))
        attn_grad = mixed_grad.astype(bf16)
        attn_grads.append(attn_grad)
        mixed_grads.append(mixed_grad)
        context_grad = order.did(nt(attn_grad, w_out_full).astype(bf16))
        if m == micro - 1:
            out_half = order.did(tn(context_chip, chip_rows(attn_grads)).astype(bf16))
            out_shard = added(scatter_chips(out_half)).astype(bf16)
        args = (context, lse_rows, kv, bias_t[m], tables, m)
        first = attend_back(qkv, order.at(context_grad), *args, 0)
        order.last = ()
        if m == micro - 1:
            order.last = tuple(pieces)
        second = attend_back(qkv, order.at(context_grad), *args, 1, first)
        query_grads.append(order.did(second[0]))
        kv_sums.append(KeySum(second[1:]))
        kv_sums[-1].hop()

    order.last = order.last + (out_shard, down_total)
    wide_part = exchanged([order.at(pieces[0], *pieces[1:])] + pieces[1:])
    wide_part = order.did(jnp.moveaxis(wide_part.reshape(parts, slab, 2, hidden_own), 0, 2).reshape(slab, 2 * ff))
    wide_total = lax.all_gather(wide_part, "sp", axis=0, tiled=True)
    query_half = order.did(tn(normed_chip, chip_rows(query_grads[:-1] + [order.at(query_grads[-1])])).astype(bf16))
    query_shard = added(scatter_chips(query_half)).astype(bf16)
    kv_hop = tuple(keys.hop() for keys in kv_sums)
    normed_grad = order.did(nt(order.at(rows_of(query_grads), *kv_hop), w_in[:, :D]))
    kv_grads = [keys.result() for keys in kv_sums]
    kv_grads = [order.did(finish_keys(own, order.at(came), tables, m)) for m, (own, came) in enumerate(kv_grads)]
    kv_grad = rows_of(kv_grads)
    kv_half = order.did(tn(normed_chip, chip_rows(kv_grads)).astype(bf16))
    normed_grad = normed_grad + nt(kv_grad, w_in[:, D:D + 4 * KW])
    gain_one_term = jnp.sum(normed_grad * normed_x1, axis=0)
    input_grad = norm_back(normed_grad, gain_one, normed_x1, scale_one, rows_of(mixed_grads)).astype(bf16)

    gain_blocks = jnp.stack([gain_one_term, gain_two_term], axis=1).astype(bf16).reshape(chips, 2, d_own, 2)
    gain_lanes = jnp.concatenate(
        [lax.dynamic_index_in_dim(gain_blocks, c, 1, keepdims=False) for c in (core, 1 - core)], axis=2
    ).reshape(chips * d_own, 4)
    kv_shard = added(scatter_chips(jnp.concatenate([kv_half, jnp.pad(gain_lanes, ((0, 0), (0, 124)))], axis=1))).astype(bf16)
    out_total, query_total, kv_total = lax.psum((tie(out_shard, down_total), query_shard, kv_shard), "sp")
    query_total, kv_total = query_total.astype(f32), kv_total.astype(f32)
    kv_piece = lambda k: kv_total[:, k * KW:(k + 1) * KW]
    gain_lanes = kv_total[:, 4 * KW:4 * KW + 4]
    gain_total = gain_lanes[:, :2] + partner(gain_lanes)[:, 2:]
    outputs = [(state[m][3] + added((order.at(out_terms[m][0]), out_terms[m][1]))).astype(bf16) for m in range(micro)]
    return (
        rows_of(outputs).reshape(tokens.shape),
        input_grad.reshape(tokens.shape),
        gain_total[:, 0],
        gain_total[:, 1],
        query_total,
        jnp.concatenate([kv_piece(0), kv_piece(2)], axis=1),
        jnp.concatenate([kv_piece(1), kv_piece(3)], axis=1),
        out_total.astype(f32),
        wide_total[:, :ff].astype(f32),
        wide_total[:, ff:].astype(f32),
        down_total.astype(f32),
    )


def solution(mesh):
    split = P("fsdp", None)
    stream = P(None, "fsdp", "sp", None)
    return jax.shard_map(
        body,
        mesh=mesh,
        in_specs=(stream, P(None, "fsdp", None), stream, P("fsdp"), P("fsdp")) + (split,) * 7,
        out_specs=(stream, stream, P("fsdp"), P("fsdp")) + (split,) * 7,
        check_vma=False,
    )
```

```python
import functools, math
import jax, jax.numpy as jnp
from jax import lax
from jax.experimental import pallas as pl
from jax.experimental.pallas import tpu as pltpu
from jax.sharding import PartitionSpec as P

D = 2560
HEADS = 32
KV_HEADS = 8
HEAD_DIM = 80
GROUP = HEADS // KV_HEADS
HALVES = 2
SCALE = HEAD_DIM ** -0.5
LOG2E = 1.0 / math.log(2.0)
QW = D // HALVES
KW = KV_HEADS * HEAD_DIM // HALVES
CHUNK = 640
SPEED = 1 << 28


def work(micros):
    return pl.CostEstimate(flops=micros * SPEED, bytes_accessed=1 << 16, transcendentals=0)


def nt(left, right):
    return lax.dot_general(left, right, (((1,), (1,)), ((), ())), preferred_element_type=jnp.float32)


def tn(left, right):
    return lax.dot_general(left, right, (((0,), (0,)), ((), ())), preferred_element_type=jnp.float32)


def nn(left, right):
    return jnp.dot(left, right, preferred_element_type=jnp.float32)


def head(h):
    return slice(h * HEAD_DIM, (h + 1) * HEAD_DIM)


def spin(x, cosine, sine_up, sine_down):
    half = HEAD_DIM // 2
    width = x.shape[1]
    return x * cosine + pltpu.roll(x, width - half, 1) * sine_up + pltpu.roll(x, half, 1) * sine_down


def project_kernel(n_ref, w_ref, cos_ref, up_ref, down_ref, out_ref):
    j = pl.program_id(0)
    x = nn(n_ref[...], w_ref[...])
    turned = spin(x, cos_ref[...], up_ref[...], down_ref[...])
    lane = lax.broadcasted_iota(jnp.int32, x.shape, 1)
    keep = (j < D // CHUNK) | (lane < KW)
    out_ref[...] = jnp.where(keep, turned, x).astype(jnp.bfloat16)


def project(normed, weights, tables):
    rows = normed.shape[0]
    chunks = (D + 4 * KW) // CHUNK
    table = pl.BlockSpec((rows, CHUNK), lambda j: (0, 0))
    return pl.pallas_call(
        project_kernel,
        grid=(chunks,),
        in_specs=[pl.BlockSpec((rows, D), lambda j: (0, 0)), pl.BlockSpec((D, CHUNK), lambda j: (0, j)), table, table, table],
        out_specs=pl.BlockSpec((rows, CHUNK), lambda j: (0, j)),
        out_shape=jax.ShapeDtypeStruct((rows, chunks * CHUNK), jnp.bfloat16),
        compiler_params=pltpu.CompilerParams(vmem_limit_bytes=48 << 20),
        cost_estimate=work(19),
        name="project",
    )(normed, weights, *tables)


def forward_kernel(blocks, q_ref, *refs):
    kv_refs = refs[:blocks]
    bias_ref, ctx_ref, lse_ref = refs[blocks:]
    rows = q_ref.shape[0]
    bias = [bias_ref[s] for s in range(blocks)]
    lane = lax.broadcasted_iota(jnp.int32, (rows, 128), 1)
    lse_all = jnp.zeros((rows, 128), jnp.float32)
    for h in range(QW // HEAD_DIM):
        c = h // GROUP
        q = q_ref[:, head(h)]
        scores = [nt(q, kv_refs[s][:, head(c)]) * (SCALE * LOG2E) + bias_ref[s] for s in range(blocks)]
        top = functools.reduce(jnp.maximum, scores).max(axis=1, keepdims=True)
        probs = [jnp.exp2(x - top) for x in scores]
        total = functools.reduce(jnp.add, probs).sum(axis=1, keepdims=True)
        ctx = functools.reduce(jnp.add, [nn(p.astype(jnp.bfloat16), kv_refs[s][:, KW + c * HEAD_DIM:KW + (c + 1) * HEAD_DIM]) for s, p in enumerate(probs)])
        ctx_ref[:, head(h)] = (ctx / total).astype(jnp.bfloat16)
        lse_all = jnp.where(lane == h, top + jnp.log2(total), lse_all)
    lse_ref[...] = lse_all


def attend(qkv, kv_blocks, bias, at):
    rows = kv_blocks[0].shape[0]
    blocks = len(kv_blocks)
    kv_spec = pl.BlockSpec((rows, 2 * KW), lambda h: (0, h))
    return pl.pallas_call(
        functools.partial(forward_kernel, blocks),
        grid=(HALVES,),
        in_specs=[pl.BlockSpec((rows, QW), lambda h: (at, h))] + [kv_spec] * blocks + [pl.BlockSpec((blocks, rows, rows), lambda h: (0, 0, 0))],
        out_specs=[pl.BlockSpec((rows, QW), lambda h: (0, h)), pl.BlockSpec((rows, 128), lambda h: (0, h))],
        out_shape=[jax.ShapeDtypeStruct((rows, D), jnp.bfloat16), jax.ShapeDtypeStruct((rows, HALVES * 128), jnp.float32)],
        compiler_params=pltpu.CompilerParams(vmem_limit_bytes=48 << 20),
        cost_estimate=work(23),
        name="attend",
    )(qkv, *kv_blocks, bias)


def backward_kernel(blocks, skipped, q_ref, dctx_ref, ctx_ref, lse_ref, *refs):
    kv_refs = refs[:blocks]
    bias_ref, cos_ref, up_ref, down_ref = refs[blocks:blocks + 4]
    dq_ref = refs[blocks + 4 + skipped]
    dkv_refs = refs[blocks + 5 + skipped:2 * blocks + 5 + skipped]
    dq_acc = refs[-1]
    rows = q_ref.shape[0]
    count = QW // HEAD_DIM
    owner = lax.broadcasted_iota(jnp.int32, (count, QW), 0)
    lane = lax.broadcasted_iota(jnp.int32, (count, QW), 1)
    pick = ((lane >= owner * HEAD_DIM) & (lane < owner * HEAD_DIM + HEAD_DIM)).astype(jnp.float32)
    product = dctx_ref[...].astype(jnp.float32) * ctx_ref[...].astype(jnp.float32)
    delta = lax.dot_general(pick, product, (((1,), (1,)), ((), ())), precision=lax.Precision.HIGHEST, preferred_element_type=jnp.float32)
    for c in range(KV_HEADS // HALVES):
        heads = range(c * GROUP, (c + 1) * GROUP)
        qs = [q_ref[:, head(h)] for h in heads]
        ds = [dctx_ref[:, head(h)] for h in heads]
        q_stack = jnp.concatenate(qs, axis=0)
        d_stack = jnp.concatenate(ds, axis=0)
        dq = [None] * GROUP
        for s in range(blocks):
            k = kv_refs[s][:, head(c)]
            v = kv_refs[s][:, KW + c * HEAD_DIM:KW + (c + 1) * HEAD_DIM]
            ps, dss = [], []
            for g, h in enumerate(heads):
                score = nt(k, qs[g]) * (SCALE * LOG2E) + bias_ref[s]
                p = jnp.exp2(score - lse_ref[h:h + 1, :])
                dp = nt(v, ds[g])
                d = (p * (dp - delta[h:h + 1, :])).astype(jnp.bfloat16)
                ps.append(p.astype(jnp.bfloat16))
                dss.append(d)
                term = tn(d, k)
                dq[g] = term if dq[g] is None else dq[g] + term
            dkv_refs[s][:, head(c)] = (nn(jnp.concatenate(dss, axis=1), q_stack) * SCALE).astype(jnp.bfloat16)
            dkv_refs[s][:, KW + c * HEAD_DIM:KW + (c + 1) * HEAD_DIM] = nn(jnp.concatenate(ps, axis=1), d_stack).astype(jnp.bfloat16)
        for g, h in enumerate(heads):
            dq_acc[:, head(h)] = dq[g] * SCALE
    for j in range(QW // CHUNK):
        part = slice(j * CHUNK, (j + 1) * CHUNK)
        dq_ref[:, part] = spin(dq_acc[:, part], cos_ref[...], -up_ref[...], -down_ref[...]).astype(jnp.bfloat16)


def attend_back(qkv, dctx, ctx, lse_rows, kv_blocks, bias_t, tables, at, half, before=None):
    rows = kv_blocks[0].shape[0]
    blocks = len(kv_blocks)
    count = QW // HEAD_DIM
    lanes = pl.BlockSpec((rows, QW), lambda h: (0, half))
    kv_spec = pl.BlockSpec((rows, 2 * KW), lambda h: (0, half))
    table = pl.BlockSpec((rows, CHUNK), lambda h: (at, 0))
    before = [] if before is None else list(before)
    inputs = 4 + blocks + 4
    outs = pl.pallas_call(
        functools.partial(backward_kernel, blocks, len(before)),
        grid=(1,),
        in_specs=[pl.BlockSpec((rows, QW), lambda h: (at, half)), lanes, lanes, pl.BlockSpec((count, rows), lambda h: (half, 0))]
        + [kv_spec] * blocks + [pl.BlockSpec((blocks, rows, rows), lambda h: (0, 0, 0)), table, table, table]
        + [pl.BlockSpec(memory_space=pl.ANY)] * len(before),
        out_specs=[lanes] + [kv_spec] * blocks,
        out_shape=[jax.ShapeDtypeStruct((rows, D), jnp.bfloat16)] + [jax.ShapeDtypeStruct((rows, 4 * KW), jnp.bfloat16)] * blocks,
        scratch_shapes=[pltpu.VMEM((rows, QW), jnp.float32)],
        input_output_aliases={inputs + k: k for k in range(len(before))},
        compiler_params=pltpu.CompilerParams(vmem_limit_bytes=48 << 20),
        cost_estimate=work(100),
        name="attend_back",
    )(qkv, dctx, ctx, lse_rows, *kv_blocks, bias_t, *tables, *before)
    return outs


RMS_EPS = 1e-05
ROPE_BASE = 1000000.0


def finish_kernel(own_ref, other_ref, cos_ref, up_ref, down_ref, out_ref):
    x = own_ref[...].astype(jnp.float32) + other_ref[...].astype(jnp.float32)
    turned = spin(x, cos_ref[...], -up_ref[...], -down_ref[...])
    lane = lax.broadcasted_iota(jnp.int32, x.shape, 1)
    out_ref[...] = jnp.where(lane < KW, turned, x).astype(jnp.bfloat16)


def finish_keys(own, other, tables, at):
    rows = own.shape[0]
    half = pl.BlockSpec((rows, 2 * KW), lambda h: (0, h))
    table = pl.BlockSpec((rows, CHUNK), lambda h: (at, 0))
    return pl.pallas_call(
        finish_kernel,
        grid=(HALVES,),
        in_specs=[half, half, table, table, table],
        out_specs=half,
        out_shape=jax.ShapeDtypeStruct(own.shape, jnp.bfloat16),
        cost_estimate=work(2),
        name="finish_keys",
    )(own, other, *tables)


def rms_scale(values):
    return lax.rsqrt(jnp.mean(values * values, axis=-1, keepdims=True) + RMS_EPS)


def norm_back(grad_normed, gain, normed_x, scale_row, grad_rest):
    scaled = grad_normed * gain
    inner = jnp.mean(scaled * normed_x, axis=-1, keepdims=True)
    return grad_rest + scale_row * (scaled - normed_x * inner)


def rope_lanes(position):
    lane = jnp.arange(CHUNK, dtype=jnp.int32) % HEAD_DIM
    half = HEAD_DIM // 2
    index = (lane % half).astype(jnp.float32)
    inverse = jnp.exp(index * (-2.0 * math.log(ROPE_BASE) / HEAD_DIM))
    angles = position.astype(jnp.float32)[:, None] * inverse[None, :]
    sine = jnp.sin(angles)
    first = (lane < half)[None, :]
    return jnp.cos(angles), jnp.where(first, -sine, 0.0), jnp.where(first, 0.0, sine)


def stream_layout(starts, places):
    begun = starts[:, None, :] <= places[None, :, None]
    doc_ids = jnp.sum(begun.astype(jnp.int32), axis=-1) - 1
    first_token = jnp.max(jnp.where(begun, starts[:, None, :], 0), axis=-1)
    return doc_ids, places[None, :] - first_token


def right_pairs(count, lowest=0):
    return [(k, k + 1) for k in range(lowest, count - 1)]


def left_pairs(count):
    return [(k + 1, k) for k in range(count - 1)]


def tie(x, *before):
    return lax.optimization_barrier((x,) + before)[0]


class Order:
    def __init__(self):
        self.last = ()

    def at(self, x, *more):
        return tie(x, *self.last, *more)

    def did(self, y):
        self.last = (y,)
        return y


def partner(x):
    return lax.ppermute(x, "fsdp", [(j, j ^ 1) for j in range(lax.axis_size("fsdp"))])


def same_core():
    parts = lax.axis_size("fsdp")
    return [list(range(c, parts, 2)) for c in range(2)]


def gather_chips(x):
    return lax.all_gather(x, "fsdp", axis=0, tiled=True, axis_index_groups=same_core())


def scatter_chips(x, *before):
    parts = lax.axis_size("fsdp")
    chips, chip = parts // 2, lax.axis_index("fsdp") // 2
    blocks = x.reshape((chips, x.shape[0] // chips) + x.shape[1:])
    take = lambda q: lax.dynamic_index_in_dim(blocks, q, 0, keepdims=False)
    came = [lax.ppermute(take(chip ^ d), "fsdp", [(j, j ^ (2 * d)) for j in range(parts)]) for d in range(1, chips)]
    return take(chip), came


def added(pieces):
    own, came = pieces
    return sum((c.astype(jnp.float32) for c in came), own.astype(jnp.float32))


def exchange(blocks):
    parts = lax.axis_size("fsdp")
    me = lax.axis_index("fsdp")
    chips, core = parts // 2, me % 2
    shape = blocks.shape[1:]
    blocks = blocks.reshape((chips, 2) + shape)
    mine = lax.dynamic_index_in_dim(blocks, core, 1, keepdims=False)
    came = partner(lax.dynamic_index_in_dim(blocks, 1 - core, 1, keepdims=False))
    return jnp.where(core == 0, jnp.stack([mine, came], axis=1), jnp.stack([came, mine], axis=1))


def exchange_chips(pair):
    parts = lax.axis_size("fsdp")
    chips, chip = parts // 2, lax.axis_index("fsdp") // 2
    own = lax.dynamic_index_in_dim(pair, chip, 0, keepdims=True)
    pieces = [own]
    for d in range(1, chips):
        block = lax.dynamic_index_in_dim(pair, chip ^ d, 0, keepdims=True)
        pieces.append(lax.ppermute(block, "fsdp", [(j, j ^ (2 * d)) for j in range(parts)]))
    return pieces


def exchanged(pieces):
    parts = lax.axis_size("fsdp")
    chip = lax.axis_index("fsdp") // 2
    out = jnp.zeros((parts // 2,) + pieces[0].shape[1:], pieces[0].dtype)
    for d, piece in enumerate(pieces):
        out = lax.dynamic_update_slice_in_dim(out, piece, chip ^ d, 0)
    return out


def columns_kernel(blocks, place_ref, gate_ref, up_ref, out_ref):
    j = pl.program_id(0)

    @pl.when(place_ref[blocks + j] == 0)
    def _():
        out_ref[...] = gate_ref[...]

    @pl.when(place_ref[blocks + j] == 1)
    def _():
        out_ref[...] = up_ref[...]


def columns_for(w_gate, w_up, picks, width):
    rows = w_gate.shape[0]
    blocks = len(picks)
    if width % 128:
        both = jnp.stack([w_gate.reshape(rows, -1, width), w_up.reshape(rows, -1, width)])
        return jnp.concatenate([both[which, :, at] for at, which in picks], axis=1)
    place = jnp.stack([jnp.asarray(x, jnp.int32) for x in [p[0] for p in picks] + [p[1] for p in picks]])
    source = lambda own: pl.BlockSpec(
        (rows, width), lambda j, place: (0, jnp.where(place[blocks + j] == own, place[j], place[0]))
    )
    return pl.pallas_call(
        functools.partial(columns_kernel, blocks),
        grid_spec=pltpu.PrefetchScalarGridSpec(
            num_scalar_prefetch=1,
            grid=(blocks,),
            in_specs=[source(0), source(1)],
            out_specs=pl.BlockSpec((rows, width), lambda j, place: (0, j)),
        ),
        out_shape=jax.ShapeDtypeStruct((rows, blocks * width), w_gate.dtype),
        cost_estimate=work(blocks),
        name="columns_for",
    )(place, w_gate, w_up)


def weave_kernel(count, chips, width, place_ref, *refs):
    out_ref = refs[-1]
    j = pl.program_id(0)
    half = 2 * width
    for d in range(chips):
        for c in range(2):
            mine, other = refs[2 * (c * chips + d):2 * (c * chips + d) + 2]
            for odd in range(2):
                @pl.when((j == 2 * d + c) & (place_ref[count] == odd))
                def _(mine=mine, other=other, c=c, odd=odd):
                    for which, ref in ((odd, mine), (1 - odd, other)):
                        for k in range(2):
                            at = which * half + k * width
                            from_lane = (k ^ c) * width
                            out_ref[:, at:at + width] = ref[:, from_lane:from_lane + width]


def weave(mine, other, places, odd, width):
    rows = mine[0].shape[0]
    count = len(mine)
    chips = count // 2
    tile = next(t for t in (160, 64, 32, 16) if rows % t == 0)
    tiles = rows // tile
    specs, arrays = [], []
    for c in range(2):
        for d in range(chips):
            index = lambda j, t, place, k=2 * d + c: (jnp.where(j == k, t, 0), 0)
            specs += [pl.BlockSpec((tile, 2 * width), index)] * 2
            arrays += [mine[c * chips + d], other[c * chips + d]]
    return pl.pallas_call(
        functools.partial(weave_kernel, count, chips, width),
        grid_spec=pltpu.PrefetchScalarGridSpec(
            num_scalar_prefetch=1,
            grid=(count, tiles),
            in_specs=specs,
            out_specs=pl.BlockSpec((tile, 4 * width), lambda j, t, place: (place[j] * tiles + t, 0)),
        ),
        out_shape=jax.ShapeDtypeStruct((count * rows, 4 * width), mine[0].dtype),
        compiler_params=pltpu.CompilerParams(vmem_limit_bytes=56 << 20),
        cost_estimate=work(21),
        name="weave",
    )(jnp.stack([jnp.asarray(x, jnp.int32) for x in places + [odd]]), *arrays)


class Reshard:
    def __init__(self, w_gate, w_up):
        parts = lax.axis_size("fsdp")
        me = lax.axis_index("fsdp")
        self.chips = parts // 2
        self.chip, self.core = me // 2, me % 2
        self.odd = lax.axis_index("sp") % 2
        self.width = w_gate.shape[1] // parts
        pair = lambda d, which: [(2 * (self.chip ^ d) + c, which) for c in (self.core, 1 - self.core)]
        self.local = columns_for(w_gate, w_up, pair(0, self.odd) + pair(0, 1 - self.odd), self.width)
        self.sent = [columns_for(w_gate, w_up, pair(d, self.odd), self.width) for d in range(1, self.chips)]

    def fetch(self):
        parts = 2 * self.chips
        half = 2 * self.width
        self.mine = [self.local[:, :half]] + [
            lax.ppermute(x, "fsdp", [(j, j ^ (2 * d)) for j in range(parts)]) for d, x in enumerate(self.sent, 1)
        ]
        pairs = [(k, k ^ 1) for k in range(lax.axis_size("sp"))]
        self.other = [self.local[:, half:]] + [lax.ppermute(x, "sp", pairs) for x in self.mine[1:]]
        return self.other[1:]

    def result(self, *before):
        mine = self.mine + [partner(x) for x in self.mine]
        other = self.other + [partner(x) for x in self.other]
        places = []
        for d in range(self.chips):
            places += [2 * (self.chip ^ d) + self.core, 2 * (self.chip ^ d) + 1 - self.core]
        return weave([tie(mine[0], *before)] + mine[1:], other, places, self.odd, self.width)


def features_kernel(count, width, core_ref, x_ref, mine_ref, other_ref):
    for c in range(2):
        @pl.when(core_ref[0] == c)
        def _(c=c):
            for q in range(count):
                at = slice(q * width, (q + 1) * width)
                mine_ref[:, at] = x_ref[:, (2 * q + c) * width:(2 * q + c + 1) * width]
                other_ref[:, at] = x_ref[:, (2 * q + 1 - c) * width:(2 * q + 2 - c) * width]


def features(x, core, width):
    rows = x.shape[0]
    count = x.shape[1] // (2 * width)
    tile = min(rows, 256)
    out = pl.BlockSpec((tile, count * width), lambda t, core: (t, 0))
    return pl.pallas_call(
        functools.partial(features_kernel, count, width),
        grid_spec=pltpu.PrefetchScalarGridSpec(
            num_scalar_prefetch=1,
            grid=(rows // tile,),
            in_specs=[pl.BlockSpec((tile, x.shape[1]), lambda t, core: (t, 0))],
            out_specs=[out, out],
        ),
        out_shape=[jax.ShapeDtypeStruct((rows, count * width), x.dtype)] * 2,
        cost_estimate=work(3),
        name="features",
    )(core.reshape(1).astype(jnp.int32), x)


def sum_tn_kernel(segments, pairs, *refs):
    lefts = [ref[...] for ref in refs[:pairs]]
    extra = refs[pairs + segments * pairs:-1]
    out_ref = refs[-1]
    width = out_ref.shape[-1] // segments
    for j in range(segments):
        rights = refs[pairs + j * pairs:pairs + (j + 1) * pairs]
        part = slice(j * width, (j + 1) * width)
        total = sum(tn(a, b[...]) for a, b in zip(lefts, rights))
        if len(out_ref.shape) == 2:
            for more in extra:
                total = total + more[:, part].astype(jnp.float32)
            out_ref[:, part] = total.astype(out_ref.dtype)
        else:
            slabs, blocks, rows, _ = out_ref.shape
            for s in range(slabs):
                for k in range(blocks):
                    at = (k * slabs + s) * rows
                    piece = total[at:at + rows]
                    for more in extra:
                        piece = piece + more[s, k, :, part].astype(jnp.float32)
                    out_ref[s, k, :, part] = piece.astype(out_ref.dtype)


def sum_tn(lefts, rights, half, *extra, weight=1, slabs=1, rows=1):
    segments, pairs = len(rights), len(lefts)
    tokens = lefts[0].shape[0]
    if segments == 1:
        width = lefts[0].shape[1] // 2
        if width % 128:
            total = sum(tn(a[:, half * width:(half + 1) * width], b) for a, b in zip(lefts, rights[0]))
            return sum((e.astype(jnp.float32) for e in extra), total).astype(jnp.bfloat16)
        shape = (width, D)
        block = (width, CHUNK)
        left = pl.BlockSpec((tokens, width), lambda i: (0, half))
        right = pl.BlockSpec((tokens, CHUNK), lambda i: (0, i))
        out = pl.BlockSpec(block, lambda i: (0, i))
    else:
        width = rights[0][0].shape[1] // 2
        if width % 128:
            cut = slice(half * width, (half + 1) * width)
            total = jnp.concatenate([sum(tn(a, b[:, cut]) for a, b in zip(lefts, r)) for r in rights], axis=1)
            total = jnp.moveaxis(total.reshape(-1, slabs, rows, segments * width), 1, 0)
            return sum((e.astype(jnp.float32) for e in extra), total).astype(jnp.bfloat16)
        blocks = CHUNK // (slabs * rows)
        shape = (slabs, D // (slabs * rows), rows, segments * width)
        left = pl.BlockSpec((tokens, CHUNK), lambda i: (0, i))
        right = pl.BlockSpec((tokens, width), lambda i: (0, half))
        out = pl.BlockSpec((slabs, blocks, rows, segments * width), lambda i: (0, i, 0, 0))
    return pl.pallas_call(
        functools.partial(sum_tn_kernel, segments, pairs),
        grid=(D // CHUNK,),
        in_specs=[left] * pairs + [right] * (segments * pairs) + [out] * len(extra),
        out_specs=out,
        out_shape=jax.ShapeDtypeStruct(shape, jnp.bfloat16),
        compiler_params=pltpu.CompilerParams(vmem_limit_bytes=56 << 20),
        cost_estimate=work((26 if segments == 2 else 16) * weight),
        name="sum_tn",
    )(*lefts, *[b for r in rights for b in r], *extra)


def ffn_kernel(n_ref, g_ref, wg_ref, wu_ref, wd_ref, hidden_ref, gate_grad_ref, up_grad_ref):
    gate = nn(n_ref[...], wg_ref[...])
    up = nn(n_ref[...], wu_ref[...])
    hidden_grad = nt(g_ref[...], wd_ref[...])
    sigm = 1.0 / (1.0 + jnp.exp(-gate))
    act = gate * sigm
    hidden_ref[...] = (act * up).astype(jnp.bfloat16)
    up_grad_ref[...] = (hidden_grad * act).astype(jnp.bfloat16)
    gate_grad_ref[...] = (hidden_grad * up * (sigm + act * (1.0 - sigm))).astype(jnp.bfloat16)


def feed_forward(n2, g, w_both, w_down):
    tokens, hidden = n2.shape[0], w_down.shape[0]
    tile = 256 if hidden % 256 == 0 else 128
    tiles = hidden // tile
    full = pl.BlockSpec((tokens, D), lambda j: (0, 0))
    out = pl.BlockSpec((tokens, tile), lambda j: (0, j))
    return pl.pallas_call(
        ffn_kernel,
        grid=(tiles,),
        in_specs=[full, full, pl.BlockSpec((D, tile), lambda j: (0, j)), pl.BlockSpec((D, tile), lambda j: (0, tiles + j)),
                  pl.BlockSpec((tile, D), lambda j: (j, 0))],
        out_specs=[out] * 3,
        out_shape=[jax.ShapeDtypeStruct((tokens, hidden), jnp.bfloat16)] * 3,
        compiler_params=pltpu.CompilerParams(vmem_limit_bytes=56 << 20),
        cost_estimate=work(36),
        name="feed_forward",
    )(n2, g, w_both, w_both, w_down)


def sum_nt_kernel(*refs):
    pairs = len(refs) // 2
    refs[-1][...] = sum(nt(refs[k][...], refs[pairs + k][...]) for k in range(pairs)).astype(jnp.bfloat16)


def sum_nt(lefts, right, weight=1):
    (tokens, depth), columns = lefts[0].shape, right.shape[0]
    tile, block = tokens // 2, columns // 2
    return pl.pallas_call(
        sum_nt_kernel,
        grid=(columns // block, tokens // tile),
        in_specs=[pl.BlockSpec((tile, depth), lambda j, i: (i, 0))] * len(lefts)
        + [pl.BlockSpec((block, depth), lambda j, i, k=k: (j, k)) for k in range(len(lefts))],
        out_specs=pl.BlockSpec((tile, block), lambda j, i: (i, j)),
        out_shape=jax.ShapeDtypeStruct((tokens, columns), jnp.bfloat16),
        compiler_params=pltpu.CompilerParams(vmem_limit_bytes=56 << 20),
        cost_estimate=work(26 * weight),
        name="sum_nt",
    )(*lefts, *([right] * len(lefts)))


def plain_nn_kernel(a_ref, b_ref, out_ref):
    out_ref[...] = nn(a_ref[...], b_ref[...]).astype(jnp.bfloat16)


def plain_nn(a, b, weight=1):
    (tokens, depth), columns = a.shape, b.shape[1]
    return pl.pallas_call(
        plain_nn_kernel,
        grid=(columns // CHUNK,),
        in_specs=[pl.BlockSpec((tokens, depth), lambda j: (0, 0)), pl.BlockSpec((depth, CHUNK), lambda j: (0, j))],
        out_specs=pl.BlockSpec((tokens, CHUNK), lambda j: (0, j)),
        out_shape=jax.ShapeDtypeStruct((tokens, columns), jnp.bfloat16),
        compiler_params=pltpu.CompilerParams(vmem_limit_bytes=56 << 20),
        cost_estimate=work(16 * weight),
        name="plain_nn",
    )(a, b)


class KeySum:
    def __init__(self, parts):
        self.parts = parts
        self.running = parts[-1]
        self.hops = 0

    def hop(self, *before):
        n = lax.axis_size("sp")
        s = self.hops
        if s:
            self.running = (self.parts[n - 1 - s].astype(jnp.float32) + self.running.astype(jnp.float32)).astype(jnp.bfloat16)
        pairs = [(n - 1 - k, n - 2 - k) for k in range(s + 1)]
        self.running = lax.ppermute(tie(self.running, *before), "sp", pairs)
        self.hops += 1
        return self.running

    def result(self):
        while self.hops < lax.axis_size("sp") - 1:
            self.hop()
        return self.parts[0], self.running


def rows_of(pieces):
    return jnp.concatenate(pieces, axis=0)


def body(tokens, doc_starts, cotangent, gain_attn, gain_ffn, w_query, w_key, w_value, w_out, w_gate, w_up, w_down):
    micro, _, rows, _ = tokens.shape
    parts = lax.axis_size("fsdp")
    chips = parts // 2
    core = lax.axis_index("fsdp") % 2
    seq = lax.axis_size("sp")
    place = lax.axis_index("sp")
    count = micro * rows
    d_own = w_query.shape[0]
    hidden_own = w_down.shape[0]
    hidden_chip = 2 * hidden_own
    bf16 = jnp.bfloat16
    f32 = jnp.float32

    gains = jnp.pad(jnp.stack([gain_attn, gain_ffn], axis=1), ((0, 0), (0, 126)))
    w_in = jnp.concatenate(
        [w_query, w_key[:, :KW], w_value[:, :KW], w_key[:, KW:], w_value[:, KW:], gains], axis=1
    )
    w_in = lax.all_gather(w_in, "fsdp", axis=0, tiled=True)
    w_out_full = lax.all_gather(w_out, "fsdp", axis=0, tiled=True)
    gain_one = w_in[:, D + 4 * KW].astype(f32)
    gain_two = w_in[:, D + 4 * KW + 1].astype(f32)
    reshard = Reshard(w_gate, w_up)
    came_columns = reshard.fetch()

    starts = doc_starts.reshape(micro, -1)
    offsets = (place - jnp.arange(seq, dtype=jnp.int32)) * rows
    key_places = (offsets[:, None] + jnp.arange(rows, dtype=jnp.int32)[None, :]).reshape(-1)
    docs, positions = stream_layout(starts, key_places)
    docs = docs.reshape(micro, seq, rows)
    key_places = key_places.reshape(seq, rows)
    tables = rope_lanes(positions.reshape(micro, seq, rows)[:, 0].reshape(count))
    allowed = (docs[:, :1, :, None] == docs[:, :, None, :]) & (
        key_places[None, :, None, :] <= key_places[None, :1, :, None]
    )
    bias = jnp.where(allowed, 0.0, -1e30).astype(f32)
    bias_t = jnp.where(jnp.swapaxes(allowed, 2, 3), 0.0, -1e30).astype(f32)

    inputs = tokens.reshape(count, D).astype(f32)
    scale_one = rms_scale(inputs)
    normed_x1 = inputs * scale_one
    normed = tie((normed_x1 * gain_one).astype(bf16), *tables, bias, bias_t)
    normed = tie(normed, *came_columns)
    w_down_other = partner(w_down)
    order = Order()
    qkv = order.did(project(normed, w_in, tables))

    g_low = cotangent.reshape(micro, rows, D)
    g_all = [gather_chips(tie(g_low[0], qkv))]
    state, n2_alls = [], []
    for m in range(micro):
        kv = [qkv[m * rows:(m + 1) * rows, D:]]
        for s in range(seq - 1):
            kv.append(lax.ppermute(kv[-1], "sp", right_pairs(seq, s)))
        context, lse = attend(order.at(qkv), kv, bias[m], m)
        lse_rows = jnp.swapaxes(lse.reshape(rows, HALVES, 128)[:, :, :QW // HEAD_DIM].reshape(rows, HEADS), 0, 1)
        mixed = inputs[m * rows:(m + 1) * rows] + nn(context, w_out_full)
        scale_two = rms_scale(mixed)
        normed_x2 = mixed * scale_two
        normed_ffn = order.did((normed_x2 * gain_two).astype(bf16))
        if m == 0:
            normed_ffn = tie(normed_ffn, g_all[0])
        n2_alls.append(gather_chips(normed_ffn))
        if m:
            g_all.append(gather_chips(tie(g_low[m], normed_ffn)))
        state.append((kv, context, lse_rows, mixed, scale_two, normed_x2))
    w_both = order.did(reshard.result(*order.last))
    w_down_chip = order.did(rows_of([order.at(w_down), w_down_other]))

    hiddens, gate_grads, up_grads, normed_grads, out_terms = [], [], [], [], []

    def forward_back(m):
        hidden, gate_grad, up_grad = feed_forward(order.at(n2_alls[m]), g_all[m], w_both, w_down_chip)
        hiddens.append(hidden)
        gate_grads.append(gate_grad)
        up_grads.append(order.did(up_grad))

    def normed_part(m, *before):
        part = order.did(sum_nt([order.at(gate_grads[m], *before), up_grads[m]], w_both))
        normed_grads.append(scatter_chips(part))

    def out_part(m, *before):
        part = order.did(plain_nn(order.at(hiddens[m], *before), w_down_chip))
        out_terms.append(scatter_chips(part))

    slab = d_own // seq
    ff = parts * hidden_own
    forward_back(0)
    normed_part(0, g_all[-1])
    for m in range(1, micro):
        forward_back(m)
    wide = dict(slabs=seq, rows=slab)
    wide_other = order.did(sum_tn(n2_alls, [[order.at(gate_grads[0])] + gate_grads[1:], up_grads], 1, **wide))
    wide_came = partner(wide_other)
    down_other = order.did(sum_tn([order.at(hiddens[0])] + hiddens[1:], [g_all], 1))
    down_came = partner(down_other)
    wide_grad = order.did(sum_tn(n2_alls, [[order.at(gate_grads[0])] + gate_grads[1:], up_grads], 0, wide_came, **wide))
    wide_mine = lax.psum_scatter(wide_grad, "sp", scatter_dimension=0, tiled=False)
    down_grad = order.did(sum_tn([order.at(hiddens[0])] + hiddens[1:], [g_all], 0, down_came))
    down_total = lax.psum(down_grad, "sp")
    normed_part(1)
    for m in range(micro):
        out_part(m)
    normed_mine, normed_other = features(order.at(normed), core, d_own)
    normed_chip = rows_of([normed_mine, partner(normed_other)])
    context_mine, context_other = features(rows_of([state[m][1] for m in range(micro)]), core, d_own)
    context_chip = rows_of([context_mine, partner(context_other)])
    order.did(normed_mine)

    mixed_grads, attn_grads, query_grads, kv_sums = [], [], [], []
    gain_two_term = 0.0
    chip_rows = lambda pieces: rows_of(pieces + [partner(p) for p in pieces])
    for m in range(micro):
        kv, context, lse_rows, mixed, scale_two, normed_x2 = state[m]
        if m == micro - 1:
            order.last = order.last + (wide_mine,)
            pieces = exchange_chips(exchange(wide_mine))
        normed_grad = added((order.at(normed_grads[m][0]), normed_grads[m][1]))
        gain_two_term = gain_two_term + jnp.sum(normed_grad * normed_x2, axis=0)
        mixed_grad = norm_back(normed_grad, gain_two, normed_x2, scale_two, g_low[m].astype(f32))
        attn_grad = mixed_grad.astype(bf16)
        attn_grads.append(attn_grad)
        mixed_grads.append(mixed_grad)
        context_grad = order.did(nt(attn_grad, w_out_full).astype(bf16))
        if m == micro - 1:
            out_half = order.did(tn(context_chip, chip_rows(attn_grads)).astype(bf16))
            out_shard = added(scatter_chips(out_half)).astype(bf16)
        args = (context, lse_rows, kv, bias_t[m], tables, m)
        first = attend_back(qkv, order.at(context_grad), *args, 0)
        order.last = ()
        if m == micro - 1:
            order.last = tuple(pieces)
        second = attend_back(qkv, order.at(context_grad), *args, 1, first)
        query_grads.append(order.did(second[0]))
        kv_sums.append(KeySum(second[1:]))
        kv_sums[-1].hop()

    order.last = order.last + (out_shard, down_total)
    wide_part = exchanged([order.at(pieces[0], *pieces[1:])] + pieces[1:])
    wide_part = order.did(jnp.moveaxis(wide_part.reshape(parts, slab, 2, hidden_own), 0, 2).reshape(slab, 2 * ff))
    wide_total = lax.all_gather(wide_part, "sp", axis=0, tiled=True)
    query_half = order.did(tn(normed_chip, chip_rows(query_grads[:-1] + [order.at(query_grads[-1])])).astype(bf16))
    query_shard = added(scatter_chips(query_half)).astype(bf16)
    kv_hop = tuple(keys.hop() for keys in kv_sums)
    normed_grad = order.did(nt(order.at(rows_of(query_grads), *kv_hop), w_in[:, :D]))
    kv_grads = [keys.result() for keys in kv_sums]
    kv_grads = [order.did(finish_keys(own, order.at(came), tables, m)) for m, (own, came) in enumerate(kv_grads)]
    kv_grad = rows_of(kv_grads)
    kv_half = order.did(tn(normed_chip, chip_rows(kv_grads)).astype(bf16))
    normed_grad = normed_grad + nt(kv_grad, w_in[:, D:D + 4 * KW])
    gain_one_term = jnp.sum(normed_grad * normed_x1, axis=0)
    input_grad = norm_back(normed_grad, gain_one, normed_x1, scale_one, rows_of(mixed_grads)).astype(bf16)

    gain_blocks = jnp.stack([gain_one_term, gain_two_term], axis=1).astype(bf16).reshape(chips, 2, d_own, 2)
    gain_lanes = jnp.concatenate(
        [lax.dynamic_index_in_dim(gain_blocks, c, 1, keepdims=False) for c in (core, 1 - core)], axis=2
    ).reshape(chips * d_own, 4)
    kv_shard = added(scatter_chips(jnp.concatenate([kv_half, jnp.pad(gain_lanes, ((0, 0), (0, 124)))], axis=1))).astype(bf16)
    out_total, query_total, kv_total = lax.psum(
        (tie(out_shard, down_total), tie(query_shard, wide_total), tie(kv_shard, wide_total)), "sp"
    )
    query_total, kv_total = query_total.astype(f32), kv_total.astype(f32)
    kv_piece = lambda k: kv_total[:, k * KW:(k + 1) * KW]
    gain_lanes = kv_total[:, 4 * KW:4 * KW + 4]
    gain_total = gain_lanes[:, :2] + partner(gain_lanes)[:, 2:]
    outputs = [(state[m][3] + added((order.at(out_terms[m][0]), out_terms[m][1]))).astype(bf16) for m in range(micro)]
    return (
        rows_of(outputs).reshape(tokens.shape),
        input_grad.reshape(tokens.shape),
        gain_total[:, 0],
        gain_total[:, 1],
        query_total,
        jnp.concatenate([kv_piece(0), kv_piece(2)], axis=1),
        jnp.concatenate([kv_piece(1), kv_piece(3)], axis=1),
        out_total.astype(f32),
        wide_total[:, :ff].astype(f32),
        wide_total[:, ff:].astype(f32),
        down_total.astype(f32),
    )


def solution(mesh):
    split = P("fsdp", None)
    stream = P(None, "fsdp", "sp", None)
    return jax.shard_map(
        body,
        mesh=mesh,
        in_specs=(stream, P(None, "fsdp", None), stream, P("fsdp"), P("fsdp")) + (split,) * 7,
        out_specs=(stream, stream, P("fsdp"), P("fsdp")) + (split,) * 7,
        check_vma=False,
    )
```

```python
import functools, math
import jax, jax.numpy as jnp
from jax import lax
from jax.experimental import pallas as pl
from jax.experimental.pallas import tpu as pltpu
from jax.sharding import PartitionSpec as P

D = 2560
HEADS = 32
KV_HEADS = 8
HEAD_DIM = 80
GROUP = HEADS // KV_HEADS
HALVES = 2
SCALE = HEAD_DIM ** -0.5
LOG2E = 1.0 / math.log(2.0)
QW = D // HALVES
KW = KV_HEADS * HEAD_DIM // HALVES
CHUNK = 640
SPEED = 1 << 28


def work(micros):
    return pl.CostEstimate(flops=micros * SPEED, bytes_accessed=1 << 16, transcendentals=0)


def nt(left, right):
    return lax.dot_general(left, right, (((1,), (1,)), ((), ())), preferred_element_type=jnp.float32)


def tn(left, right):
    return lax.dot_general(left, right, (((0,), (0,)), ((), ())), preferred_element_type=jnp.float32)


def nn(left, right):
    return jnp.dot(left, right, preferred_element_type=jnp.float32)


def head(h):
    return slice(h * HEAD_DIM, (h + 1) * HEAD_DIM)


def spin(x, cosine, sine_up, sine_down):
    half = HEAD_DIM // 2
    width = x.shape[1]
    return x * cosine + pltpu.roll(x, width - half, 1) * sine_up + pltpu.roll(x, half, 1) * sine_down


def project_kernel(n_ref, w_ref, cos_ref, up_ref, down_ref, out_ref):
    j = pl.program_id(0)
    x = nn(n_ref[...], w_ref[...])
    turned = spin(x, cos_ref[...], up_ref[...], down_ref[...])
    lane = lax.broadcasted_iota(jnp.int32, x.shape, 1)
    keep = (j < D // CHUNK) | (lane < KW)
    out_ref[...] = jnp.where(keep, turned, x).astype(jnp.bfloat16)


def project(normed, weights, tables):
    rows = normed.shape[0]
    chunks = (D + 4 * KW) // CHUNK
    table = pl.BlockSpec((rows, CHUNK), lambda j: (0, 0))
    return pl.pallas_call(
        project_kernel,
        grid=(chunks,),
        in_specs=[pl.BlockSpec((rows, D), lambda j: (0, 0)), pl.BlockSpec((D, CHUNK), lambda j: (0, j)), table, table, table],
        out_specs=pl.BlockSpec((rows, CHUNK), lambda j: (0, j)),
        out_shape=jax.ShapeDtypeStruct((rows, chunks * CHUNK), jnp.bfloat16),
        compiler_params=pltpu.CompilerParams(vmem_limit_bytes=48 << 20),
        cost_estimate=work(19),
        name="project",
    )(normed, weights, *tables)


def forward_kernel(blocks, q_ref, *refs):
    kv_refs = refs[:blocks]
    bias_ref, ctx_ref, lse_ref = refs[blocks:]
    rows = q_ref.shape[0]
    bias = [bias_ref[s] for s in range(blocks)]
    lane = lax.broadcasted_iota(jnp.int32, (rows, 128), 1)
    lse_all = jnp.zeros((rows, 128), jnp.float32)
    for h in range(QW // HEAD_DIM):
        c = h // GROUP
        q = q_ref[:, head(h)]
        scores = [nt(q, kv_refs[s][:, head(c)]) * (SCALE * LOG2E) + bias_ref[s] for s in range(blocks)]
        top = functools.reduce(jnp.maximum, scores).max(axis=1, keepdims=True)
        probs = [jnp.exp2(x - top) for x in scores]
        total = functools.reduce(jnp.add, probs).sum(axis=1, keepdims=True)
        ctx = functools.reduce(jnp.add, [nn(p.astype(jnp.bfloat16), kv_refs[s][:, KW + c * HEAD_DIM:KW + (c + 1) * HEAD_DIM]) for s, p in enumerate(probs)])
        ctx_ref[:, head(h)] = (ctx / total).astype(jnp.bfloat16)
        lse_all = jnp.where(lane == h, top + jnp.log2(total), lse_all)
    lse_ref[...] = lse_all


def attend(qkv, kv_blocks, bias, at):
    rows = kv_blocks[0].shape[0]
    blocks = len(kv_blocks)
    kv_spec = pl.BlockSpec((rows, 2 * KW), lambda h: (0, h))
    return pl.pallas_call(
        functools.partial(forward_kernel, blocks),
        grid=(HALVES,),
        in_specs=[pl.BlockSpec((rows, QW), lambda h: (at, h))] + [kv_spec] * blocks + [pl.BlockSpec((blocks, rows, rows), lambda h: (0, 0, 0))],
        out_specs=[pl.BlockSpec((rows, QW), lambda h: (0, h)), pl.BlockSpec((rows, 128), lambda h: (0, h))],
        out_shape=[jax.ShapeDtypeStruct((rows, D), jnp.bfloat16), jax.ShapeDtypeStruct((rows, HALVES * 128), jnp.float32)],
        compiler_params=pltpu.CompilerParams(vmem_limit_bytes=48 << 20),
        cost_estimate=work(23),
        name="attend",
    )(qkv, *kv_blocks, bias)


def backward_kernel(blocks, skipped, q_ref, dctx_ref, ctx_ref, lse_ref, *refs):
    kv_refs = refs[:blocks]
    bias_ref, cos_ref, up_ref, down_ref = refs[blocks:blocks + 4]
    dq_ref = refs[blocks + 4 + skipped]
    dkv_refs = refs[blocks + 5 + skipped:2 * blocks + 5 + skipped]
    dq_acc = refs[-1]
    rows = q_ref.shape[0]
    count = QW // HEAD_DIM
    owner = lax.broadcasted_iota(jnp.int32, (count, QW), 0)
    lane = lax.broadcasted_iota(jnp.int32, (count, QW), 1)
    pick = ((lane >= owner * HEAD_DIM) & (lane < owner * HEAD_DIM + HEAD_DIM)).astype(jnp.float32)
    product = dctx_ref[...].astype(jnp.float32) * ctx_ref[...].astype(jnp.float32)
    delta = lax.dot_general(pick, product, (((1,), (1,)), ((), ())), precision=lax.Precision.HIGHEST, preferred_element_type=jnp.float32)
    for c in range(KV_HEADS // HALVES):
        heads = range(c * GROUP, (c + 1) * GROUP)
        qs = [q_ref[:, head(h)] for h in heads]
        ds = [dctx_ref[:, head(h)] for h in heads]
        q_stack = jnp.concatenate(qs, axis=0)
        d_stack = jnp.concatenate(ds, axis=0)
        dq = [None] * GROUP
        for s in range(blocks):
            k = kv_refs[s][:, head(c)]
            v = kv_refs[s][:, KW + c * HEAD_DIM:KW + (c + 1) * HEAD_DIM]
            ps, dss = [], []
            for g, h in enumerate(heads):
                score = nt(k, qs[g]) * (SCALE * LOG2E) + bias_ref[s]
                p = jnp.exp2(score - lse_ref[h:h + 1, :])
                dp = nt(v, ds[g])
                d = (p * (dp - delta[h:h + 1, :])).astype(jnp.bfloat16)
                ps.append(p.astype(jnp.bfloat16))
                dss.append(d)
                term = tn(d, k)
                dq[g] = term if dq[g] is None else dq[g] + term
            dkv_refs[s][:, head(c)] = (nn(jnp.concatenate(dss, axis=1), q_stack) * SCALE).astype(jnp.bfloat16)
            dkv_refs[s][:, KW + c * HEAD_DIM:KW + (c + 1) * HEAD_DIM] = nn(jnp.concatenate(ps, axis=1), d_stack).astype(jnp.bfloat16)
        for g, h in enumerate(heads):
            dq_acc[:, head(h)] = dq[g] * SCALE
    for j in range(QW // CHUNK):
        part = slice(j * CHUNK, (j + 1) * CHUNK)
        dq_ref[:, part] = spin(dq_acc[:, part], cos_ref[...], -up_ref[...], -down_ref[...]).astype(jnp.bfloat16)


def attend_back(qkv, dctx, ctx, lse_rows, kv_blocks, bias_t, tables, at, half, before=None):
    rows = kv_blocks[0].shape[0]
    blocks = len(kv_blocks)
    count = QW // HEAD_DIM
    lanes = pl.BlockSpec((rows, QW), lambda h: (0, half))
    kv_spec = pl.BlockSpec((rows, 2 * KW), lambda h: (0, half))
    table = pl.BlockSpec((rows, CHUNK), lambda h: (at, 0))
    before = [] if before is None else list(before)
    inputs = 4 + blocks + 4
    outs = pl.pallas_call(
        functools.partial(backward_kernel, blocks, len(before)),
        grid=(1,),
        in_specs=[pl.BlockSpec((rows, QW), lambda h: (at, half)), lanes, lanes, pl.BlockSpec((count, rows), lambda h: (half, 0))]
        + [kv_spec] * blocks + [pl.BlockSpec((blocks, rows, rows), lambda h: (0, 0, 0)), table, table, table]
        + [pl.BlockSpec(memory_space=pl.ANY)] * len(before),
        out_specs=[lanes] + [kv_spec] * blocks,
        out_shape=[jax.ShapeDtypeStruct((rows, D), jnp.bfloat16)] + [jax.ShapeDtypeStruct((rows, 4 * KW), jnp.bfloat16)] * blocks,
        scratch_shapes=[pltpu.VMEM((rows, QW), jnp.float32)],
        input_output_aliases={inputs + k: k for k in range(len(before))},
        compiler_params=pltpu.CompilerParams(vmem_limit_bytes=48 << 20),
        cost_estimate=work(100),
        name="attend_back",
    )(qkv, dctx, ctx, lse_rows, *kv_blocks, bias_t, *tables, *before)
    return outs


RMS_EPS = 1e-05
ROPE_BASE = 1000000.0


def finish_kernel(own_ref, other_ref, cos_ref, up_ref, down_ref, out_ref):
    x = own_ref[...].astype(jnp.float32) + other_ref[...].astype(jnp.float32)
    turned = spin(x, cos_ref[...], -up_ref[...], -down_ref[...])
    lane = lax.broadcasted_iota(jnp.int32, x.shape, 1)
    out_ref[...] = jnp.where(lane < KW, turned, x).astype(jnp.bfloat16)


def finish_keys(own, other, tables, at):
    rows = own.shape[0]
    half = pl.BlockSpec((rows, 2 * KW), lambda h: (0, h))
    table = pl.BlockSpec((rows, CHUNK), lambda h: (at, 0))
    return pl.pallas_call(
        finish_kernel,
        grid=(HALVES,),
        in_specs=[half, half, table, table, table],
        out_specs=half,
        out_shape=jax.ShapeDtypeStruct(own.shape, jnp.bfloat16),
        cost_estimate=work(2),
        name="finish_keys",
    )(own, other, *tables)


def rms_scale(values):
    return lax.rsqrt(jnp.mean(values * values, axis=-1, keepdims=True) + RMS_EPS)


def norm_back(grad_normed, gain, normed_x, scale_row, grad_rest):
    scaled = grad_normed * gain
    inner = jnp.mean(scaled * normed_x, axis=-1, keepdims=True)
    return grad_rest + scale_row * (scaled - normed_x * inner)


def rope_lanes(position):
    lane = jnp.arange(CHUNK, dtype=jnp.int32) % HEAD_DIM
    half = HEAD_DIM // 2
    index = (lane % half).astype(jnp.float32)
    inverse = jnp.exp(index * (-2.0 * math.log(ROPE_BASE) / HEAD_DIM))
    angles = position.astype(jnp.float32)[:, None] * inverse[None, :]
    sine = jnp.sin(angles)
    first = (lane < half)[None, :]
    return jnp.cos(angles), jnp.where(first, -sine, 0.0), jnp.where(first, 0.0, sine)


def stream_layout(starts, places):
    begun = starts[:, None, :] <= places[None, :, None]
    doc_ids = jnp.sum(begun.astype(jnp.int32), axis=-1) - 1
    first_token = jnp.max(jnp.where(begun, starts[:, None, :], 0), axis=-1)
    return doc_ids, places[None, :] - first_token


def right_pairs(count, lowest=0):
    return [(k, k + 1) for k in range(lowest, count - 1)]


def left_pairs(count):
    return [(k + 1, k) for k in range(count - 1)]


def tie(x, *before):
    return lax.optimization_barrier((x,) + before)[0]


class Order:
    def __init__(self):
        self.last = ()

    def at(self, x, *more):
        return tie(x, *self.last, *more)

    def did(self, y):
        self.last = (y,)
        return y


def partner(x):
    return lax.ppermute(x, "fsdp", [(j, j ^ 1) for j in range(lax.axis_size("fsdp"))])


def same_core():
    parts = lax.axis_size("fsdp")
    return [list(range(c, parts, 2)) for c in range(2)]


def gather_chips(x):
    return lax.all_gather(x, "fsdp", axis=0, tiled=True, axis_index_groups=same_core())


def scatter_chips(x, *before):
    parts = lax.axis_size("fsdp")
    chips, chip = parts // 2, lax.axis_index("fsdp") // 2
    blocks = x.reshape((chips, x.shape[0] // chips) + x.shape[1:])
    take = lambda q: lax.dynamic_index_in_dim(blocks, q, 0, keepdims=False)
    came = [lax.ppermute(take(chip ^ d), "fsdp", [(j, j ^ (2 * d)) for j in range(parts)]) for d in range(1, chips)]
    return take(chip), came


def added(pieces):
    own, came = pieces
    return sum((c.astype(jnp.float32) for c in came), own.astype(jnp.float32))


def exchange(blocks):
    parts = lax.axis_size("fsdp")
    me = lax.axis_index("fsdp")
    chips, core = parts // 2, me % 2
    shape = blocks.shape[1:]
    blocks = blocks.reshape((chips, 2) + shape)
    mine = lax.dynamic_index_in_dim(blocks, core, 1, keepdims=False)
    came = partner(lax.dynamic_index_in_dim(blocks, 1 - core, 1, keepdims=False))
    return jnp.where(core == 0, jnp.stack([mine, came], axis=1), jnp.stack([came, mine], axis=1))


def exchange_chips(pair):
    parts = lax.axis_size("fsdp")
    chips, chip = parts // 2, lax.axis_index("fsdp") // 2
    own = lax.dynamic_index_in_dim(pair, chip, 0, keepdims=True)
    pieces = [own]
    for d in range(1, chips):
        block = lax.dynamic_index_in_dim(pair, chip ^ d, 0, keepdims=True)
        pieces.append(lax.ppermute(block, "fsdp", [(j, j ^ (2 * d)) for j in range(parts)]))
    return pieces


def exchanged(pieces):
    parts = lax.axis_size("fsdp")
    chip = lax.axis_index("fsdp") // 2
    out = jnp.zeros((parts // 2,) + pieces[0].shape[1:], pieces[0].dtype)
    for d, piece in enumerate(pieces):
        out = lax.dynamic_update_slice_in_dim(out, piece, chip ^ d, 0)
    return out


def columns_kernel(blocks, place_ref, gate_ref, up_ref, out_ref):
    j = pl.program_id(0)

    @pl.when(place_ref[blocks + j] == 0)
    def _():
        out_ref[...] = gate_ref[...]

    @pl.when(place_ref[blocks + j] == 1)
    def _():
        out_ref[...] = up_ref[...]


def columns_for(w_gate, w_up, picks, width):
    rows = w_gate.shape[0]
    blocks = len(picks)
    if width % 128:
        both = jnp.stack([w_gate.reshape(rows, -1, width), w_up.reshape(rows, -1, width)])
        return jnp.concatenate([both[which, :, at] for at, which in picks], axis=1)
    place = jnp.stack([jnp.asarray(x, jnp.int32) for x in [p[0] for p in picks] + [p[1] for p in picks]])
    source = lambda own: pl.BlockSpec(
        (rows, width), lambda j, place: (0, jnp.where(place[blocks + j] == own, place[j], place[0]))
    )
    return pl.pallas_call(
        functools.partial(columns_kernel, blocks),
        grid_spec=pltpu.PrefetchScalarGridSpec(
            num_scalar_prefetch=1,
            grid=(blocks,),
            in_specs=[source(0), source(1)],
            out_specs=pl.BlockSpec((rows, width), lambda j, place: (0, j)),
        ),
        out_shape=jax.ShapeDtypeStruct((rows, blocks * width), w_gate.dtype),
        cost_estimate=work(blocks),
        name="columns_for",
    )(place, w_gate, w_up)


def weave_kernel(count, chips, width, place_ref, *refs):
    out_ref = refs[-1]
    j = pl.program_id(0)
    half = 2 * width
    for d in range(chips):
        for c in range(2):
            mine, other = refs[2 * (c * chips + d):2 * (c * chips + d) + 2]
            for odd in range(2):
                @pl.when((j == 2 * d + c) & (place_ref[count] == odd))
                def _(mine=mine, other=other, c=c, odd=odd):
                    for which, ref in ((odd, mine), (1 - odd, other)):
                        for k in range(2):
                            at = which * half + k * width
                            from_lane = (k ^ c) * width
                            out_ref[:, at:at + width] = ref[:, from_lane:from_lane + width]


def weave(mine, other, places, odd, width):
    rows = mine[0].shape[0]
    count = len(mine)
    chips = count // 2
    tile = next(t for t in (160, 64, 32, 16) if rows % t == 0)
    tiles = rows // tile
    specs, arrays = [], []
    for c in range(2):
        for d in range(chips):
            index = lambda j, t, place, k=2 * d + c: (jnp.where(j == k, t, 0), 0)
            specs += [pl.BlockSpec((tile, 2 * width), index)] * 2
            arrays += [mine[c * chips + d], other[c * chips + d]]
    return pl.pallas_call(
        functools.partial(weave_kernel, count, chips, width),
        grid_spec=pltpu.PrefetchScalarGridSpec(
            num_scalar_prefetch=1,
            grid=(count, tiles),
            in_specs=specs,
            out_specs=pl.BlockSpec((tile, 4 * width), lambda j, t, place: (place[j] * tiles + t, 0)),
        ),
        out_shape=jax.ShapeDtypeStruct((count * rows, 4 * width), mine[0].dtype),
        compiler_params=pltpu.CompilerParams(vmem_limit_bytes=56 << 20),
        cost_estimate=work(21),
        name="weave",
    )(jnp.stack([jnp.asarray(x, jnp.int32) for x in places + [odd]]), *arrays)


class Reshard:
    def __init__(self, w_gate, w_up):
        parts = lax.axis_size("fsdp")
        me = lax.axis_index("fsdp")
        self.chips = parts // 2
        self.chip, self.core = me // 2, me % 2
        self.odd = lax.axis_index("sp") % 2
        self.width = w_gate.shape[1] // parts
        pair = lambda d, which: [(2 * (self.chip ^ d) + c, which) for c in (self.core, 1 - self.core)]
        self.local = columns_for(w_gate, w_up, pair(0, self.odd) + pair(0, 1 - self.odd), self.width)
        self.sent = [columns_for(w_gate, w_up, pair(d, self.odd), self.width) for d in range(1, self.chips)]

    def fetch(self):
        parts = 2 * self.chips
        half = 2 * self.width
        self.mine = [self.local[:, :half]] + [
            lax.ppermute(x, "fsdp", [(j, j ^ (2 * d)) for j in range(parts)]) for d, x in enumerate(self.sent, 1)
        ]
        pairs = [(k, k ^ 1) for k in range(lax.axis_size("sp"))]
        self.other = [self.local[:, half:]] + [lax.ppermute(x, "sp", pairs) for x in self.mine[1:]]
        return self.other[1:]

    def result(self, *before):
        mine = self.mine + [partner(x) for x in self.mine]
        other = self.other + [partner(x) for x in self.other]
        places = []
        for d in range(self.chips):
            places += [2 * (self.chip ^ d) + self.core, 2 * (self.chip ^ d) + 1 - self.core]
        return weave([tie(mine[0], *before)] + mine[1:], other, places, self.odd, self.width)


def features_kernel(count, width, core_ref, x_ref, mine_ref, other_ref):
    for c in range(2):
        @pl.when(core_ref[0] == c)
        def _(c=c):
            for q in range(count):
                at = slice(q * width, (q + 1) * width)
                mine_ref[:, at] = x_ref[:, (2 * q + c) * width:(2 * q + c + 1) * width]
                other_ref[:, at] = x_ref[:, (2 * q + 1 - c) * width:(2 * q + 2 - c) * width]


def features(x, core, width):
    rows = x.shape[0]
    count = x.shape[1] // (2 * width)
    tile = min(rows, 256)
    out = pl.BlockSpec((tile, count * width), lambda t, core: (t, 0))
    return pl.pallas_call(
        functools.partial(features_kernel, count, width),
        grid_spec=pltpu.PrefetchScalarGridSpec(
            num_scalar_prefetch=1,
            grid=(rows // tile,),
            in_specs=[pl.BlockSpec((tile, x.shape[1]), lambda t, core: (t, 0))],
            out_specs=[out, out],
        ),
        out_shape=[jax.ShapeDtypeStruct((rows, count * width), x.dtype)] * 2,
        cost_estimate=work(3),
        name="features",
    )(core.reshape(1).astype(jnp.int32), x)


def sum_tn_kernel(segments, pairs, *refs):
    lefts = [ref[...] for ref in refs[:pairs]]
    extra = refs[pairs + segments * pairs:-1]
    out_ref = refs[-1]
    width = out_ref.shape[-1] // segments
    for j in range(segments):
        rights = refs[pairs + j * pairs:pairs + (j + 1) * pairs]
        part = slice(j * width, (j + 1) * width)
        total = sum(tn(a, b[...]) for a, b in zip(lefts, rights))
        if len(out_ref.shape) == 2:
            for more in extra:
                total = total + more[:, part].astype(jnp.float32)
            out_ref[:, part] = total.astype(out_ref.dtype)
        else:
            slabs, blocks, rows, _ = out_ref.shape
            for s in range(slabs):
                for k in range(blocks):
                    at = (k * slabs + s) * rows
                    piece = total[at:at + rows]
                    for more in extra:
                        piece = piece + more[s, k, :, part].astype(jnp.float32)
                    out_ref[s, k, :, part] = piece.astype(out_ref.dtype)


def sum_tn(lefts, rights, half, *extra, weight=1, slabs=1, rows=1):
    segments, pairs = len(rights), len(lefts)
    tokens = lefts[0].shape[0]
    if segments == 1:
        width = lefts[0].shape[1] // 2
        if width % 128:
            total = sum(tn(a[:, half * width:(half + 1) * width], b) for a, b in zip(lefts, rights[0]))
            return sum((e.astype(jnp.float32) for e in extra), total).astype(jnp.bfloat16)
        shape = (width, D)
        block = (width, CHUNK)
        left = pl.BlockSpec((tokens, width), lambda i: (0, half))
        right = pl.BlockSpec((tokens, CHUNK), lambda i: (0, i))
        out = pl.BlockSpec(block, lambda i: (0, i))
    else:
        width = rights[0][0].shape[1] // 2
        if width % 128:
            cut = slice(half * width, (half + 1) * width)
            total = jnp.concatenate([sum(tn(a, b[:, cut]) for a, b in zip(lefts, r)) for r in rights], axis=1)
            total = jnp.moveaxis(total.reshape(-1, slabs, rows, segments * width), 1, 0)
            return sum((e.astype(jnp.float32) for e in extra), total).astype(jnp.bfloat16)
        blocks = CHUNK // (slabs * rows)
        shape = (slabs, D // (slabs * rows), rows, segments * width)
        left = pl.BlockSpec((tokens, CHUNK), lambda i: (0, i))
        right = pl.BlockSpec((tokens, width), lambda i: (0, half))
        out = pl.BlockSpec((slabs, blocks, rows, segments * width), lambda i: (0, i, 0, 0))
    return pl.pallas_call(
        functools.partial(sum_tn_kernel, segments, pairs),
        grid=(D // CHUNK,),
        in_specs=[left] * pairs + [right] * (segments * pairs) + [out] * len(extra),
        out_specs=out,
        out_shape=jax.ShapeDtypeStruct(shape, jnp.bfloat16),
        compiler_params=pltpu.CompilerParams(vmem_limit_bytes=56 << 20),
        cost_estimate=work((26 if segments == 2 else 16) * weight),
        name="sum_tn",
    )(*lefts, *[b for r in rights for b in r], *extra)


def ffn_kernel(n_ref, g_ref, wg_ref, wu_ref, wd_ref, hidden_ref, gate_grad_ref, up_grad_ref):
    gate = nn(n_ref[...], wg_ref[...])
    up = nn(n_ref[...], wu_ref[...])
    hidden_grad = nt(g_ref[...], wd_ref[...])
    sigm = 1.0 / (1.0 + jnp.exp(-gate))
    act = gate * sigm
    hidden_ref[...] = (act * up).astype(jnp.bfloat16)
    up_grad_ref[...] = (hidden_grad * act).astype(jnp.bfloat16)
    gate_grad_ref[...] = (hidden_grad * up * (sigm + act * (1.0 - sigm))).astype(jnp.bfloat16)


def feed_forward(n2, g, w_both, w_down):
    tokens, hidden = n2.shape[0], w_down.shape[0]
    tile = 256 if hidden % 256 == 0 else 128
    tiles = hidden // tile
    full = pl.BlockSpec((tokens, D), lambda j: (0, 0))
    out = pl.BlockSpec((tokens, tile), lambda j: (0, j))
    return pl.pallas_call(
        ffn_kernel,
        grid=(tiles,),
        in_specs=[full, full, pl.BlockSpec((D, tile), lambda j: (0, j)), pl.BlockSpec((D, tile), lambda j: (0, tiles + j)),
                  pl.BlockSpec((tile, D), lambda j: (j, 0))],
        out_specs=[out] * 3,
        out_shape=[jax.ShapeDtypeStruct((tokens, hidden), jnp.bfloat16)] * 3,
        compiler_params=pltpu.CompilerParams(vmem_limit_bytes=56 << 20),
        cost_estimate=work(36),
        name="feed_forward",
    )(n2, g, w_both, w_both, w_down)


def sum_nt_kernel(*refs):
    pairs = len(refs) // 2
    refs[-1][...] = sum(nt(refs[k][...], refs[pairs + k][...]) for k in range(pairs)).astype(jnp.bfloat16)


def sum_nt(lefts, right, weight=1):
    (tokens, depth), columns = lefts[0].shape, right.shape[0]
    tile, block = tokens // 2, columns // 2
    return pl.pallas_call(
        sum_nt_kernel,
        grid=(columns // block, tokens // tile),
        in_specs=[pl.BlockSpec((tile, depth), lambda j, i: (i, 0))] * len(lefts)
        + [pl.BlockSpec((block, depth), lambda j, i, k=k: (j, k)) for k in range(len(lefts))],
        out_specs=pl.BlockSpec((tile, block), lambda j, i: (i, j)),
        out_shape=jax.ShapeDtypeStruct((tokens, columns), jnp.bfloat16),
        compiler_params=pltpu.CompilerParams(vmem_limit_bytes=56 << 20),
        cost_estimate=work(26 * weight),
        name="sum_nt",
    )(*lefts, *([right] * len(lefts)))


def plain_nn_kernel(a_ref, b_ref, out_ref):
    out_ref[...] = nn(a_ref[...], b_ref[...]).astype(jnp.bfloat16)


def plain_nn(a, b, weight=1):
    (tokens, depth), columns = a.shape, b.shape[1]
    return pl.pallas_call(
        plain_nn_kernel,
        grid=(columns // CHUNK,),
        in_specs=[pl.BlockSpec((tokens, depth), lambda j: (0, 0)), pl.BlockSpec((depth, CHUNK), lambda j: (0, j))],
        out_specs=pl.BlockSpec((tokens, CHUNK), lambda j: (0, j)),
        out_shape=jax.ShapeDtypeStruct((tokens, columns), jnp.bfloat16),
        compiler_params=pltpu.CompilerParams(vmem_limit_bytes=56 << 20),
        cost_estimate=work(16 * weight),
        name="plain_nn",
    )(a, b)


class KeySum:
    def __init__(self, parts):
        self.parts = parts
        self.running = parts[-1]
        self.hops = 0

    def hop(self, *before):
        n = lax.axis_size("sp")
        s = self.hops
        if s:
            self.running = (self.parts[n - 1 - s].astype(jnp.float32) + self.running.astype(jnp.float32)).astype(jnp.bfloat16)
        pairs = [(n - 1 - k, n - 2 - k) for k in range(s + 1)]
        self.running = lax.ppermute(tie(self.running, *before), "sp", pairs)
        self.hops += 1
        return self.running

    def result(self):
        while self.hops < lax.axis_size("sp") - 1:
            self.hop()
        return self.parts[0], self.running


def rows_of(pieces):
    return jnp.concatenate(pieces, axis=0)


def body(tokens, doc_starts, cotangent, gain_attn, gain_ffn, w_query, w_key, w_value, w_out, w_gate, w_up, w_down):
    micro, _, rows, _ = tokens.shape
    parts = lax.axis_size("fsdp")
    chips = parts // 2
    core = lax.axis_index("fsdp") % 2
    seq = lax.axis_size("sp")
    place = lax.axis_index("sp")
    count = micro * rows
    d_own = w_query.shape[0]
    hidden_own = w_down.shape[0]
    hidden_chip = 2 * hidden_own
    bf16 = jnp.bfloat16
    f32 = jnp.float32

    gains = jnp.pad(jnp.stack([gain_attn, gain_ffn], axis=1), ((0, 0), (0, 126)))
    w_in = jnp.concatenate(
        [w_query, w_key[:, :KW], w_value[:, :KW], w_key[:, KW:], w_value[:, KW:], gains], axis=1
    )
    w_in = lax.all_gather(w_in, "fsdp", axis=0, tiled=True)
    w_out_full = lax.all_gather(w_out, "fsdp", axis=0, tiled=True)
    gain_one = w_in[:, D + 4 * KW].astype(f32)
    gain_two = w_in[:, D + 4 * KW + 1].astype(f32)
    reshard = Reshard(w_gate, w_up)
    came_columns = reshard.fetch()

    starts = doc_starts.reshape(micro, -1)
    offsets = (place - jnp.arange(seq, dtype=jnp.int32)) * rows
    key_places = (offsets[:, None] + jnp.arange(rows, dtype=jnp.int32)[None, :]).reshape(-1)
    docs, positions = stream_layout(starts, key_places)
    docs = docs.reshape(micro, seq, rows)
    key_places = key_places.reshape(seq, rows)
    tables = rope_lanes(positions.reshape(micro, seq, rows)[:, 0].reshape(count))
    allowed = (docs[:, :1, :, None] == docs[:, :, None, :]) & (
        key_places[None, :, None, :] <= key_places[None, :1, :, None]
    )
    bias = jnp.where(allowed, 0.0, -1e30).astype(f32)
    bias_t = jnp.where(jnp.swapaxes(allowed, 2, 3), 0.0, -1e30).astype(f32)

    inputs = tokens.reshape(count, D).astype(f32)
    scale_one = rms_scale(inputs)
    normed_x1 = inputs * scale_one
    normed = tie((normed_x1 * gain_one).astype(bf16), *tables, bias, bias_t)
    normed = tie(normed, *came_columns)
    w_down_other = partner(w_down)
    order = Order()
    qkv = order.did(project(normed, w_in, tables))

    g_low = cotangent.reshape(micro, rows, D)
    g_all = [gather_chips(tie(g_low[0], qkv))]
    state, n2_alls = [], []
    for m in range(micro):
        kv = [qkv[m * rows:(m + 1) * rows, D:]]
        for s in range(seq - 1):
            kv.append(lax.ppermute(kv[-1], "sp", right_pairs(seq, s)))
        context, lse = attend(order.at(qkv), kv, bias[m], m)
        lse_rows = jnp.swapaxes(lse.reshape(rows, HALVES, 128)[:, :, :QW // HEAD_DIM].reshape(rows, HEADS), 0, 1)
        mixed = inputs[m * rows:(m + 1) * rows] + nn(context, w_out_full)
        scale_two = rms_scale(mixed)
        normed_x2 = mixed * scale_two
        normed_ffn = order.did((normed_x2 * gain_two).astype(bf16))
        if m == 0:
            normed_ffn = tie(normed_ffn, g_all[0])
        n2_alls.append(gather_chips(normed_ffn))
        if m:
            g_all.append(gather_chips(tie(g_low[m], normed_ffn)))
        state.append((kv, context, lse_rows, mixed, scale_two, normed_x2))
    w_both = order.did(reshard.result(*order.last))
    w_down_chip = order.did(rows_of([order.at(w_down), w_down_other]))

    hiddens, gate_grads, up_grads, normed_grads, out_terms = [], [], [], [], []

    def forward_back(m):
        hidden, gate_grad, up_grad = feed_forward(order.at(n2_alls[m]), g_all[m], w_both, w_down_chip)
        hiddens.append(hidden)
        gate_grads.append(gate_grad)
        up_grads.append(order.did(up_grad))

    def normed_part(m, *before):
        part = order.did(sum_nt([order.at(gate_grads[m], *before), up_grads[m]], w_both))
        normed_grads.append(scatter_chips(part))

    def out_part(m, *before):
        part = order.did(plain_nn(order.at(hiddens[m], *before), w_down_chip))
        out_terms.append(scatter_chips(part))

    slab = d_own // seq
    ff = parts * hidden_own
    forward_back(0)
    normed_part(0, g_all[-1])
    for m in range(1, micro):
        forward_back(m)
    wide = dict(slabs=seq, rows=slab)
    wide_other = order.did(sum_tn(n2_alls, [[order.at(gate_grads[0])] + gate_grads[1:], up_grads], 1, **wide))
    wide_came = partner(wide_other)
    down_other = order.did(sum_tn([order.at(hiddens[0])] + hiddens[1:], [g_all], 1))
    down_came = partner(down_other)
    wide_grad = order.did(sum_tn(n2_alls, [[order.at(gate_grads[0])] + gate_grads[1:], up_grads], 0, wide_came, **wide))
    wide_mine = lax.psum_scatter(wide_grad, "sp", scatter_dimension=0, tiled=False)
    down_grad = order.did(sum_tn([order.at(hiddens[0])] + hiddens[1:], [g_all], 0, down_came))
    down_total = lax.psum(down_grad, "sp")
    normed_part(1)
    for m in range(micro):
        out_part(m)
    normed_mine, normed_other = features(order.at(normed), core, d_own)
    normed_chip = rows_of([normed_mine, partner(normed_other)])
    context_mine, context_other = features(rows_of([state[m][1] for m in range(micro)]), core, d_own)
    context_chip = rows_of([context_mine, partner(context_other)])
    order.did(normed_mine)

    mixed_grads, attn_grads, query_grads, kv_sums = [], [], [], []
    gain_two_term = 0.0
    chip_rows = lambda pieces: rows_of(pieces + [partner(p) for p in pieces])
    for m in range(micro):
        kv, context, lse_rows, mixed, scale_two, normed_x2 = state[m]
        if m == micro - 1:
            order.last = order.last + (wide_mine,)
            pieces = exchange_chips(exchange(wide_mine))
        normed_grad = added((order.at(normed_grads[m][0]), normed_grads[m][1]))
        gain_two_term = gain_two_term + jnp.sum(normed_grad * normed_x2, axis=0)
        mixed_grad = norm_back(normed_grad, gain_two, normed_x2, scale_two, g_low[m].astype(f32))
        attn_grad = mixed_grad.astype(bf16)
        attn_grads.append(attn_grad)
        mixed_grads.append(mixed_grad)
        context_grad = order.did(nt(attn_grad, w_out_full).astype(bf16))
        if m == micro - 1:
            out_half = order.did(tn(context_chip, chip_rows(attn_grads)).astype(bf16))
            out_shard = added(scatter_chips(out_half)).astype(bf16)
        args = (context, lse_rows, kv, bias_t[m], tables, m)
        first = attend_back(qkv, order.at(context_grad), *args, 0)
        order.last = ()
        if m == micro - 1:
            order.last = tuple(pieces)
        second = attend_back(qkv, order.at(context_grad), *args, 1, first)
        query_grads.append(order.did(second[0]))
        kv_sums.append(KeySum(second[1:]))
        kv_sums[-1].hop()

    order.last = order.last + (out_shard, down_total)
    wide_part = exchanged([order.at(pieces[0], *pieces[1:])] + pieces[1:])
    wide_part = order.did(jnp.moveaxis(wide_part.reshape(parts, slab, 2, hidden_own), 0, 2).reshape(slab, 2 * ff))
    query_half = order.did(tn(normed_chip, chip_rows(query_grads[:-1] + [order.at(query_grads[-1])])).astype(bf16))
    query_shard = added(scatter_chips(query_half)).astype(bf16)
    kv_hop = tuple(keys.hop() for keys in kv_sums)
    normed_grad = order.did(nt(order.at(rows_of(query_grads), *kv_hop), w_in[:, :D]))
    kv_grads = [keys.result() for keys in kv_sums]
    kv_grads = [order.did(finish_keys(own, order.at(came), tables, m)) for m, (own, came) in enumerate(kv_grads)]
    wide_total = lax.all_gather(order.at(wide_part), "sp", axis=0, tiled=True)
    kv_grad = rows_of(kv_grads)
    kv_half = order.did(tn(normed_chip, chip_rows(kv_grads)).astype(bf16))
    normed_grad = normed_grad + nt(kv_grad, w_in[:, D:D + 4 * KW])
    gain_one_term = jnp.sum(normed_grad * normed_x1, axis=0)
    input_grad = norm_back(normed_grad, gain_one, normed_x1, scale_one, rows_of(mixed_grads)).astype(bf16)

    gain_blocks = jnp.stack([gain_one_term, gain_two_term], axis=1).astype(bf16).reshape(chips, 2, d_own, 2)
    gain_lanes = jnp.concatenate(
        [lax.dynamic_index_in_dim(gain_blocks, c, 1, keepdims=False) for c in (core, 1 - core)], axis=2
    ).reshape(chips * d_own, 4)
    kv_shard = added(scatter_chips(jnp.concatenate([kv_half, jnp.pad(gain_lanes, ((0, 0), (0, 124)))], axis=1))).astype(bf16)
    out_total, query_total, kv_total = lax.psum(
        (tie(out_shard, down_total), tie(query_shard, wide_total), tie(kv_shard, wide_total)), "sp"
    )
    query_total, kv_total = query_total.astype(f32), kv_total.astype(f32)
    kv_piece = lambda k: kv_total[:, k * KW:(k + 1) * KW]
    gain_lanes = kv_total[:, 4 * KW:4 * KW + 4]
    gain_total = gain_lanes[:, :2] + partner(gain_lanes)[:, 2:]
    outputs = [(state[m][3] + added((order.at(out_terms[m][0]), out_terms[m][1]))).astype(bf16) for m in range(micro)]
    return (
        rows_of(outputs).reshape(tokens.shape),
        input_grad.reshape(tokens.shape),
        gain_total[:, 0],
        gain_total[:, 1],
        query_total,
        jnp.concatenate([kv_piece(0), kv_piece(2)], axis=1),
        jnp.concatenate([kv_piece(1), kv_piece(3)], axis=1),
        out_total.astype(f32),
        wide_total[:, :ff].astype(f32),
        wide_total[:, ff:].astype(f32),
        down_total.astype(f32),
    )


def solution(mesh):
    split = P("fsdp", None)
    stream = P(None, "fsdp", "sp", None)
    return jax.shard_map(
        body,
        mesh=mesh,
        in_specs=(stream, P(None, "fsdp", None), stream, P("fsdp"), P("fsdp")) + (split,) * 7,
        out_specs=(stream, stream, P("fsdp"), P("fsdp")) + (split,) * 7,
        check_vma=False,
    )
```

```python
import functools, math
import jax, jax.numpy as jnp
from jax import lax
from jax.experimental import pallas as pl
from jax.experimental.pallas import tpu as pltpu
from jax.sharding import PartitionSpec as P

D = 2560
HEADS = 32
KV_HEADS = 8
HEAD_DIM = 80
GROUP = HEADS // KV_HEADS
HALVES = 2
SCALE = HEAD_DIM ** -0.5
LOG2E = 1.0 / math.log(2.0)
QW = D // HALVES
KW = KV_HEADS * HEAD_DIM // HALVES
CHUNK = 640
SPEED = 1 << 28


def work(micros):
    return pl.CostEstimate(flops=micros * SPEED, bytes_accessed=1 << 16, transcendentals=0)


def nt(left, right):
    return lax.dot_general(left, right, (((1,), (1,)), ((), ())), preferred_element_type=jnp.float32)


def tn(left, right):
    return lax.dot_general(left, right, (((0,), (0,)), ((), ())), preferred_element_type=jnp.float32)


def nn(left, right):
    return jnp.dot(left, right, preferred_element_type=jnp.float32)


def head(h):
    return slice(h * HEAD_DIM, (h + 1) * HEAD_DIM)


def spin(x, cosine, sine_up, sine_down):
    half = HEAD_DIM // 2
    width = x.shape[1]
    return x * cosine + pltpu.roll(x, width - half, 1) * sine_up + pltpu.roll(x, half, 1) * sine_down


def project_kernel(n_ref, w_ref, cos_ref, up_ref, down_ref, out_ref):
    j = pl.program_id(0)
    x = nn(n_ref[...], w_ref[...])
    turned = spin(x, cos_ref[...], up_ref[...], down_ref[...])
    lane = lax.broadcasted_iota(jnp.int32, x.shape, 1)
    keep = (j < D // CHUNK) | (lane < KW)
    out_ref[...] = jnp.where(keep, turned, x).astype(jnp.bfloat16)


def project(normed, weights, tables):
    rows = normed.shape[0]
    chunks = (D + 4 * KW) // CHUNK
    table = pl.BlockSpec((rows, CHUNK), lambda j: (0, 0))
    return pl.pallas_call(
        project_kernel,
        grid=(chunks,),
        in_specs=[pl.BlockSpec((rows, D), lambda j: (0, 0)), pl.BlockSpec((D, CHUNK), lambda j: (0, j)), table, table, table],
        out_specs=pl.BlockSpec((rows, CHUNK), lambda j: (0, j)),
        out_shape=jax.ShapeDtypeStruct((rows, chunks * CHUNK), jnp.bfloat16),
        compiler_params=pltpu.CompilerParams(vmem_limit_bytes=48 << 20),
        cost_estimate=work(19),
        name="project",
    )(normed, weights, *tables)


def forward_kernel(blocks, q_ref, *refs):
    kv_refs = refs[:blocks]
    bias_ref, ctx_ref, lse_ref = refs[blocks:]
    rows = q_ref.shape[0]
    bias = [bias_ref[s] for s in range(blocks)]
    lane = lax.broadcasted_iota(jnp.int32, (rows, 128), 1)
    lse_all = jnp.zeros((rows, 128), jnp.float32)
    for h in range(QW // HEAD_DIM):
        c = h // GROUP
        q = q_ref[:, head(h)]
        scores = [nt(q, kv_refs[s][:, head(c)]) * (SCALE * LOG2E) + bias_ref[s] for s in range(blocks)]
        top = functools.reduce(jnp.maximum, scores).max(axis=1, keepdims=True)
        probs = [jnp.exp2(x - top) for x in scores]
        total = functools.reduce(jnp.add, probs).sum(axis=1, keepdims=True)
        ctx = functools.reduce(jnp.add, [nn(p.astype(jnp.bfloat16), kv_refs[s][:, KW + c * HEAD_DIM:KW + (c + 1) * HEAD_DIM]) for s, p in enumerate(probs)])
        ctx_ref[:, head(h)] = (ctx / total).astype(jnp.bfloat16)
        lse_all = jnp.where(lane == h, top + jnp.log2(total), lse_all)
    lse_ref[...] = lse_all


def attend(qkv, kv_blocks, bias, at):
    rows = kv_blocks[0].shape[0]
    blocks = len(kv_blocks)
    kv_spec = pl.BlockSpec((rows, 2 * KW), lambda h: (0, h))
    return pl.pallas_call(
        functools.partial(forward_kernel, blocks),
        grid=(HALVES,),
        in_specs=[pl.BlockSpec((rows, QW), lambda h: (at, h))] + [kv_spec] * blocks + [pl.BlockSpec((blocks, rows, rows), lambda h: (0, 0, 0))],
        out_specs=[pl.BlockSpec((rows, QW), lambda h: (0, h)), pl.BlockSpec((rows, 128), lambda h: (0, h))],
        out_shape=[jax.ShapeDtypeStruct((rows, D), jnp.bfloat16), jax.ShapeDtypeStruct((rows, HALVES * 128), jnp.float32)],
        compiler_params=pltpu.CompilerParams(vmem_limit_bytes=48 << 20),
        cost_estimate=work(23),
        name="attend",
    )(qkv, *kv_blocks, bias)


def backward_kernel(blocks, skipped, q_ref, dctx_ref, ctx_ref, lse_ref, *refs):
    kv_refs = refs[:blocks]
    bias_ref, cos_ref, up_ref, down_ref = refs[blocks:blocks + 4]
    dq_ref = refs[blocks + 4 + skipped]
    dkv_refs = refs[blocks + 5 + skipped:2 * blocks + 5 + skipped]
    dq_acc = refs[-1]
    rows = q_ref.shape[0]
    count = QW // HEAD_DIM
    owner = lax.broadcasted_iota(jnp.int32, (count, QW), 0)
    lane = lax.broadcasted_iota(jnp.int32, (count, QW), 1)
    pick = ((lane >= owner * HEAD_DIM) & (lane < owner * HEAD_DIM + HEAD_DIM)).astype(jnp.float32)
    product = dctx_ref[...].astype(jnp.float32) * ctx_ref[...].astype(jnp.float32)
    delta = lax.dot_general(pick, product, (((1,), (1,)), ((), ())), precision=lax.Precision.HIGHEST, preferred_element_type=jnp.float32)
    for c in range(KV_HEADS // HALVES):
        heads = range(c * GROUP, (c + 1) * GROUP)
        qs = [q_ref[:, head(h)] for h in heads]
        ds = [dctx_ref[:, head(h)] for h in heads]
        q_stack = jnp.concatenate(qs, axis=0)
        d_stack = jnp.concatenate(ds, axis=0)
        dq = [None] * GROUP
        for s in range(blocks):
            k = kv_refs[s][:, head(c)]
            v = kv_refs[s][:, KW + c * HEAD_DIM:KW + (c + 1) * HEAD_DIM]
            ps, dss = [], []
            for g, h in enumerate(heads):
                score = nt(k, qs[g]) * (SCALE * LOG2E) + bias_ref[s]
                p = jnp.exp2(score - lse_ref[h:h + 1, :])
                dp = nt(v, ds[g])
                d = (p * (dp - delta[h:h + 1, :])).astype(jnp.bfloat16)
                ps.append(p.astype(jnp.bfloat16))
                dss.append(d)
                term = tn(d, k)
                dq[g] = term if dq[g] is None else dq[g] + term
            dkv_refs[s][:, head(c)] = (nn(jnp.concatenate(dss, axis=1), q_stack) * SCALE).astype(jnp.bfloat16)
            dkv_refs[s][:, KW + c * HEAD_DIM:KW + (c + 1) * HEAD_DIM] = nn(jnp.concatenate(ps, axis=1), d_stack).astype(jnp.bfloat16)
        for g, h in enumerate(heads):
            dq_acc[:, head(h)] = dq[g] * SCALE
    for j in range(QW // CHUNK):
        part = slice(j * CHUNK, (j + 1) * CHUNK)
        dq_ref[:, part] = spin(dq_acc[:, part], cos_ref[...], -up_ref[...], -down_ref[...]).astype(jnp.bfloat16)


def attend_back(qkv, dctx, ctx, lse_rows, kv_blocks, bias_t, tables, at, half, before=None):
    rows = kv_blocks[0].shape[0]
    blocks = len(kv_blocks)
    count = QW // HEAD_DIM
    lanes = pl.BlockSpec((rows, QW), lambda h: (0, half))
    kv_spec = pl.BlockSpec((rows, 2 * KW), lambda h: (0, half))
    table = pl.BlockSpec((rows, CHUNK), lambda h: (at, 0))
    before = [] if before is None else list(before)
    inputs = 4 + blocks + 4
    outs = pl.pallas_call(
        functools.partial(backward_kernel, blocks, len(before)),
        grid=(1,),
        in_specs=[pl.BlockSpec((rows, QW), lambda h: (at, half)), lanes, lanes, pl.BlockSpec((count, rows), lambda h: (half, 0))]
        + [kv_spec] * blocks + [pl.BlockSpec((blocks, rows, rows), lambda h: (0, 0, 0)), table, table, table]
        + [pl.BlockSpec(memory_space=pl.ANY)] * len(before),
        out_specs=[lanes] + [kv_spec] * blocks,
        out_shape=[jax.ShapeDtypeStruct((rows, D), jnp.bfloat16)] + [jax.ShapeDtypeStruct((rows, 4 * KW), jnp.bfloat16)] * blocks,
        scratch_shapes=[pltpu.VMEM((rows, QW), jnp.float32)],
        input_output_aliases={inputs + k: k for k in range(len(before))},
        compiler_params=pltpu.CompilerParams(vmem_limit_bytes=48 << 20),
        cost_estimate=work(100),
        name="attend_back",
    )(qkv, dctx, ctx, lse_rows, *kv_blocks, bias_t, *tables, *before)
    return outs


RMS_EPS = 1e-05
ROPE_BASE = 1000000.0


def finish_kernel(own_ref, other_ref, cos_ref, up_ref, down_ref, out_ref):
    x = own_ref[...].astype(jnp.float32) + other_ref[...].astype(jnp.float32)
    turned = spin(x, cos_ref[...], -up_ref[...], -down_ref[...])
    lane = lax.broadcasted_iota(jnp.int32, x.shape, 1)
    out_ref[...] = jnp.where(lane < KW, turned, x).astype(jnp.bfloat16)


def finish_keys(own, other, tables, at):
    rows = own.shape[0]
    half = pl.BlockSpec((rows, 2 * KW), lambda h: (0, h))
    table = pl.BlockSpec((rows, CHUNK), lambda h: (at, 0))
    return pl.pallas_call(
        finish_kernel,
        grid=(HALVES,),
        in_specs=[half, half, table, table, table],
        out_specs=half,
        out_shape=jax.ShapeDtypeStruct(own.shape, jnp.bfloat16),
        cost_estimate=work(2),
        name="finish_keys",
    )(own, other, *tables)


def rms_scale(values):
    return lax.rsqrt(jnp.mean(values * values, axis=-1, keepdims=True) + RMS_EPS)


def norm_back(grad_normed, gain, normed_x, scale_row, grad_rest):
    scaled = grad_normed * gain
    inner = jnp.mean(scaled * normed_x, axis=-1, keepdims=True)
    return grad_rest + scale_row * (scaled - normed_x * inner)


def rope_lanes(position):
    lane = jnp.arange(CHUNK, dtype=jnp.int32) % HEAD_DIM
    half = HEAD_DIM // 2
    index = (lane % half).astype(jnp.float32)
    inverse = jnp.exp(index * (-2.0 * math.log(ROPE_BASE) / HEAD_DIM))
    angles = position.astype(jnp.float32)[:, None] * inverse[None, :]
    sine = jnp.sin(angles)
    first = (lane < half)[None, :]
    return jnp.cos(angles), jnp.where(first, -sine, 0.0), jnp.where(first, 0.0, sine)


def stream_layout(starts, places):
    begun = starts[:, None, :] <= places[None, :, None]
    doc_ids = jnp.sum(begun.astype(jnp.int32), axis=-1) - 1
    first_token = jnp.max(jnp.where(begun, starts[:, None, :], 0), axis=-1)
    return doc_ids, places[None, :] - first_token


def right_pairs(count, lowest=0):
    return [(k, k + 1) for k in range(lowest, count - 1)]


def left_pairs(count):
    return [(k + 1, k) for k in range(count - 1)]


def tie(x, *before):
    return lax.optimization_barrier((x,) + before)[0]


class Order:
    def __init__(self):
        self.last = ()

    def at(self, x, *more):
        return tie(x, *self.last, *more)

    def did(self, y):
        self.last = (y,)
        return y


def partner(x):
    return lax.ppermute(x, "fsdp", [(j, j ^ 1) for j in range(lax.axis_size("fsdp"))])


def same_core():
    parts = lax.axis_size("fsdp")
    return [list(range(c, parts, 2)) for c in range(2)]


def gather_chips(x):
    return lax.all_gather(x, "fsdp", axis=0, tiled=True, axis_index_groups=same_core())


def scatter_chips(x, *before):
    parts = lax.axis_size("fsdp")
    chips, chip = parts // 2, lax.axis_index("fsdp") // 2
    blocks = x.reshape((chips, x.shape[0] // chips) + x.shape[1:])
    take = lambda q: lax.dynamic_index_in_dim(blocks, q, 0, keepdims=False)
    came = [lax.ppermute(take(chip ^ d), "fsdp", [(j, j ^ (2 * d)) for j in range(parts)]) for d in range(1, chips)]
    return take(chip), came


def added(pieces):
    own, came = pieces
    return sum((c.astype(jnp.float32) for c in came), own.astype(jnp.float32))


def exchange(blocks):
    parts = lax.axis_size("fsdp")
    me = lax.axis_index("fsdp")
    chips, core = parts // 2, me % 2
    shape = blocks.shape[1:]
    blocks = blocks.reshape((chips, 2) + shape)
    mine = lax.dynamic_index_in_dim(blocks, core, 1, keepdims=False)
    came = partner(lax.dynamic_index_in_dim(blocks, 1 - core, 1, keepdims=False))
    return jnp.where(core == 0, jnp.stack([mine, came], axis=1), jnp.stack([came, mine], axis=1))


def exchange_chips(pair):
    parts = lax.axis_size("fsdp")
    chips, chip = parts // 2, lax.axis_index("fsdp") // 2
    own = lax.dynamic_index_in_dim(pair, chip, 0, keepdims=True)
    pieces = [own]
    for d in range(1, chips):
        block = lax.dynamic_index_in_dim(pair, chip ^ d, 0, keepdims=True)
        pieces.append(lax.ppermute(block, "fsdp", [(j, j ^ (2 * d)) for j in range(parts)]))
    return pieces


def exchanged(pieces):
    parts = lax.axis_size("fsdp")
    chip = lax.axis_index("fsdp") // 2
    out = jnp.zeros((parts // 2,) + pieces[0].shape[1:], pieces[0].dtype)
    for d, piece in enumerate(pieces):
        out = lax.dynamic_update_slice_in_dim(out, piece, chip ^ d, 0)
    return out


def columns_kernel(blocks, place_ref, gate_ref, up_ref, out_ref):
    j = pl.program_id(0)

    @pl.when(place_ref[blocks + j] == 0)
    def _():
        out_ref[...] = gate_ref[...]

    @pl.when(place_ref[blocks + j] == 1)
    def _():
        out_ref[...] = up_ref[...]


def columns_for(w_gate, w_up, picks, width):
    rows = w_gate.shape[0]
    blocks = len(picks)
    if width % 128:
        both = jnp.stack([w_gate.reshape(rows, -1, width), w_up.reshape(rows, -1, width)])
        return jnp.concatenate([both[which, :, at] for at, which in picks], axis=1)
    place = jnp.stack([jnp.asarray(x, jnp.int32) for x in [p[0] for p in picks] + [p[1] for p in picks]])
    source = lambda own: pl.BlockSpec(
        (rows, width), lambda j, place: (0, jnp.where(place[blocks + j] == own, place[j], place[0]))
    )
    return pl.pallas_call(
        functools.partial(columns_kernel, blocks),
        grid_spec=pltpu.PrefetchScalarGridSpec(
            num_scalar_prefetch=1,
            grid=(blocks,),
            in_specs=[source(0), source(1)],
            out_specs=pl.BlockSpec((rows, width), lambda j, place: (0, j)),
        ),
        out_shape=jax.ShapeDtypeStruct((rows, blocks * width), w_gate.dtype),
        cost_estimate=work(blocks),
        name="columns_for",
    )(place, w_gate, w_up)


def weave_kernel(count, chips, width, place_ref, *refs):
    out_ref = refs[-1]
    j = pl.program_id(0)
    half = 2 * width
    for d in range(chips):
        for c in range(2):
            mine, other = refs[2 * (c * chips + d):2 * (c * chips + d) + 2]
            for odd in range(2):
                @pl.when((j == 2 * d + c) & (place_ref[count] == odd))
                def _(mine=mine, other=other, c=c, odd=odd):
                    for which, ref in ((odd, mine), (1 - odd, other)):
                        for k in range(2):
                            at = which * half + k * width
                            from_lane = (k ^ c) * width
                            out_ref[:, at:at + width] = ref[:, from_lane:from_lane + width]


def weave(mine, other, places, odd, width):
    rows = mine[0].shape[0]
    count = len(mine)
    chips = count // 2
    tile = next(t for t in (160, 64, 32, 16) if rows % t == 0)
    tiles = rows // tile
    specs, arrays = [], []
    for c in range(2):
        for d in range(chips):
            index = lambda j, t, place, k=2 * d + c: (jnp.where(j == k, t, 0), 0)
            specs += [pl.BlockSpec((tile, 2 * width), index)] * 2
            arrays += [mine[c * chips + d], other[c * chips + d]]
    return pl.pallas_call(
        functools.partial(weave_kernel, count, chips, width),
        grid_spec=pltpu.PrefetchScalarGridSpec(
            num_scalar_prefetch=1,
            grid=(count, tiles),
            in_specs=specs,
            out_specs=pl.BlockSpec((tile, 4 * width), lambda j, t, place: (place[j] * tiles + t, 0)),
        ),
        out_shape=jax.ShapeDtypeStruct((count * rows, 4 * width), mine[0].dtype),
        compiler_params=pltpu.CompilerParams(vmem_limit_bytes=56 << 20),
        cost_estimate=work(21),
        name="weave",
    )(jnp.stack([jnp.asarray(x, jnp.int32) for x in places + [odd]]), *arrays)


class Reshard:
    def __init__(self, w_gate, w_up):
        parts = lax.axis_size("fsdp")
        me = lax.axis_index("fsdp")
        self.chips = parts // 2
        self.chip, self.core = me // 2, me % 2
        self.odd = lax.axis_index("sp") % 2
        self.width = w_gate.shape[1] // parts
        pair = lambda d, which: [(2 * (self.chip ^ d) + c, which) for c in (self.core, 1 - self.core)]
        self.local = columns_for(w_gate, w_up, pair(0, self.odd) + pair(0, 1 - self.odd), self.width)
        self.sent = [columns_for(w_gate, w_up, pair(d, self.odd), self.width) for d in range(1, self.chips)]

    def fetch(self):
        parts = 2 * self.chips
        half = 2 * self.width
        self.mine = [self.local[:, :half]] + [
            lax.ppermute(x, "fsdp", [(j, j ^ (2 * d)) for j in range(parts)]) for d, x in enumerate(self.sent, 1)
        ]
        pairs = [(k, k ^ 1) for k in range(lax.axis_size("sp"))]
        self.other = [self.local[:, half:]] + [lax.ppermute(x, "sp", pairs) for x in self.mine[1:]]
        return self.other[1:]

    def result(self, *before):
        mine = self.mine + [partner(x) for x in self.mine]
        other = self.other + [partner(x) for x in self.other]
        places = []
        for d in range(self.chips):
            places += [2 * (self.chip ^ d) + self.core, 2 * (self.chip ^ d) + 1 - self.core]
        return weave([tie(mine[0], *before)] + mine[1:], other, places, self.odd, self.width)


def features_kernel(count, width, core_ref, x_ref, mine_ref, other_ref):
    for c in range(2):
        @pl.when(core_ref[0] == c)
        def _(c=c):
            for q in range(count):
                at = slice(q * width, (q + 1) * width)
                mine_ref[:, at] = x_ref[:, (2 * q + c) * width:(2 * q + c + 1) * width]
                other_ref[:, at] = x_ref[:, (2 * q + 1 - c) * width:(2 * q + 2 - c) * width]


def features(x, core, width):
    rows = x.shape[0]
    count = x.shape[1] // (2 * width)
    tile = min(rows, 256)
    out = pl.BlockSpec((tile, count * width), lambda t, core: (t, 0))
    return pl.pallas_call(
        functools.partial(features_kernel, count, width),
        grid_spec=pltpu.PrefetchScalarGridSpec(
            num_scalar_prefetch=1,
            grid=(rows // tile,),
            in_specs=[pl.BlockSpec((tile, x.shape[1]), lambda t, core: (t, 0))],
            out_specs=[out, out],
        ),
        out_shape=[jax.ShapeDtypeStruct((rows, count * width), x.dtype)] * 2,
        cost_estimate=work(3),
        name="features",
    )(core.reshape(1).astype(jnp.int32), x)


def sum_tn_kernel(segments, pairs, *refs):
    lefts = [ref[...] for ref in refs[:pairs]]
    extra = refs[pairs + segments * pairs:-1]
    out_ref = refs[-1]
    width = out_ref.shape[-1] // segments
    for j in range(segments):
        rights = refs[pairs + j * pairs:pairs + (j + 1) * pairs]
        part = slice(j * width, (j + 1) * width)
        total = sum(tn(a, b[...]) for a, b in zip(lefts, rights))
        if len(out_ref.shape) == 2:
            for more in extra:
                total = total + more[:, part].astype(jnp.float32)
            out_ref[:, part] = total.astype(out_ref.dtype)
        else:
            slabs, blocks, rows, _ = out_ref.shape
            for s in range(slabs):
                for k in range(blocks):
                    at = (k * slabs + s) * rows
                    piece = total[at:at + rows]
                    for more in extra:
                        piece = piece + more[s, k, :, part].astype(jnp.float32)
                    out_ref[s, k, :, part] = piece.astype(out_ref.dtype)


def sum_tn(lefts, rights, half, *extra, weight=1, slabs=1, rows=1):
    segments, pairs = len(rights), len(lefts)
    tokens = lefts[0].shape[0]
    if segments == 1:
        width = lefts[0].shape[1] // 2
        if width % 128:
            total = sum(tn(a[:, half * width:(half + 1) * width], b) for a, b in zip(lefts, rights[0]))
            return sum((e.astype(jnp.float32) for e in extra), total).astype(jnp.bfloat16)
        shape = (width, D)
        block = (width, CHUNK)
        left = pl.BlockSpec((tokens, width), lambda i: (0, half))
        right = pl.BlockSpec((tokens, CHUNK), lambda i: (0, i))
        out = pl.BlockSpec(block, lambda i: (0, i))
    else:
        width = rights[0][0].shape[1] // 2
        if width % 128:
            cut = slice(half * width, (half + 1) * width)
            total = jnp.concatenate([sum(tn(a, b[:, cut]) for a, b in zip(lefts, r)) for r in rights], axis=1)
            total = jnp.moveaxis(total.reshape(-1, slabs, rows, segments * width), 1, 0)
            return sum((e.astype(jnp.float32) for e in extra), total).astype(jnp.bfloat16)
        blocks = CHUNK // (slabs * rows)
        shape = (slabs, D // (slabs * rows), rows, segments * width)
        left = pl.BlockSpec((tokens, CHUNK), lambda i: (0, i))
        right = pl.BlockSpec((tokens, width), lambda i: (0, half))
        out = pl.BlockSpec((slabs, blocks, rows, segments * width), lambda i: (0, i, 0, 0))
    return pl.pallas_call(
        functools.partial(sum_tn_kernel, segments, pairs),
        grid=(D // CHUNK,),
        in_specs=[left] * pairs + [right] * (segments * pairs) + [out] * len(extra),
        out_specs=out,
        out_shape=jax.ShapeDtypeStruct(shape, jnp.bfloat16),
        compiler_params=pltpu.CompilerParams(vmem_limit_bytes=56 << 20),
        cost_estimate=work((26 if segments == 2 else 16) * weight),
        name="sum_tn",
    )(*lefts, *[b for r in rights for b in r], *extra)


def ffn_kernel(n_ref, g_ref, wg_ref, wu_ref, wd_ref, hidden_ref, gate_grad_ref, up_grad_ref):
    gate = nn(n_ref[...], wg_ref[...])
    up = nn(n_ref[...], wu_ref[...])
    hidden_grad = nt(g_ref[...], wd_ref[...])
    sigm = 1.0 / (1.0 + jnp.exp(-gate))
    act = gate * sigm
    hidden_ref[...] = (act * up).astype(jnp.bfloat16)
    up_grad_ref[...] = (hidden_grad * act).astype(jnp.bfloat16)
    gate_grad_ref[...] = (hidden_grad * up * (sigm + act * (1.0 - sigm))).astype(jnp.bfloat16)


def feed_forward(n2, g, w_both, w_down):
    tokens, hidden = n2.shape[0], w_down.shape[0]
    tile = 256 if hidden % 256 == 0 else 128
    tiles = hidden // tile
    full = pl.BlockSpec((tokens, D), lambda j: (0, 0))
    out = pl.BlockSpec((tokens, tile), lambda j: (0, j))
    return pl.pallas_call(
        ffn_kernel,
        grid=(tiles,),
        in_specs=[full, full, pl.BlockSpec((D, tile), lambda j: (0, j)), pl.BlockSpec((D, tile), lambda j: (0, tiles + j)),
                  pl.BlockSpec((tile, D), lambda j: (j, 0))],
        out_specs=[out] * 3,
        out_shape=[jax.ShapeDtypeStruct((tokens, hidden), jnp.bfloat16)] * 3,
        compiler_params=pltpu.CompilerParams(vmem_limit_bytes=56 << 20),
        cost_estimate=work(36),
        name="feed_forward",
    )(n2, g, w_both, w_both, w_down)


def sum_nt_kernel(*refs):
    pairs = len(refs) // 2
    refs[-1][...] = sum(nt(refs[k][...], refs[pairs + k][...]) for k in range(pairs)).astype(jnp.bfloat16)


def sum_nt(lefts, right, weight=1):
    (tokens, depth), columns = lefts[0].shape, right.shape[0]
    tile, block = tokens // 2, columns // 2
    return pl.pallas_call(
        sum_nt_kernel,
        grid=(columns // block, tokens // tile),
        in_specs=[pl.BlockSpec((tile, depth), lambda j, i: (i, 0))] * len(lefts)
        + [pl.BlockSpec((block, depth), lambda j, i, k=k: (j, k)) for k in range(len(lefts))],
        out_specs=pl.BlockSpec((tile, block), lambda j, i: (i, j)),
        out_shape=jax.ShapeDtypeStruct((tokens, columns), jnp.bfloat16),
        compiler_params=pltpu.CompilerParams(vmem_limit_bytes=56 << 20),
        cost_estimate=work(26 * weight),
        name="sum_nt",
    )(*lefts, *([right] * len(lefts)))


def plain_nn_kernel(a_ref, b_ref, out_ref):
    out_ref[...] = nn(a_ref[...], b_ref[...]).astype(jnp.bfloat16)


def plain_nn(a, b, weight=1):
    (tokens, depth), columns = a.shape, b.shape[1]
    return pl.pallas_call(
        plain_nn_kernel,
        grid=(columns // CHUNK,),
        in_specs=[pl.BlockSpec((tokens, depth), lambda j: (0, 0)), pl.BlockSpec((depth, CHUNK), lambda j: (0, j))],
        out_specs=pl.BlockSpec((tokens, CHUNK), lambda j: (0, j)),
        out_shape=jax.ShapeDtypeStruct((tokens, columns), jnp.bfloat16),
        compiler_params=pltpu.CompilerParams(vmem_limit_bytes=56 << 20),
        cost_estimate=work(16 * weight),
        name="plain_nn",
    )(a, b)


class KeySum:
    def __init__(self, parts):
        self.parts = parts
        self.running = parts[-1]
        self.hops = 0

    def hop(self, *before):
        n = lax.axis_size("sp")
        s = self.hops
        if s:
            self.running = (self.parts[n - 1 - s].astype(jnp.float32) + self.running.astype(jnp.float32)).astype(jnp.bfloat16)
        pairs = [(n - 1 - k, n - 2 - k) for k in range(s + 1)]
        self.running = lax.ppermute(tie(self.running, *before), "sp", pairs)
        self.hops += 1
        return self.running

    def result(self):
        while self.hops < lax.axis_size("sp") - 1:
            self.hop()
        return self.parts[0], self.running


def rows_of(pieces):
    return jnp.concatenate(pieces, axis=0)


def body(tokens, doc_starts, cotangent, gain_attn, gain_ffn, w_query, w_key, w_value, w_out, w_gate, w_up, w_down):
    micro, _, rows, _ = tokens.shape
    parts = lax.axis_size("fsdp")
    chips = parts // 2
    core = lax.axis_index("fsdp") % 2
    seq = lax.axis_size("sp")
    place = lax.axis_index("sp")
    count = micro * rows
    d_own = w_query.shape[0]
    hidden_own = w_down.shape[0]
    hidden_chip = 2 * hidden_own
    bf16 = jnp.bfloat16
    f32 = jnp.float32

    gains = jnp.pad(jnp.stack([gain_attn, gain_ffn], axis=1), ((0, 0), (0, 126)))
    w_in = jnp.concatenate(
        [w_query, w_key[:, :KW], w_value[:, :KW], w_key[:, KW:], w_value[:, KW:], gains], axis=1
    )
    w_in = lax.all_gather(w_in, "fsdp", axis=0, tiled=True)
    w_out_full = lax.all_gather(w_out, "fsdp", axis=0, tiled=True)
    gain_one = w_in[:, D + 4 * KW].astype(f32)
    gain_two = w_in[:, D + 4 * KW + 1].astype(f32)
    reshard = Reshard(w_gate, w_up)
    came_columns = reshard.fetch()

    starts = doc_starts.reshape(micro, -1)
    offsets = (place - jnp.arange(seq, dtype=jnp.int32)) * rows
    key_places = (offsets[:, None] + jnp.arange(rows, dtype=jnp.int32)[None, :]).reshape(-1)
    docs, positions = stream_layout(starts, key_places)
    docs = docs.reshape(micro, seq, rows)
    key_places = key_places.reshape(seq, rows)
    tables = rope_lanes(positions.reshape(micro, seq, rows)[:, 0].reshape(count))
    allowed = (docs[:, :1, :, None] == docs[:, :, None, :]) & (
        key_places[None, :, None, :] <= key_places[None, :1, :, None]
    )
    bias = jnp.where(allowed, 0.0, -1e30).astype(f32)
    bias_t = jnp.where(jnp.swapaxes(allowed, 2, 3), 0.0, -1e30).astype(f32)

    inputs = tokens.reshape(count, D).astype(f32)
    scale_one = rms_scale(inputs)
    normed_x1 = inputs * scale_one
    normed = tie((normed_x1 * gain_one).astype(bf16), *tables, bias, bias_t)
    normed = tie(normed, *came_columns)
    w_down_other = partner(w_down)
    order = Order()
    qkv = order.did(project(normed, w_in, tables))

    g_low = cotangent.reshape(micro, rows, D)
    g_all = [gather_chips(tie(g_low[0], qkv))]
    state, n2_alls = [], []
    for m in range(micro):
        kv = [qkv[m * rows:(m + 1) * rows, D:]]
        for s in range(seq - 1):
            kv.append(lax.ppermute(kv[-1], "sp", right_pairs(seq, s)))
        context, lse = attend(order.at(qkv), kv, bias[m], m)
        lse_rows = jnp.swapaxes(lse.reshape(rows, HALVES, 128)[:, :, :QW // HEAD_DIM].reshape(rows, HEADS), 0, 1)
        mixed = inputs[m * rows:(m + 1) * rows] + nn(context, w_out_full)
        scale_two = rms_scale(mixed)
        normed_x2 = mixed * scale_two
        normed_ffn = order.did((normed_x2 * gain_two).astype(bf16))
        if m == 0:
            normed_ffn = tie(normed_ffn, g_all[0])
        n2_alls.append(gather_chips(normed_ffn))
        if m:
            g_all.append(gather_chips(tie(g_low[m], normed_ffn)))
        state.append((kv, context, lse_rows, mixed, scale_two, normed_x2))
    w_both = order.did(reshard.result(*order.last))
    w_down_chip = order.did(rows_of([order.at(w_down), w_down_other]))

    hiddens, gate_grads, up_grads, normed_grads, out_terms = [], [], [], [], []

    def forward_back(m):
        hidden, gate_grad, up_grad = feed_forward(order.at(n2_alls[m]), g_all[m], w_both, w_down_chip)
        hiddens.append(hidden)
        gate_grads.append(gate_grad)
        up_grads.append(order.did(up_grad))

    def normed_part(m, *before):
        part = order.did(sum_nt([order.at(gate_grads[m], *before), up_grads[m]], w_both))
        normed_grads.append(scatter_chips(part))

    def out_part(m, *before):
        part = order.did(plain_nn(order.at(hiddens[m], *before), w_down_chip))
        out_terms.append(scatter_chips(part))

    slab = d_own // seq
    ff = parts * hidden_own
    forward_back(0)
    normed_part(0, g_all[-1])
    for m in range(1, micro):
        forward_back(m)
    wide = dict(slabs=seq, rows=slab)
    wide_other = order.did(sum_tn(n2_alls, [[order.at(gate_grads[0])] + gate_grads[1:], up_grads], 1, **wide))
    wide_came = partner(wide_other)
    down_other = order.did(sum_tn([order.at(hiddens[0])] + hiddens[1:], [g_all], 1))
    down_came = partner(down_other)
    wide_grad = order.did(sum_tn(n2_alls, [[order.at(gate_grads[0])] + gate_grads[1:], up_grads], 0, wide_came, **wide))
    wide_mine = lax.psum_scatter(wide_grad, "sp", scatter_dimension=0, tiled=False)
    down_grad = order.did(sum_tn([order.at(hiddens[0])] + hiddens[1:], [g_all], 0, down_came))
    down_total = lax.psum(down_grad, "sp")
    normed_part(1)
    for m in range(micro):
        out_part(m)
    normed_mine, normed_other = features(order.at(normed), core, d_own)
    normed_chip = rows_of([normed_mine, partner(normed_other)])
    context_mine, context_other = features(rows_of([state[m][1] for m in range(micro)]), core, d_own)
    context_chip = rows_of([context_mine, partner(context_other)])
    order.did(normed_mine)

    mixed_grads, attn_grads, query_grads, kv_sums = [], [], [], []
    gain_two_term = 0.0
    chip_rows = lambda pieces: rows_of(pieces + [partner(p) for p in pieces])
    for m in range(micro):
        kv, context, lse_rows, mixed, scale_two, normed_x2 = state[m]
        if m == micro - 1:
            order.last = order.last + (wide_mine,)
            pieces = exchange_chips(exchange(wide_mine))
        normed_grad = added((order.at(normed_grads[m][0]), normed_grads[m][1]))
        gain_two_term = gain_two_term + jnp.sum(normed_grad * normed_x2, axis=0)
        mixed_grad = norm_back(normed_grad, gain_two, normed_x2, scale_two, g_low[m].astype(f32))
        attn_grad = mixed_grad.astype(bf16)
        attn_grads.append(attn_grad)
        mixed_grads.append(mixed_grad)
        context_grad = order.did(nt(attn_grad, w_out_full).astype(bf16))
        if m == micro - 1:
            out_half = order.did(tn(context_chip, chip_rows(attn_grads)).astype(bf16))
            out_shard = added(scatter_chips(out_half)).astype(bf16)
        args = (context, lse_rows, kv, bias_t[m], tables, m)
        first = attend_back(qkv, order.at(context_grad), *args, 0)
        order.last = ()
        if m == micro - 1:
            order.last = tuple(pieces)
        second = attend_back(qkv, order.at(context_grad), *args, 1, first)
        query_grads.append(order.did(second[0]))
        kv_sums.append(KeySum(second[1:]))
        kv_sums[-1].hop()

    order.last = order.last + (out_shard,)
    wide_part = exchanged([order.at(pieces[0], *pieces[1:])] + pieces[1:])
    wide_part = order.did(jnp.moveaxis(wide_part.reshape(parts, slab, 2, hidden_own), 0, 2).reshape(slab, 2 * ff))
    query_half = order.did(tn(normed_chip, chip_rows(query_grads[:-1] + [order.at(query_grads[-1])])).astype(bf16))
    query_shard = added(scatter_chips(query_half)).astype(bf16)
    kv_hop = tuple(keys.hop() for keys in kv_sums)
    normed_grad = order.did(nt(order.at(rows_of(query_grads), *kv_hop), w_in[:, :D]))
    kv_grads = [keys.result() for keys in kv_sums]
    kv_grads = [order.did(finish_keys(own, order.at(came), tables, m)) for m, (own, came) in enumerate(kv_grads)]
    wide_total = lax.all_gather(order.at(wide_part), "sp", axis=0, tiled=True)
    kv_grad = rows_of(kv_grads)
    kv_half = order.did(tn(normed_chip, chip_rows(kv_grads)).astype(bf16))
    normed_grad = normed_grad + nt(kv_grad, w_in[:, D:D + 4 * KW])
    gain_one_term = jnp.sum(normed_grad * normed_x1, axis=0)
    input_grad = norm_back(normed_grad, gain_one, normed_x1, scale_one, rows_of(mixed_grads)).astype(bf16)

    gain_blocks = jnp.stack([gain_one_term, gain_two_term], axis=1).astype(bf16).reshape(chips, 2, d_own, 2)
    gain_lanes = jnp.concatenate(
        [lax.dynamic_index_in_dim(gain_blocks, c, 1, keepdims=False) for c in (core, 1 - core)], axis=2
    ).reshape(chips * d_own, 4)
    kv_shard = added(scatter_chips(jnp.concatenate([kv_half, jnp.pad(gain_lanes, ((0, 0), (0, 124)))], axis=1))).astype(bf16)
    out_total, query_total, kv_total = lax.psum(
        (tie(out_shard, down_total), tie(query_shard, wide_total), tie(kv_shard, wide_total)), "sp"
    )
    query_total, kv_total = query_total.astype(f32), kv_total.astype(f32)
    kv_piece = lambda k: kv_total[:, k * KW:(k + 1) * KW]
    gain_lanes = kv_total[:, 4 * KW:4 * KW + 4]
    gain_total = gain_lanes[:, :2] + partner(gain_lanes)[:, 2:]
    outputs = [(state[m][3] + added((order.at(out_terms[m][0]), out_terms[m][1]))).astype(bf16) for m in range(micro)]
    return (
        rows_of(outputs).reshape(tokens.shape),
        input_grad.reshape(tokens.shape),
        gain_total[:, 0],
        gain_total[:, 1],
        query_total,
        jnp.concatenate([kv_piece(0), kv_piece(2)], axis=1),
        jnp.concatenate([kv_piece(1), kv_piece(3)], axis=1),
        out_total.astype(f32),
        wide_total[:, :ff].astype(f32),
        wide_total[:, ff:].astype(f32),
        order.at(down_total).astype(f32),
    )


def solution(mesh):
    split = P("fsdp", None)
    stream = P(None, "fsdp", "sp", None)
    return jax.shard_map(
        body,
        mesh=mesh,
        in_specs=(stream, P(None, "fsdp", None), stream, P("fsdp"), P("fsdp")) + (split,) * 7,
        out_specs=(stream, stream, P("fsdp"), P("fsdp")) + (split,) * 7,
        check_vma=False,
    )
```
